256 devices in a mesh: frames: 128 (over z, y, x_hi, core), mp: 2 (over x_lo).
Axes of the slice: x: 4 (x_hi: 2, x_lo: 2; x = x_hi * 2 + x_lo), y: 4, z: 8, core: 2. Of those that a mesh axis runs over, the one named last changes fastest.
Arguments:
- normed: bfloat16 [128, 512, 1536], P('frames'), may hold values from -24 to 24
- out_grad: bfloat16 [128, 512, 768], P('frames', None, 'mp'), may hold values from -24 to 24
- w_qkv: bfloat16 [1536, 3, 768], P('frames', None, 'mp'), may hold values from -0.15625 to 0.15625
Outputs:
- input_grad: bfloat16 [128, 512, 1536], P('frames', None, 'mp')
- weight_grad: float32 [1536, 3, 768], P('frames', None, 'mp')
The draws below stay inside these ranges and needn't reach their ends.
All inputs are finite; a program needn't handle non-finite values.
Results may differ from the reference program's by a relative error of at most 0.012.
Values may be sent and summed in bfloat16 or wider, within the bound.
No kernel may reach another device: no remote copies, remote signals or barrier semaphores. Data moves between devices by JAX's collectives and lax.ppermute only.
A program may use at most 128 MiB of HBM per device.

```python
import math
import jax
import jax.numpy as jnp
from jax import lax

D = 1536
HEAD_DIM = 64
PATCHES = 512
ATT = 768
FRAMES = 128


def strengthened(entries, own_key, source, target, parts, factor):
    def block_of(dim):
        return (jnp.arange(entries.shape[dim]) // (entries.shape[dim] // parts)).reshape((-1,) + (1,) * (entries.ndim - 1 - dim))

    first = jax.random.permutation(own_key, parts)[block_of(target)]
    other_side = (block_of(target) + parts // 2) % parts
    return jnp.where((block_of(source) == first) | (block_of(source) == other_side), factor * entries, entries)


def steps_of(stream_key, dims, shards, smallest, largest):
    level, own = 1.0, jax.random.fold_in(stream_key, 6)
    for position, parts in shards:
        draws = jnp.exp(jax.random.uniform(jax.random.fold_in(own, position), (parts,), jnp.float32, smallest / len(shards), largest / len(shards)))
        level = level * jnp.repeat(draws, dims[position] // parts).reshape([-1 if axis == position else 1 for axis in range(len(dims))])
    return level


def scatter_about(key, dims, spread, limit, shards=(), kind=jnp.bfloat16):
    level = steps_of(key, dims, shards, -0.22, 0.18) if shards else 1.0
    values = jax.random.normal(key, dims, jnp.float32) * spread * level
    return jnp.minimum(jnp.maximum(values, -limit), limit).astype(kind)


def gaussian_with(stream_key, shape, spread, bound, shards, heavy, kind=jnp.bfloat16):
    result = spread * jax.random.normal(stream_key, shape, jnp.float32)
    if shards:
        result = result * steps_of(stream_key, shape, shards, -0.22, 0.18)
    return jnp.clip(strengthened(result, jax.random.fold_in(stream_key, 3), *heavy), -bound, bound).astype(kind)


def setup_inputs(seed: int = 0) -> dict:
    seeds = jax.random.split(jax.random.key(seed), 4)
    normed = gaussian_with(seeds[0], (FRAMES, PATCHES, D), 1.0, 24.0, ((0, 128),), (0, 2, 128, 5.5))
    out_grad = scatter_about(seeds[1], (FRAMES, PATCHES, ATT), 4.0, 24.0, ((0, 128), (2, 2)))
    w_qkv = scatter_about(seeds[2], (D, 3, ATT), D ** -0.5, 0.15625, ((0, 128), (2, 2)))
    return {"normed": normed, "out_grad": out_grad, "w_qkv": w_qkv}


def attend(proj, upstream):
    steps_len, count, _, width = proj.shape
    heads = width // HEAD_DIM
    scale = HEAD_DIM ** -0.5
    shaped = lax.optimization_barrier(proj).astype(jnp.float32).reshape(steps_len, count, 3, heads, HEAD_DIM)
    query = shaped[:, :, 0]
    keys = shaped[:, :, 1]
    values = shaped[:, :, 2]
    upper = upstream.astype(jnp.float32).reshape(steps_len, count, heads, HEAD_DIM)
    scores = jnp.einsum("fpne,gpne->pnfg", query, keys) * scale
    weights = jnp.exp(scores)
    weights = weights / jnp.sum(weights, axis=-1, keepdims=True)
    probs = lax.optimization_barrier(weights.astype(jnp.bfloat16)).astype(jnp.float32)
    dvalues = jnp.einsum("pnfg,fpne->gpne", probs, upper).astype(jnp.bfloat16)
    dprobs = jnp.einsum("fpne,gpne->pnfg", upper, values)
    center = jnp.sum(weights * dprobs, axis=-1, keepdims=True)
    dscores = lax.optimization_barrier((weights * (dprobs - center) * scale).astype(jnp.bfloat16)).astype(jnp.float32)
    dquery = jnp.einsum("pnfg,gpne->fpne", dscores, keys).astype(jnp.bfloat16)
    dkeys = jnp.einsum("pnfg,fpne->gpne", dscores, query).astype(jnp.bfloat16)
    return jnp.stack([dquery, dkeys, dvalues], axis=2).reshape(steps_len, count, 3, width)


def reference(normed, out_grad, w_qkv):
    frames_all, patches, width = normed.shape
    columns_all = w_qkv.shape[2]
    patch_block = math.gcd(patches, 16)
    flat_weight = w_qkv.reshape(width, 3 * columns_all)

    def one_block(running, index):
        start = (index * patch_block).astype(jnp.int32)
        tokens = lax.dynamic_slice_in_dim(normed, start, patch_block, 1)
        upstream = lax.dynamic_slice_in_dim(out_grad, start, patch_block, 1)
        token_rows = tokens.reshape(frames_all * patch_block, width)
        proj = jnp.dot(token_rows, flat_weight, preferred_element_type=jnp.float32).astype(jnp.bfloat16)
        grads = attend(proj.reshape(frames_all, patch_block, 3, columns_all), upstream)
        grads = grads.reshape(frames_all * patch_block, 3 * columns_all)
        partial_value = lax.dot_general(grads, flat_weight, (((1,), (1,)), ((), ())), preferred_element_type=jnp.float32)
        running = running + lax.dot_general(token_rows, grads, (((0,), (0,)), ((), ())), preferred_element_type=jnp.float32)
        return running, partial_value.astype(jnp.bfloat16).reshape(frames_all, patch_block, width)

    start_sum = jnp.zeros((width, 3 * columns_all), jnp.float32)
    running, pieces = lax.scan(one_block, start_sum, jnp.arange(patches // patch_block, dtype=jnp.int32))
    input_grad = jnp.transpose(pieces, (1, 0, 2, 3)).reshape(frames_all, patches, width)
    weight_grad = (running * (1.0 / frames_all)).reshape(width, 3, columns_all)
    return input_grad, weight_grad
```

```python
import jax
import jax.numpy as jnp
from jax import lax
from jax.sharding import Mesh, PartitionSpec as P

HEAD_DIM = 64
Z, Y, XH, C, MP = 8, 4, 2, 2, 2
FR = ("z", "y", "xh", "c")
bf16, f32 = jnp.bfloat16, jnp.float32
SWAP = [(1, 2), (2, 1)]


def attend(proj, upstream):
    steps_len, count, _, half = proj.shape
    heads = half // HEAD_DIM
    scale = HEAD_DIM ** (-0.5)
    shaped = proj.reshape(steps_len, count, 3, heads, HEAD_DIM)
    query = shaped[:, :, 0]
    keys = shaped[:, :, 1]
    values = shaped[:, :, 2]
    upper = upstream.reshape(steps_len, count, heads, HEAD_DIM)
    scores = jnp.einsum("fpne,gpne->pnfg", query, keys, preferred_element_type=f32) * scale
    weights = jnp.exp(scores)
    weights = weights / jnp.sum(weights, axis=-1, keepdims=True)
    probs = weights.astype(bf16)
    dvalues = jnp.einsum("pnfg,fpne->gpne", probs, upper, preferred_element_type=f32).astype(bf16)
    dprobs = jnp.einsum("fpne,gpne->pnfg", upper, values, preferred_element_type=f32)
    center = jnp.sum(weights * dprobs, axis=-1, keepdims=True)
    dscores = (weights * (dprobs - center) * scale).astype(bf16)
    dquery = jnp.einsum("pnfg,gpne->fpne", dscores, keys, preferred_element_type=f32).astype(bf16)
    dkeys = jnp.einsum("pnfg,fpne->gpne", dscores, query, preferred_element_type=f32).astype(bf16)
    return jnp.stack([dquery, dkeys, dvalues], axis=2).reshape(steps_len, count, 3, half)


def swap_c(x):
    return lax.ppermute(x, "c", [(0, 1), (1, 0)])


def gather_weight(w):
    n = w.shape[1]
    c = lax.axis_index("c")
    xh = lax.axis_index("xh")
    other = swap_c(w)
    pair = jnp.where(c == 0, jnp.concatenate([w, other], 0), jnp.concatenate([other, w], 0))
    block = jnp.where(xh == c, pair, lax.ppermute(pair, ("xh", "c"), SWAP))
    over_z = lax.all_to_all(
        jnp.broadcast_to(block[None], (Z,) + block.shape), "z", 0, 0, tiled=True
    )
    over_y = lax.all_to_all(
        jnp.broadcast_to(over_z[None], (Y,) + over_z.shape), "y", 0, 0, tiled=True
    )
    rest = swap_c(over_y)
    mine = over_y.transpose(1, 0, 2, 3)
    rest = rest.transpose(1, 0, 2, 3)
    full = jnp.where(c == 0, jnp.stack([mine, rest], 2), jnp.stack([rest, mine], 2))
    return full.reshape(Z * Y * XH * 24, n)


def reduce_weight(term):
    n = term.shape[1]
    c = lax.axis_index("c")
    xh = lax.axis_index("xh")
    parts = term.reshape(Z, Y, XH, 24, n)
    mine = lax.dynamic_index_in_dim(parts, c, 2, keepdims=False)
    rest = lax.dynamic_index_in_dim(parts, 1 - c, 2, keepdims=False)
    total = mine.astype(f32) + swap_c(rest).astype(f32)
    total = total.astype(bf16).transpose(1, 0, 2, 3)
    got = lax.all_to_all(total, "y", 0, 0, tiled=True)
    total = jnp.sum(got.astype(f32), 0).astype(bf16)
    got = lax.all_to_all(total, "z", 0, 0, tiled=True)
    total = jnp.sum(got.astype(f32), 0)
    total = total + 0.0
    moved = lax.ppermute(total, ("xh", "c"), SWAP)
    total = jnp.where(xh == c, total, moved)
    halves = total.reshape(2, 12, n)
    mine = lax.dynamic_index_in_dim(halves, c, 0, keepdims=False)
    rest = lax.dynamic_index_in_dim(halves, 1 - c, 0, keepdims=False)
    return mine + swap_c(rest)


def on_device(normed, out_grad, w_qkv):
    frames_dev, patches, width = normed.shape
    half = out_grad.shape[2]
    out_cols = width // MP
    groups = Z * Y * XH * C
    count = patches // groups
    m = lax.axis_index("mp")
    tokens = jnp.concatenate([normed, out_grad], axis=2).reshape(groups, count, width + half)
    tokens = lax.all_to_all(tokens, FR, 0, 0, tiled=True)
    rows = tokens[:, :, :width].reshape(groups * count, width)
    upper = tokens[:, :, width:]
    weight = gather_weight(w_qkv.reshape(w_qkv.shape[0], 3 * half))

    proj = jnp.dot(rows, weight, preferred_element_type=f32).astype(bf16)
    grads = attend(proj.reshape(groups, count, 3, half), upper).reshape(groups * count, 3 * half)

    partial = lax.dot_general(
        grads, weight, (((1,), (1,)), ((), ())), preferred_element_type=f32
    ).astype(bf16)
    keep = lax.dynamic_slice_in_dim(partial, m * out_cols, out_cols, 1)
    give = lax.dynamic_slice_in_dim(partial, (1 - m) * out_cols, out_cols, 1)
    got = lax.ppermute(give, "mp", [(0, 1), (1, 0)])
    summed = (keep.astype(f32) + got.astype(f32)).astype(bf16)
    back = lax.all_to_all(summed.reshape(groups, count, out_cols), FR, 0, 0, tiled=True)
    input_grad = back.reshape(frames_dev, patches, out_cols)

    term = lax.dot_general(
        rows, grads, (((0,), (0,)), ((), ())), preferred_element_type=f32
    ).astype(bf16)
    weight_grad = reduce_weight(term) * (1.0 / groups)
    return (input_grad, weight_grad.reshape(w_qkv.shape))


def solution(mesh):
    fine = Mesh(mesh.devices.reshape(Z, Y, XH, C, MP), ("z", "y", "xh", "c", "mp"))
    in_specs = (P(FR, None, None), P(FR, None, "mp"), P(FR, None, "mp"))
    out_specs = (P(FR, None, "mp"), P(FR, None, "mp"))
    return jax.shard_map(
        on_device, mesh=fine, in_specs=in_specs, out_specs=out_specs, check_vma=False
    )
```

```python
import jax
import jax.numpy as jnp
from jax import lax
from jax.sharding import Mesh, PartitionSpec as P

HEAD_DIM = 64
Z, Y, XH, C, MP = 8, 4, 2, 2, 2
FR = ("z", "y", "xh", "c")
bf16, f32 = jnp.bfloat16, jnp.float32
SWAP = [(1, 2), (2, 1)]


def attend(proj, upstream):
    steps_len, count, _, half = proj.shape
    heads = half // HEAD_DIM
    scale = HEAD_DIM ** (-0.5)
    shaped = proj.reshape(steps_len, count, 3, heads, HEAD_DIM)
    query = shaped[:, :, 0]
    keys = shaped[:, :, 1]
    values = shaped[:, :, 2]
    upper = upstream.reshape(steps_len, count, heads, HEAD_DIM)
    scores = jnp.einsum("fpne,gpne->pnfg", query, keys, preferred_element_type=f32) * scale
    weights = jnp.exp(scores)
    weights = weights / jnp.sum(weights, axis=-1, keepdims=True)
    probs = weights.astype(bf16)
    dvalues = jnp.einsum("pnfg,fpne->gpne", probs, upper, preferred_element_type=f32).astype(bf16)
    dprobs = jnp.einsum("fpne,gpne->pnfg", upper, values, preferred_element_type=f32)
    center = jnp.sum(weights * dprobs, axis=-1, keepdims=True)
    dscores = (weights * (dprobs - center) * scale).astype(bf16)
    dquery = jnp.einsum("pnfg,gpne->fpne", dscores, keys, preferred_element_type=f32).astype(bf16)
    dkeys = jnp.einsum("pnfg,fpne->gpne", dscores, query, preferred_element_type=f32).astype(bf16)
    return jnp.stack([dquery, dkeys, dvalues], axis=2).reshape(steps_len, count, 3, half)


def swap_c(x):
    return lax.ppermute(x, "c", [(0, 1), (1, 0)])


def shift(x, axis, size, by):
    return lax.ppermute(x, axis, [(i, (i + by) % size) for i in range(size)])


def gather_weight(w):
    n = w.shape[1]
    c, xh = lax.axis_index("c"), lax.axis_index("xh")
    y, z = lax.axis_index("y"), lax.axis_index("z")
    other = swap_c(w)
    pair = jnp.where(c == 0, jnp.concatenate([w, other], 0), jnp.concatenate([other, w], 0))
    block = jnp.where(xh == c, pair, lax.ppermute(pair, ("xh", "c"), SWAP))
    over_z = jnp.stack([block] + [shift(block, "z", Z, Z - t) for t in range(1, Z)], 0)
    before = shift(over_z, "y", Y, 1)
    after = shift(over_z, "y", Y, Y - 1)
    far_low = shift(before[: Z // 2], "y", Y, 1)
    far_high = shift(after[Z // 2 :], "y", Y, Y - 1)
    pieces = [over_z, after, before, far_low, far_high]
    rest = [swap_c(p) for p in pieces]

    def joined(own, after, before, low, high):
        return jnp.stack([own, after, jnp.concatenate([low, high], 0), before], 1)

    mine, rest = joined(*pieces), joined(*rest)
    full = jnp.where(c == 0, jnp.stack([mine, rest], 2), jnp.stack([rest, mine], 2))
    full = jnp.roll(full, (z, y), (0, 1))
    return full.reshape(Z * Y * XH * 24, n)


def reduce_weight(term):
    n = term.shape[1]
    c, xh = lax.axis_index("c"), lax.axis_index("xh")
    y, z = lax.axis_index("y"), lax.axis_index("z")
    parts = term.reshape(Z, Y, XH, 24, n)
    mine = lax.dynamic_index_in_dim(parts, c, 2, keepdims=False)
    rest = lax.dynamic_index_in_dim(parts, 1 - c, 2, keepdims=False)
    total = mine.astype(f32) + swap_c(rest).astype(f32)
    h = Z // 2

    def of_y(by):
        return lax.dynamic_index_in_dim(total, (y + by) % Y, 1, keepdims=False)

    own, after, far, before = of_y(0), of_y(1), of_y(2), of_y(3)
    up_far = shift(far[:h].astype(bf16), "y", Y, 1)
    down_far = shift(far[h:].astype(bf16), "y", Y, Y - 1)
    up_high = shift(after[h:].astype(bf16), "y", Y, 1)
    down_low = shift(before[:h].astype(bf16), "y", Y, Y - 1)
    up_low = shift((after[:h] + up_far.astype(f32)).astype(bf16), "y", Y, 1)
    down_high = shift((before[h:] + down_far.astype(f32)).astype(bf16), "y", Y, Y - 1)
    low = own[:h] + up_low.astype(f32) + down_low.astype(f32)
    high = own[h:] + up_high.astype(f32) + down_high.astype(f32)
    total = jnp.concatenate([low, high], 0)
    sent = total.astype(bf16)
    got = [
        shift(lax.dynamic_index_in_dim(sent, (z + t) % Z, 0, keepdims=False), "z", Z, t)
        for t in range(1, Z)
    ]
    total = lax.dynamic_index_in_dim(total, z, 0, keepdims=False)
    for piece in got:
        total = total + piece.astype(f32)
    moved = lax.ppermute(total, ("xh", "c"), SWAP)
    total = jnp.where(xh == c, total, moved)
    halves = total.reshape(2, 12, n)
    mine = lax.dynamic_index_in_dim(halves, c, 0, keepdims=False)
    rest = lax.dynamic_index_in_dim(halves, 1 - c, 0, keepdims=False)
    return mine + swap_c(rest)


def on_device(normed, out_grad, w_qkv):
    frames_dev, patches, width = normed.shape
    half = out_grad.shape[2]
    out_cols = width // MP
    groups = Z * Y * XH * C
    count = patches // groups
    m = lax.axis_index("mp")
    tokens = jnp.concatenate([normed, out_grad], axis=2).reshape(groups, count, width + half)
    tokens = lax.all_to_all(tokens, FR, 0, 0, tiled=True)
    rows = tokens[:, :, :width].reshape(groups * count, width)
    upper = tokens[:, :, width:]
    weight = gather_weight(w_qkv.reshape(w_qkv.shape[0], 3 * half))

    proj = jnp.dot(rows, weight, preferred_element_type=f32).astype(bf16)
    grads = attend(proj.reshape(groups, count, 3, half), upper).reshape(groups * count, 3 * half)

    partial = lax.dot_general(
        grads, weight, (((1,), (1,)), ((), ())), preferred_element_type=f32
    ).astype(bf16)
    keep = lax.dynamic_slice_in_dim(partial, m * out_cols, out_cols, 1)
    give = lax.dynamic_slice_in_dim(partial, (1 - m) * out_cols, out_cols, 1)
    got = lax.ppermute(give, "mp", [(0, 1), (1, 0)])
    summed = (keep.astype(f32) + got.astype(f32)).astype(bf16)
    back = lax.all_to_all(summed.reshape(groups, count, out_cols), FR, 0, 0, tiled=True)
    input_grad = back.reshape(frames_dev, patches, out_cols)

    term = lax.dot_general(
        rows, grads, (((0,), (0,)), ((), ())), preferred_element_type=f32
    ).astype(bf16)
    weight_grad = reduce_weight(term) * (1.0 / groups)
    return (input_grad, weight_grad.reshape(w_qkv.shape))


def solution(mesh):
    fine = Mesh(mesh.devices.reshape(Z, Y, XH, C, MP), ("z", "y", "xh", "c", "mp"))
    in_specs = (P(FR, None, None), P(FR, None, "mp"), P(FR, None, "mp"))
    out_specs = (P(FR, None, "mp"), P(FR, None, "mp"))
    return jax.shard_map(
        on_device, mesh=fine, in_specs=in_specs, out_specs=out_specs, check_vma=False
    )
```

```python
import functools
import jax
import jax.numpy as jnp
from jax import lax
from jax.experimental import pallas as pl
from jax.experimental.pallas import tpu as pltpu
from jax.sharding import Mesh, PartitionSpec as P

HEAD_DIM = 64
Z, Y, XH, C, MP = 8, 4, 2, 2, 2
F = 128
bf16, f32 = jnp.bfloat16, jnp.float32
NT = (((1,), (1,)), ((), ()))
TN = (((0,), (0,)), ((), ()))


def dot(a, b, dims):
    return lax.dot_general(a, b, dims, preferred_element_type=f32)


def assemble_kernel(where_ref, *refs):
    mine, rest, w_ref = refs[:Y], refs[Y : 2 * Y], refs[2 * Y]
    z, y, c = where_ref[0], where_ref[1], where_ref[2]
    for by in range(Y):
        to_y = lax.rem(by + y, Y)
        for t in range(Z):
            a = mine[by][t].astype(f32)
            b = rest[by][t].astype(f32)
            first = jnp.where(c == 0, a, b)
            second = jnp.where(c == 0, b, a)
            w_ref[lax.rem(t + z, Z) * Y + to_y] = jnp.concatenate([first, second], 0).astype(bf16)


def assemble(where, mine, rest):
    n = mine[0].shape[-1]
    vm = pl.BlockSpec(memory_space=pltpu.VMEM)
    return pl.pallas_call(
        assemble_kernel,
        out_shape=jax.ShapeDtypeStruct((Z * Y, XH * 24, n), bf16),
        in_specs=[pl.BlockSpec(memory_space=pltpu.SMEM)] + [vm] * (2 * Y),
        out_specs=vm,
        compiler_params=pltpu.CompilerParams(vmem_limit_bytes=40 * 2**20),
        cost_estimate=pl.CostEstimate(flops=0, bytes_accessed=8 * 2**20, transcendentals=0),
        name="assemble_weight",
    )(where, *mine, *rest)


def core_kernel(where_ref, t_ref, w_ref, g_ref, give_ref, keep_ref, s_ref):
    width = w_ref.shape[0]
    rows, half = t_ref.shape[0], t_ref.shape[1] - width
    count = rows // F
    out_cols = width // MP
    scale = HEAD_DIM ** (-0.5)
    pairs = half // 128
    x = t_ref[:, :width]
    for j in range(3):
        cols = slice(j * half, (j + 1) * half)
        part = jnp.dot(x, w_ref[:, cols], preferred_element_type=f32).astype(bf16)
        for pair in range(pairs):
            s_ref[j * pairs + pair] = part[:, pair * 128 : (pair + 1) * 128].astype(f32)
    for pair in range(pairs):
        s_ref[3 * pairs + pair] = t_ref[:, width + pair * 128 : width + (pair + 1) * 128].astype(f32)
    low = lax.broadcasted_iota(jnp.int32, (F, 128), 1) < HEAD_DIM
    zero = jnp.zeros((F, 128), f32)

    def split(v):
        return jnp.concatenate([jnp.where(low, v, zero), jnp.where(low, zero, v)], 0).astype(bf16)

    for p in range(count):
        at = pl.ds(p, F, stride=count)
        for pair in range(pairs):
            q, k, v, u = (s_ref[j * pairs + pair, at, :] for j in range(4))
            q2 = split(q * scale)
            u2 = split(u)
            k = k.astype(bf16)
            v = v.astype(bf16)
            weights = jnp.exp(dot(q2, k, NT))
            weights = weights / jnp.sum(weights, axis=-1, keepdims=True)
            dprobs = dot(u2, v, NT)
            center = jnp.sum(weights * dprobs, axis=-1, keepdims=True)
            dscores = (weights * (dprobs - center)).astype(bf16)
            dv = dot(weights.astype(bf16), u2, TN)
            dk = dot(dscores, q2, TN)
            both = jnp.dot(dscores, k, preferred_element_type=f32) * scale
            dq = jnp.where(low, both[:F], both[F:])
            for j, part in enumerate((dq, dk, dv)):
                s_ref[j * pairs + pair, at, :] = part
    g = jnp.concatenate([s_ref[i] for i in range(3 * pairs)], 1).astype(bf16)
    g_ref[...] = g
    m = where_ref[3]
    give_at = pl.multiple_of((1 - m) * out_cols, out_cols)
    keep_at = pl.multiple_of(m * out_cols, out_cols)
    give_ref[...] = dot(g, w_ref[pl.ds(give_at, out_cols), :], NT).astype(bf16)
    keep_ref[...] = dot(g, w_ref[pl.ds(keep_at, out_cols), :], NT).astype(bf16)


def core(where, tokens, w):
    rows, half = tokens.shape[0], tokens.shape[1] - w.shape[0]
    vm = pl.BlockSpec(memory_space=pltpu.VMEM)
    out_cols = w.shape[0] // MP
    return pl.pallas_call(
        core_kernel,
        out_shape=(
            jax.ShapeDtypeStruct((rows, 3 * half), bf16),
            jax.ShapeDtypeStruct((rows, out_cols), bf16),
            jax.ShapeDtypeStruct((rows, out_cols), bf16),
        ),
        in_specs=[pl.BlockSpec(memory_space=pltpu.SMEM)] + [vm] * 2,
        out_specs=(vm, vm, vm),
        scratch_shapes=[pltpu.VMEM((4 * half // 128, rows, 128), f32)],
        compiler_params=pltpu.CompilerParams(vmem_limit_bytes=48 * 2**20),
        cost_estimate=pl.CostEstimate(
            flops=4 * rows * w.shape[0] * 3 * half, bytes_accessed=8 * 2**20, transcendentals=0
        ),
        name="attention_core",
    )(where, tokens, w)


def term_kernel(parts, where_ref, *refs):
    xs, gs = refs[:parts], refs[parts : 2 * parts]
    mine_ref, rest_ref = refs[2 * parts :]
    z, y, c = where_ref[0], where_ref[1], where_ref[2]
    width = Z * Y * XH * 24
    step = 384
    for i in range(width // step):
        total = dot(xs[0][:, i * step : (i + 1) * step], gs[0][...], TN)
        for x, g in zip(xs[1:], gs[1:]):
            total = total + dot(x[:, i * step : (i + 1) * step], g[...], TN)
        for b in range(step // 48):
            at = i * (step // 48) + b
            first = total[b * 48 : b * 48 + 24]
            second = total[b * 48 + 24 : b * 48 + 48]
            by = lax.rem(at % Y + Y - y, Y)
            t = lax.rem(at // Y + Z - z, Z)
            mine_ref[by, t] = jnp.where(c == 0, first, second).astype(bf16)
            rest_ref[by, t] = jnp.where(c == 0, second, first).astype(bf16)


def terms(where, xs, gs):
    n = gs[0].shape[1]
    vm = pl.BlockSpec(memory_space=pltpu.VMEM)
    shape = jax.ShapeDtypeStruct((Y, Z, 24, n), bf16)
    return pl.pallas_call(
        functools.partial(term_kernel, len(xs)),
        out_shape=(shape, shape),
        in_specs=[pl.BlockSpec(memory_space=pltpu.SMEM)] + [vm] * (2 * len(xs)),
        out_specs=(vm, vm),
        compiler_params=pltpu.CompilerParams(vmem_limit_bytes=48 * 2**20),
        cost_estimate=pl.CostEstimate(
            flops=2 * 512 * 1536 * n, bytes_accessed=8 * 2**20, transcendentals=0
        ),
        name="weight_terms",
    )(where, *xs, *gs)


FR = ("z", "y", "xh", "c")
SWAP = [(1, 2), (2, 1)]


def swap_c(x):
    return lax.ppermute(x, "c", [(0, 1), (1, 0)])


def shift(x, axis, size, by):
    return lax.ppermute(x, axis, [(i, (i + by) % size) for i in range(size)])


def gather_over_z(w):
    c, xh = lax.axis_index("c"), lax.axis_index("xh")
    other = swap_c(w)
    pair = jnp.where(c == 0, jnp.concatenate([w, other], 0), jnp.concatenate([other, w], 0))
    block = jnp.where(xh == c, pair, lax.ppermute(pair, ("xh", "c"), SWAP))
    return jnp.stack([block] + [shift(block, "z", Z, Z - t) for t in range(1, Z)], 0)


def reduce_weight(mine, rest):
    n = mine.shape[-1]
    c, xh = lax.axis_index("c"), lax.axis_index("xh")
    got = swap_c(rest)
    h = Z // 2
    own, after, far, before = (mine[i].astype(f32) + got[i].astype(f32) for i in range(Y))
    up_far = shift(far[:h].astype(bf16), "y", Y, 1)
    down_far = shift(far[h:].astype(bf16), "y", Y, Y - 1)
    up_high = shift(after[h:].astype(bf16), "y", Y, 1)
    down_low = shift(before[:h].astype(bf16), "y", Y, Y - 1)
    up_low = shift((after[:h] + up_far.astype(f32)).astype(bf16), "y", Y, 1)
    down_high = shift((before[h:] + down_far.astype(f32)).astype(bf16), "y", Y, Y - 1)
    low = own[:h] + up_low.astype(f32) + down_low.astype(f32)
    high = own[h:] + up_high.astype(f32) + down_high.astype(f32)
    blocks = [low[i] for i in range(h)] + [high[i] for i in range(h)]
    total = blocks[0]
    for t in range(1, Z):
        total = total + shift(blocks[t].astype(bf16), "z", Z, t).astype(f32)
    moved = lax.ppermute(total, ("xh", "c"), SWAP)
    total = jnp.where(xh == c, total, moved)
    first, second = total[:12], total[12:]
    return jnp.where(c == 0, first, second) + swap_c(jnp.where(c == 0, second, first))


def on_device(normed, out_grad, w_qkv):
    frames_dev, patches, width = normed.shape
    half = out_grad.shape[2]
    out_cols = width // MP
    count = patches // F
    n = 3 * half
    where = jnp.stack([lax.axis_index(a) for a in ("z", "y", "c", "mp")]).astype(jnp.int32)
    tokens = jnp.concatenate([normed, out_grad], axis=2).reshape(F, count, width + half)

    own = gather_over_z(w_qkv.reshape(w_qkv.shape[0], n))
    after, far, before = (shift(own, "y", Y, Y - t) for t in range(1, Y))
    tokens, _ = lax.optimization_barrier((tokens, own))
    tokens = lax.all_to_all(tokens, FR, 0, 0, tiled=True).reshape(F * count, width + half)
    mine = [own, after, far, before]
    weight = assemble(where, mine, [swap_c(p) for p in mine]).reshape(width, n)

    grads, give, keep = core(where, tokens, weight)
    got = lax.ppermute(give, "mp", [(0, 1), (1, 0)])
    summed = (keep.astype(f32) + got.astype(f32)).astype(bf16)
    back = lax.all_to_all(summed.reshape(F, count, out_cols), FR, 0, 0, tiled=True)
    input_grad = back.reshape(frames_dev, patches, out_cols)

    weight_grad = reduce_weight(*terms(where, [tokens], [grads])) * (1.0 / F)
    return (input_grad, weight_grad.reshape(w_qkv.shape))


def solution(mesh):
    fine = Mesh(mesh.devices.reshape(Z, Y, XH, C, MP), ("z", "y", "xh", "c", "mp"))
    in_specs = (P(FR, None, None), P(FR, None, "mp"), P(FR, None, "mp"))
    out_specs = (P(FR, None, "mp"), P(FR, None, "mp"))
    return jax.shard_map(
        on_device, mesh=fine, in_specs=in_specs, out_specs=out_specs, check_vma=False
    )
```

```python
import jax
import jax.numpy as jnp
from jax import lax
from jax.experimental import pallas as pl
from jax.experimental.pallas import tpu as pltpu
from jax.sharding import Mesh, PartitionSpec as P

HEAD_DIM = 64
Z, Y, XH, C, MP = 8, 4, 2, 2, 2
F = 128
ROWS = 12
bf16, f32 = jnp.bfloat16, jnp.float32
NT = (((1,), (1,)), ((), ()))
TN = (((0,), (0,)), ((), ()))


def dot(a, b, dims):
    return lax.dot_general(a, b, dims, preferred_element_type=f32)


def assemble_kernel(where_ref, mine_ref, rest_ref, w_ref):
    y, c = where_ref[1], where_ref[2]
    for z in range(Z):
        for by in range(Y):
            a = mine_ref[z, by].astype(f32)
            b = rest_ref[z, by].astype(f32)
            first = jnp.where(c == 0, a, b)
            second = jnp.where(c == 0, b, a)
            rows = [first[:ROWS], second[:ROWS], first[ROWS:], second[ROWS:]]
            w_ref[z * Y + lax.rem(by + y, Y)] = jnp.concatenate(rows, 0).astype(bf16)


def assemble(where, mine, rest):
    n = mine.shape[-1]
    vm = pl.BlockSpec(memory_space=pltpu.VMEM)
    return pl.pallas_call(
        assemble_kernel,
        out_shape=jax.ShapeDtypeStruct((Z * Y, XH * C * ROWS, n), bf16),
        in_specs=[pl.BlockSpec(memory_space=pltpu.SMEM), vm, vm],
        out_specs=vm,
        compiler_params=pltpu.CompilerParams(vmem_limit_bytes=40 * 2**20),
        cost_estimate=pl.CostEstimate(flops=0, bytes_accessed=8 * 2**20, transcendentals=0),
        name="assemble_weight",
    )(where, mine, rest)


def core_kernel(where_ref, t_ref, o_ref, w_ref, g_ref, give_ref, keep_ref, s_ref):
    part_cols = o_ref.shape[1]
    rows, half = t_ref.shape[0], t_ref.shape[1] - part_cols
    count = rows // F
    scale = HEAD_DIM ** (-0.5)
    pairs = half // 128
    m = where_ref[3]
    near = pl.ds(pl.multiple_of(m * part_cols, part_cols), part_cols)
    away = pl.ds(pl.multiple_of((1 - m) * part_cols, part_cols), part_cols)
    for j in range(3):
        cols = slice(j * half, (j + 1) * half)
        part = jnp.dot(t_ref[:, :part_cols], w_ref[near, cols], preferred_element_type=f32)
        part += jnp.dot(o_ref[...], w_ref[away, cols], preferred_element_type=f32)
        part = part.astype(bf16)
        for pair in range(pairs):
            s_ref[j * pairs + pair] = part[:, pair * 128 : (pair + 1) * 128].astype(f32)
    for pair in range(pairs):
        at = part_cols + pair * 128
        s_ref[3 * pairs + pair] = t_ref[:, at : at + 128].astype(f32)
    low = lax.broadcasted_iota(jnp.int32, (F, 128), 1) < HEAD_DIM
    zero = jnp.zeros((F, 128), f32)

    def split(v):
        return jnp.concatenate([jnp.where(low, v, zero), jnp.where(low, zero, v)], 0).astype(bf16)

    for p in range(count):
        at = pl.ds(p, F, stride=count)
        for pair in range(pairs):
            q, k, v, u = (s_ref[j * pairs + pair, at, :] for j in range(4))
            q2 = split(q * scale)
            u2 = split(u)
            k = k.astype(bf16)
            v = v.astype(bf16)
            weights = jnp.exp(dot(q2, k, NT))
            weights = weights / jnp.sum(weights, axis=-1, keepdims=True)
            dprobs = dot(u2, v, NT)
            center = jnp.sum(weights * dprobs, axis=-1, keepdims=True)
            dscores = (weights * (dprobs - center)).astype(bf16)
            dv = dot(weights.astype(bf16), u2, TN)
            dk = dot(dscores, q2, TN)
            both = jnp.dot(dscores, k, preferred_element_type=f32) * scale
            dq = jnp.where(low, both[:F], both[F:])
            for j, part in enumerate((dq, dk, dv)):
                s_ref[j * pairs + pair, at, :] = part
    g = jnp.concatenate([s_ref[i] for i in range(3 * pairs)], 1).astype(bf16)
    g_ref[...] = g
    give_ref[...] = dot(g, w_ref[away, :], NT).astype(bf16)
    keep_ref[...] = dot(g, w_ref[near, :], NT).astype(bf16)


def core(where, tokens, others, w):
    rows, part_cols = others.shape
    half = tokens.shape[1] - part_cols
    vm = pl.BlockSpec(memory_space=pltpu.VMEM)
    return pl.pallas_call(
        core_kernel,
        out_shape=(
            jax.ShapeDtypeStruct((rows, 3 * half), bf16),
            jax.ShapeDtypeStruct((rows, part_cols), bf16),
            jax.ShapeDtypeStruct((rows, part_cols), bf16),
        ),
        in_specs=[pl.BlockSpec(memory_space=pltpu.SMEM)] + [vm] * 3,
        out_specs=(vm, vm, vm),
        scratch_shapes=[pltpu.VMEM((4 * half // 128, rows, 128), f32)],
        compiler_params=pltpu.CompilerParams(vmem_limit_bytes=48 * 2**20),
        cost_estimate=pl.CostEstimate(
            flops=4 * rows * w.shape[0] * 3 * half, bytes_accessed=8 * 2**20, transcendentals=0
        ),
        name="attention_core",
    )(where, tokens, others, w)


def term_kernel(where_ref, t_ref, o_ref, g_ref, mine_ref, rest_ref):
    z, y, c, m = (where_ref[i] for i in range(4))
    part_cols = o_ref.shape[1]
    step, unit = 384, XH * C * ROWS
    g = g_ref[...]
    for ref, of in ((t_ref, m), (o_ref, 1 - m)):
        for i in range(part_cols // step):
            total = dot(ref[:, i * step : (i + 1) * step], g, TN)
            for b in range(step // unit):
                quarters = [total[b * unit + r * ROWS :][:ROWS] for r in range(4)]
                first = jnp.concatenate([quarters[0], quarters[2]], 0)
                second = jnp.concatenate([quarters[1], quarters[3]], 0)
                by = lax.rem(b % Y + Y - y, Y)
                at = (i * step // unit + b) // Y
                t = lax.rem(of * (Z // MP) + at + Z - z, Z)
                mine_ref[by, t] = jnp.where(c == 0, first, second).astype(bf16)
                rest_ref[by, t] = jnp.where(c == 0, second, first).astype(bf16)


def terms(where, tokens, others, grads):
    n = grads.shape[1]
    vm = pl.BlockSpec(memory_space=pltpu.VMEM)
    shape = jax.ShapeDtypeStruct((Y, Z, XH * ROWS, n), bf16)
    return pl.pallas_call(
        term_kernel,
        out_shape=(shape, shape),
        in_specs=[pl.BlockSpec(memory_space=pltpu.SMEM)] + [vm] * 3,
        out_specs=(vm, vm),
        compiler_params=pltpu.CompilerParams(vmem_limit_bytes=48 * 2**20),
        cost_estimate=pl.CostEstimate(
            flops=2 * 512 * 1536 * n, bytes_accessed=8 * 2**20, transcendentals=0
        ),
        name="weight_terms",
    )(where, tokens, others, grads)


FR = ("z", "y", "xh", "c")
PAIR = [(0, 1), (1, 0)]


def shift(x, axis, size, by):
    return lax.ppermute(x, axis, [(i, (i + by) % size) for i in range(size)])


def gather_weight(w):
    xh = lax.axis_index("xh")
    other = lax.ppermute(w, "xh", PAIR)
    block = jnp.where(xh == 0, jnp.concatenate([w, other], 0), jnp.concatenate([other, w], 0))
    over_y = jnp.stack([block] + [shift(block, "y", Y, Y - t) for t in range(1, Y)], 0)
    return lax.all_gather(over_y, "z", axis=0)


def reduce_weight(mine, rest, early, late):
    xh = lax.axis_index("xh")
    got = lax.ppermute(rest, "c", PAIR)
    h = Z // 2
    own, after, far, before = (mine[i].astype(f32) + got[i].astype(f32) for i in range(Y))
    up_far = shift(far[:h].astype(bf16), "y", Y, 1)
    down_far = shift(far[h:].astype(bf16), "y", Y, Y - 1)
    up_high = shift(after[h:].astype(bf16), "y", Y, 1)
    down_low = shift(before[:h].astype(bf16), "y", Y, Y - 1)
    up_low = (after[:h] + up_far.astype(f32)).astype(bf16)
    down_high = (before[h:] + down_far.astype(f32)).astype(bf16)
    up_low, down_high, early = lax.optimization_barrier((up_low, down_high, early))
    up_low = shift(up_low, "y", Y, 1)
    down_high = shift(down_high, "y", Y, Y - 1)
    low = own[:h] + up_low.astype(f32) + down_low.astype(f32)
    high = own[h:] + up_high.astype(f32) + down_high.astype(f32)
    blocks = [low[i] for i in range(h)] + [high[i] for i in range(h)]
    total = blocks[0]
    for t in range(1, Z):
        total = total + shift(blocks[t].astype(bf16), "z", Z, t).astype(f32)
    back = late(early)
    total, back = lax.optimization_barrier((total, back))
    first, second = total[:ROWS], total[ROWS:]
    moved = lax.ppermute(jnp.where(xh == 0, second, first), "xh", PAIR)
    return jnp.where(xh == 0, first, second) + moved, back


def on_device(normed, out_grad, w_qkv):
    frames_dev, patches, width = normed.shape
    half = out_grad.shape[2]
    cols = width // MP
    count = patches // F
    n = 3 * half
    where = jnp.stack([lax.axis_index(a) for a in ("z", "y", "c", "mp")]).astype(jnp.int32)
    m = lax.axis_index("mp")
    part = lax.dynamic_slice_in_dim(normed, m * cols, cols, 2)
    tokens = jnp.concatenate([part, out_grad], axis=2).reshape(F, count, cols + half)

    mine = gather_weight(w_qkv.reshape(w_qkv.shape[0], n))
    tokens = lax.all_to_all(tokens, FR, 0, 0, tiled=True)
    others = lax.ppermute(tokens[:, :, :cols], "mp", PAIR).reshape(F * count, cols)
    tokens = tokens.reshape(F * count, cols + half)
    weight = assemble(where, mine, lax.ppermute(mine, "c", PAIR)).reshape(width, n)

    grads, give, keep = core(where, tokens, others, weight)
    got = lax.ppermute(give, "mp", PAIR)
    summed = (keep.astype(f32) + got.astype(f32)).astype(bf16)

    def to_frames(x):
        return lax.all_to_all(x.reshape(F, count, cols), FR, 0, 0, tiled=True)

    mine, rest = terms(where, tokens, others, grads)
    weight_grad, back = reduce_weight(mine, rest, summed, to_frames)
    input_grad = back.reshape(frames_dev, patches, cols)
    weight_grad = weight_grad * (1.0 / F)
    return (input_grad, weight_grad.reshape(w_qkv.shape))


def solution(mesh):
    fine = Mesh(mesh.devices.reshape(Z, Y, XH, C, MP), ("z", "y", "xh", "c", "mp"))
    in_specs = (P(FR, None, None), P(FR, None, "mp"), P(FR, None, "mp"))
    out_specs = (P(FR, None, "mp"), P(FR, None, "mp"))
    return jax.shard_map(
        on_device, mesh=fine, in_specs=in_specs, out_specs=out_specs, check_vma=False
    )
```

```python
import jax
import jax.numpy as jnp
from jax import lax
from jax.experimental import pallas as pl
from jax.experimental.pallas import tpu as pltpu
from jax.sharding import Mesh, PartitionSpec as P

HEAD_DIM = 64
Z, Y, XH, C, MP = 8, 4, 2, 2, 2
F = 128
ROWS = 12
bf16, f32 = jnp.bfloat16, jnp.float32
NT = (((1,), (1,)), ((), ()))
TN = (((0,), (0,)), ((), ()))


def dot(a, b, dims):
    return lax.dot_general(a, b, dims, preferred_element_type=f32)


def assemble_kernel(where_ref, *refs):
    w_ref = refs[-1]
    z, y, c = where_ref[0], where_ref[1], where_ref[2]
    half = Z // 2
    for by in range(Y):
        for t in range(Z):
            if by == 2:
                which, at = (3, t) if t < half else (4, t - half)
            else:
                which, at = (0, 1, None, 2)[by], t
            a = refs[which][at].astype(f32)
            b = refs[which + 5][at].astype(f32)
            first = jnp.where(c == 0, a, b)
            second = jnp.where(c == 0, b, a)
            rows = [first[:ROWS], second[:ROWS], first[ROWS:], second[ROWS:]]
            to = lax.bitwise_xor(z, t) * Y + lax.rem(by + y, Y)
            w_ref[to] = jnp.concatenate(rows, 0).astype(bf16)


def assemble(where, mine, rest):
    n = mine[0].shape[-1]
    vm = pl.BlockSpec(memory_space=pltpu.VMEM)
    return pl.pallas_call(
        assemble_kernel,
        out_shape=jax.ShapeDtypeStruct((Z * Y, XH * C * ROWS, n), bf16),
        in_specs=[pl.BlockSpec(memory_space=pltpu.SMEM)] + [vm] * 10,
        out_specs=vm,
        compiler_params=pltpu.CompilerParams(vmem_limit_bytes=40 * 2**20),
        cost_estimate=pl.CostEstimate(flops=0, bytes_accessed=8 * 2**20, transcendentals=0),
        name="assemble_weight",
    )(where, *mine, *rest)


def core_kernel(where_ref, t_ref, o_ref, w_ref, g_ref, give_ref, keep_ref, s_ref):
    part_cols = o_ref.shape[1]
    rows, half = t_ref.shape[0], t_ref.shape[1] - part_cols
    count = rows // F
    scale = HEAD_DIM ** (-0.5)
    pairs = half // 128
    m = where_ref[3]
    near = pl.ds(pl.multiple_of(m * part_cols, part_cols), part_cols)
    away = pl.ds(pl.multiple_of((1 - m) * part_cols, part_cols), part_cols)
    for j in range(3):
        cols = slice(j * half, (j + 1) * half)
        part = jnp.dot(t_ref[:, :part_cols], w_ref[near, cols], preferred_element_type=f32)
        part += jnp.dot(o_ref[...], w_ref[away, cols], preferred_element_type=f32)
        part = part.astype(bf16)
        for pair in range(pairs):
            s_ref[j * pairs + pair] = part[:, pair * 128 : (pair + 1) * 128].astype(f32)
    for pair in range(pairs):
        at = part_cols + pair * 128
        s_ref[3 * pairs + pair] = t_ref[:, at : at + 128].astype(f32)
    low = lax.broadcasted_iota(jnp.int32, (F, 128), 1) < HEAD_DIM
    zero = jnp.zeros((F, 128), f32)

    def split(v):
        return jnp.concatenate([jnp.where(low, v, zero), jnp.where(low, zero, v)], 0).astype(bf16)

    for p in range(count):
        at = pl.ds(p, F, stride=count)
        for pair in range(pairs):
            q, k, v, u = (s_ref[j * pairs + pair, at, :] for j in range(4))
            q2 = split(q * scale)
            u2 = split(u)
            k = k.astype(bf16)
            v = v.astype(bf16)
            weights = jnp.exp(dot(q2, k, NT))
            weights = weights / jnp.sum(weights, axis=-1, keepdims=True)
            dprobs = dot(u2, v, NT)
            center = jnp.sum(weights * dprobs, axis=-1, keepdims=True)
            dscores = (weights * (dprobs - center)).astype(bf16)
            dv = dot(weights.astype(bf16), u2, TN)
            dk = dot(dscores, q2, TN)
            both = jnp.dot(dscores, k, preferred_element_type=f32) * scale
            dq = jnp.where(low, both[:F], both[F:])
            for j, part in enumerate((dq, dk, dv)):
                s_ref[j * pairs + pair, at, :] = part
    g = jnp.concatenate([s_ref[i] for i in range(3 * pairs)], 1).astype(bf16)
    g_ref[...] = g
    give_ref[...] = dot(g, w_ref[away, :], NT).astype(bf16)
    keep_ref[...] = dot(g, w_ref[near, :], NT).astype(bf16)


def core(where, tokens, others, w):
    rows, part_cols = others.shape
    half = tokens.shape[1] - part_cols
    vm = pl.BlockSpec(memory_space=pltpu.VMEM)
    return pl.pallas_call(
        core_kernel,
        out_shape=(
            jax.ShapeDtypeStruct((rows, 3 * half), bf16),
            jax.ShapeDtypeStruct((rows, part_cols), bf16),
            jax.ShapeDtypeStruct((rows, part_cols), bf16),
        ),
        in_specs=[pl.BlockSpec(memory_space=pltpu.SMEM)] + [vm] * 3,
        out_specs=(vm, vm, vm),
        scratch_shapes=[pltpu.VMEM((4 * half // 128, rows, 128), f32)],
        compiler_params=pltpu.CompilerParams(vmem_limit_bytes=48 * 2**20),
        cost_estimate=pl.CostEstimate(
            flops=4 * rows * w.shape[0] * 3 * half, bytes_accessed=8 * 2**20, transcendentals=0
        ),
        name="attention_core",
    )(where, tokens, others, w)


def term_kernel(where_ref, t_ref, o_ref, g_ref, mine_ref, rest_ref):
    z, y, c, m = (where_ref[i] for i in range(4))
    part_cols = o_ref.shape[1]
    step, unit = 384, XH * C * ROWS
    g = g_ref[...]
    for ref, of in ((t_ref, m), (o_ref, 1 - m)):
        for i in range(part_cols // step):
            total = dot(ref[:, i * step : (i + 1) * step], g, TN)
            for b in range(step // unit):
                quarters = [total[b * unit + r * ROWS :][:ROWS] for r in range(4)]
                first = jnp.concatenate([quarters[0], quarters[2]], 0)
                second = jnp.concatenate([quarters[1], quarters[3]], 0)
                by = lax.rem(b % Y + Y - y, Y)
                at = (i * step // unit + b) // Y
                t = lax.bitwise_xor(of * (Z // MP) + at, z)
                mine_ref[by, t] = jnp.where(c == 0, first, second).astype(bf16)
                rest_ref[by, t] = jnp.where(c == 0, second, first).astype(bf16)


def terms(where, tokens, others, grads):
    n = grads.shape[1]
    vm = pl.BlockSpec(memory_space=pltpu.VMEM)
    shape = jax.ShapeDtypeStruct((Y, Z, XH * ROWS, n), bf16)
    return pl.pallas_call(
        term_kernel,
        out_shape=(shape, shape),
        in_specs=[pl.BlockSpec(memory_space=pltpu.SMEM)] + [vm] * 3,
        out_specs=(vm, vm),
        compiler_params=pltpu.CompilerParams(vmem_limit_bytes=48 * 2**20),
        cost_estimate=pl.CostEstimate(
            flops=2 * 512 * 1536 * n, bytes_accessed=8 * 2**20, transcendentals=0
        ),
        name="weight_terms",
    )(where, tokens, others, grads)


FR = ("z", "y", "xh", "c")
PAIR = [(0, 1), (1, 0)]


def shift(x, axis, size, by):
    return lax.ppermute(x, axis, [(i, (i + by) % size) for i in range(size)])


def across(x, axis, size, by):
    return lax.ppermute(x, axis, [(i, i ^ by) for i in range(size)])


def over_xh_and_pair(w):
    xh = lax.axis_index("xh")
    other = lax.ppermute(w, "xh", PAIR)
    block = jnp.where(xh == 0, jnp.concatenate([w, other], 0), jnp.concatenate([other, w], 0))
    return jnp.stack([block, across(block, "z", Z, 1)], 0)


def over_y(own):
    before = shift(own, "y", Y, 1)
    after = shift(own, "y", Y, Y - 1)
    low = shift(before[: Z // 2], "y", Y, 1)
    high = shift(after[Z // 2 :], "y", Y, Y - 1)
    return [own, after, before, low, high]


def reduce_weight(mine, rest, got, finish, late):
    xh = lax.axis_index("xh")
    other = lax.ppermute(rest, "c", PAIR)
    h = Z // 2
    own, after, far, before = (mine[i].astype(f32) + other[i].astype(f32) for i in range(Y))
    up_far = shift(far[:h].astype(bf16), "y", Y, 1)
    down_far = shift(far[h:].astype(bf16), "y", Y, Y - 1)
    up_high = shift(after[h:].astype(bf16), "y", Y, 1)
    down_low = shift(before[:h].astype(bf16), "y", Y, Y - 1)
    up_far, down_far, got = lax.optimization_barrier((up_far, down_far, got))
    summed = finish(got)
    up_low = (after[:h] + up_far.astype(f32)).astype(bf16)
    down_high = (before[h:] + down_far.astype(f32)).astype(bf16)
    up_low, down_high, summed = lax.optimization_barrier((up_low, down_high, summed))
    up_low = shift(up_low, "y", Y, 1)
    down_high = shift(down_high, "y", Y, Y - 1)
    low = own[:h] + up_low.astype(f32) + down_low.astype(f32)
    high = own[h:] + up_high.astype(f32) + down_high.astype(f32)
    blocks = [low[i] for i in range(h)] + [high[i] for i in range(h)]
    sent = jnp.stack(blocks[1::2], 0).astype(bf16)
    pair = across(sent, "z", Z, 1).astype(f32)
    blocks = [blocks[2 * i] + pair[i] for i in range(h)]
    total = blocks[0]
    for i in range(1, h):
        total = total + across(blocks[i].astype(bf16), "z", Z, 2 * i).astype(f32)
    back = late(summed)
    total, back = lax.optimization_barrier((total, back))
    first, second = total[:ROWS], total[ROWS:]
    moved = lax.ppermute(jnp.where(xh == 0, second, first), "xh", PAIR)
    return jnp.where(xh == 0, first, second) + moved, back


def on_device(normed, out_grad, w_qkv):
    frames_dev, patches, width = normed.shape
    half = out_grad.shape[2]
    cols = width // MP
    count = patches // F
    n = 3 * half
    where = jnp.stack([lax.axis_index(a) for a in ("z", "y", "c", "mp")]).astype(jnp.int32)
    m = lax.axis_index("mp")
    part = lax.dynamic_slice_in_dim(normed, m * cols, cols, 2)
    tokens = jnp.concatenate([part, out_grad], axis=2).reshape(F, count, cols + half)

    pair = over_xh_and_pair(w_qkv.reshape(w_qkv.shape[0], n))
    tokens, pair = lax.optimization_barrier((tokens, pair))
    tokens = lax.all_to_all(tokens, FR, 0, 0, tiled=True)
    own = jnp.concatenate([pair] + [across(pair, "z", Z, 2 * i) for i in range(1, Z // 2)], 0)
    part = tokens[:, :, :cols]
    own, part = lax.optimization_barrier((own, part))
    others = lax.ppermute(part, "mp", PAIR)
    mine = over_y(own)
    mine, others = lax.optimization_barrier((mine, others))
    others = others.reshape(F * count, cols)
    tokens = tokens.reshape(F * count, cols + half)
    rest = [lax.ppermute(p, "c", PAIR) for p in mine]
    weight = assemble(where, mine, rest).reshape(width, n)

    grads, give, keep = core(where, tokens, others, weight)
    got = lax.ppermute(give, "mp", PAIR)

    def finish(got):
        return (keep.astype(f32) + got.astype(f32)).astype(bf16)

    def to_frames(x):
        return lax.all_to_all(x.reshape(F, count, cols), FR, 0, 0, tiled=True)

    mine, rest = terms(where, tokens, others, grads)
    weight_grad, back = reduce_weight(mine, rest, got, finish, to_frames)
    input_grad = back.reshape(frames_dev, patches, cols)
    weight_grad = weight_grad * (1.0 / F)
    return (input_grad, weight_grad.reshape(w_qkv.shape))


def solution(mesh):
    fine = Mesh(mesh.devices.reshape(Z, Y, XH, C, MP), ("z", "y", "xh", "c", "mp"))
    in_specs = (P(FR, None, None), P(FR, None, "mp"), P(FR, None, "mp"))
    out_specs = (P(FR, None, "mp"), P(FR, None, "mp"))
    return jax.shard_map(
        on_device, mesh=fine, in_specs=in_specs, out_specs=out_specs, check_vma=False
    )
```

```python
import jax
import jax.numpy as jnp
from jax import lax
from jax.experimental import pallas as pl
from jax.experimental.pallas import tpu as pltpu
from jax.sharding import Mesh, PartitionSpec as P

HEAD_DIM = 64
Z, Y, XH, C, MP = 8, 4, 2, 2, 2
F = 128
ROWS = 12
bf16, f32 = jnp.bfloat16, jnp.float32
NT = (((1,), (1,)), ((), ()))
TN = (((0,), (0,)), ((), ()))


def dot(a, b, dims):
    return lax.dot_general(a, b, dims, preferred_element_type=f32)


def core_kernel(where_ref, t_ref, o_ref, *refs):
    pieces = refs[:10]
    g_ref, give_ref, keep_ref, w_ref, s_ref, d_ref = refs[10:]
    z, y, c, m = (where_ref[i] for i in range(4))
    unit = XH * C * ROWS
    for by in range(Y):
        for t in range(Z):
            if by == 2:
                which, at = (3, t) if t < Z // 2 else (4, t - Z // 2)
            else:
                which, at = (0, 1, None, 2)[by], t
            a = pieces[which][at].astype(f32)
            b = pieces[which + 5][at].astype(f32)
            first = jnp.where(c == 0, a, b)
            second = jnp.where(c == 0, b, a)
            rows = [first[:ROWS], second[:ROWS], first[ROWS:], second[ROWS:]]
            to = lax.bitwise_xor(z, t) * Y + lax.rem(by + y, Y)
            to = pl.ds(pl.multiple_of(to * unit, unit), unit)
            w_ref[to, :] = jnp.concatenate(rows, 0).astype(bf16)

    part_cols = o_ref.shape[1]
    rows, half = t_ref.shape[0], t_ref.shape[1] - part_cols
    count = rows // F
    scale = HEAD_DIM ** (-0.5)
    pairs = half // 128
    near = pl.ds(pl.multiple_of(m * part_cols, part_cols), part_cols)
    away = pl.ds(pl.multiple_of((1 - m) * part_cols, part_cols), part_cols)
    for j in range(3):
        cols = slice(j * half, (j + 1) * half)
        part = jnp.dot(t_ref[:, :part_cols], w_ref[near, cols], preferred_element_type=f32)
        part += jnp.dot(o_ref[...], w_ref[away, cols], preferred_element_type=f32)
        part = part.astype(bf16)
        for pair in range(pairs):
            s_ref[j * pairs + pair] = part[:, pair * 128 : (pair + 1) * 128].astype(f32)
    for pair in range(pairs):
        at = part_cols + pair * 128
        s_ref[3 * pairs + pair] = t_ref[:, at : at + 128].astype(f32)
    low = lax.broadcasted_iota(jnp.int32, (F, 128), 1) < HEAD_DIM
    zero = jnp.zeros((F, 128), f32)

    def split(v):
        return jnp.concatenate([jnp.where(low, v, zero), jnp.where(low, zero, v)], 0).astype(bf16)

    for p in range(count):
        at = pl.ds(p, F, stride=count)
        for pair in range(pairs):
            q, k, v, u = (s_ref[j * pairs + pair, at, :] for j in range(4))
            q2 = split(q * scale)
            u2 = split(u)
            k = k.astype(bf16)
            v = v.astype(bf16)
            weights = jnp.exp(dot(q2, k, NT))
            weights = weights / jnp.sum(weights, axis=-1, keepdims=True)
            dprobs = dot(u2, v, NT)
            center = jnp.sum(weights * dprobs, axis=-1, keepdims=True)
            dscores = (weights * (dprobs - center)).astype(bf16)
            dv = dot(weights.astype(bf16), u2, TN)
            dk = dot(dscores, q2, TN)
            both = jnp.dot(dscores, k, preferred_element_type=f32) * scale
            dq = jnp.where(low, both[:F], both[F:])
            for j, part in enumerate((dq, dk, dv)):
                d_ref[j * pairs + pair, at, :] = part
    g = jnp.concatenate([d_ref[i] for i in range(3 * pairs)], 1).astype(bf16)
    g_ref[...] = g
    give_ref[...] = dot(g, w_ref[away, :], NT).astype(bf16)
    keep_ref[...] = dot(g, w_ref[near, :], NT).astype(bf16)


def core(where, tokens, others, mine, rest):
    rows, part_cols = others.shape
    half = tokens.shape[1] - part_cols
    width, n = MP * part_cols, 3 * half
    vm = pl.BlockSpec(memory_space=pltpu.VMEM)
    return pl.pallas_call(
        core_kernel,
        out_shape=(
            jax.ShapeDtypeStruct((rows, n), bf16),
            jax.ShapeDtypeStruct((rows, part_cols), bf16),
            jax.ShapeDtypeStruct((rows, part_cols), bf16),
        ),
        in_specs=[pl.BlockSpec(memory_space=pltpu.SMEM)] + [vm] * 12,
        out_specs=(vm, vm, vm),
        scratch_shapes=[
            pltpu.VMEM((width, n), bf16),
            pltpu.VMEM((4 * half // 128, rows, 128), f32),
            pltpu.VMEM((3 * half // 128, rows, 128), f32),
        ],
        compiler_params=pltpu.CompilerParams(vmem_limit_bytes=48 * 2**20),
        cost_estimate=pl.CostEstimate(
            flops=4 * rows * width * n, bytes_accessed=8 * 2**20, transcendentals=0
        ),
        name="attention_core",
    )(where, tokens, others, *mine, *rest)


def term_kernel(where_ref, t_ref, o_ref, g_ref, mine_ref, *refs):
    rest_refs, rest_ref = refs[:Y], refs[Y]
    z, y, c, m = (where_ref[i] for i in range(4))
    part_cols = o_ref.shape[1]
    step, unit = 384, XH * C * ROWS
    g = g_ref[...]
    for ref, of in ((t_ref, m), (o_ref, 1 - m)):
        for i in range(part_cols // step):
            total = dot(ref[:, i * step : (i + 1) * step], g, TN)
            for b in range(step // unit):
                quarters = [total[b * unit + r * ROWS :][:ROWS] for r in range(4)]
                first = jnp.concatenate([quarters[0], quarters[2]], 0)
                second = jnp.concatenate([quarters[1], quarters[3]], 0)
                by = lax.rem(b % Y + Y - y, Y)
                at = (i * step // unit + b) // Y
                t = lax.bitwise_xor(of * (Z // MP) + at, z)
                mine_ref[by, t] = jnp.where(c == 0, first, second).astype(bf16)
                rest_ref[by, t] = jnp.where(c == 0, second, first).astype(bf16)
    for by in range(Y):
        rest_refs[by][...] = rest_ref[by]


def terms(where, tokens, others, grads):
    n = grads.shape[1]
    vm = pl.BlockSpec(memory_space=pltpu.VMEM)
    shape = (Y, Z, XH * ROWS, n)
    return pl.pallas_call(
        term_kernel,
        out_shape=[jax.ShapeDtypeStruct(shape, bf16)] + [jax.ShapeDtypeStruct(shape[1:], bf16)] * Y,
        in_specs=[pl.BlockSpec(memory_space=pltpu.SMEM)] + [vm] * 3,
        out_specs=[vm] * (1 + Y),
        scratch_shapes=[pltpu.VMEM(shape, bf16)],
        compiler_params=pltpu.CompilerParams(vmem_limit_bytes=48 * 2**20),
        cost_estimate=pl.CostEstimate(
            flops=2 * 512 * 1536 * n, bytes_accessed=8 * 2**20, transcendentals=0
        ),
        name="weight_terms",
    )(where, tokens, others, grads)


FR = ("z", "y", "xh", "c")
PAIR = [(0, 1), (1, 0)]


def shift(x, axis, size, by):
    return lax.ppermute(x, axis, [(i, (i + by) % size) for i in range(size)])


def across(x, axis, size, by):
    return lax.ppermute(x, axis, [(i, i ^ by) for i in range(size)])


ZX = ("z", "xh")


def over_xh_and_pair(w):
    even = lax.axis_index("xh") == 0
    a, b, d = (across(w, ZX, Z * XH, by) for by in (1, 2, 3))
    first = jnp.concatenate([jnp.where(even, w, a), jnp.where(even, a, w)], 0)
    second = jnp.concatenate([jnp.where(even, b, d), jnp.where(even, d, b)], 0)
    return jnp.stack([first, second], 0)


def over_y(own):
    before = shift(own, "y", Y, 1)
    after = shift(own, "y", Y, Y - 1)
    low = shift(before[: Z // 2], "y", Y, 1)
    high = shift(after[Z // 2 :], "y", Y, Y - 1)
    return [own, after, before, low, high]


def reduce_weight(mine, rest, got, finish, late):
    even = lax.axis_index("xh") == 0
    rest = list(rest)
    rest[2] = lax.ppermute(rest[2], "c", PAIR)
    other = [rest[i] if i == 2 else lax.ppermute(rest[i], "c", PAIR) for i in range(Y)]
    h = Z // 2
    own, after, far, before = (mine[i].astype(f32) + other[i].astype(f32) for i in range(Y))
    up_far = shift(far[:h].astype(bf16), "y", Y, 1)
    down_far = shift(far[h:].astype(bf16), "y", Y, Y - 1)
    up_high = shift(after[h:].astype(bf16), "y", Y, 1)
    down_low = shift(before[:h].astype(bf16), "y", Y, Y - 1)
    up_far, down_far, got = lax.optimization_barrier((up_far, down_far, got))
    summed = finish(got)
    up_low = (after[:h] + up_far.astype(f32)).astype(bf16)
    down_high = (before[h:] + down_far.astype(f32)).astype(bf16)
    up_low, down_high, summed = lax.optimization_barrier((up_low, down_high, summed))
    up_low = shift(up_low, "y", Y, 1)
    down_high = shift(down_high, "y", Y, Y - 1)
    low = own[:h] + up_low.astype(f32) + down_low.astype(f32)
    high = own[h:] + up_high.astype(f32) + down_high.astype(f32)
    blocks = jnp.concatenate([low, high], 0)
    kept = jnp.where(even, blocks[:, :ROWS], blocks[:, ROWS:])
    sent = jnp.where(even, blocks[:, ROWS:], blocks[:, :ROWS])
    total = kept[0::2]
    for by, x in ((2, kept[1::2]), (1, sent[0::2]), (3, sent[1::2])):
        total = total + across(x.astype(bf16), ZX, Z * XH, by).astype(f32)
    back = late(summed)
    total, back = lax.optimization_barrier((total, back))
    result = total[0]
    for i in range(1, h):
        result = result + across(total[i].astype(bf16), "z", Z, 2 * i).astype(f32)
    return result, back


def on_device(normed, out_grad, w_qkv):
    frames_dev, patches, width = normed.shape
    half = out_grad.shape[2]
    cols = width // MP
    count = patches // F
    n = 3 * half
    where = jnp.stack([lax.axis_index(a) for a in ("z", "y", "c", "mp")]).astype(jnp.int32)
    m = lax.axis_index("mp")
    part = lax.dynamic_slice_in_dim(normed, m * cols, cols, 2)
    tokens = jnp.concatenate([part, out_grad], axis=2).reshape(F, count, cols + half)

    pair = over_xh_and_pair(w_qkv.reshape(w_qkv.shape[0], n))
    tokens, pair = lax.optimization_barrier((tokens, pair))
    tokens = lax.all_to_all(tokens, FR, 0, 0, tiled=True)
    own = jnp.concatenate([pair] + [across(pair, "z", Z, 2 * i) for i in range(1, Z // 2)], 0)
    part = tokens[:, :, :cols]
    own, part = lax.optimization_barrier((own, part))
    others = lax.ppermute(part, "mp", PAIR)
    mine = over_y(own)
    others = others.reshape(F * count, cols)
    tokens = tokens.reshape(F * count, cols + half)
    rest = [lax.ppermute(p, "c", PAIR) for p in mine[:3]]
    mine, others, tokens = lax.optimization_barrier((mine, others, tokens))
    rest = rest + [lax.ppermute(p, "c", PAIR) for p in mine[3:]]

    grads, give, keep = core(where, tokens, others, mine, rest)
    got = lax.ppermute(give, "mp", PAIR)

    def finish(got):
        return (keep.astype(f32) + got.astype(f32)).astype(bf16)

    def to_frames(x):
        return lax.all_to_all(x.reshape(F, count, cols), FR, 0, 0, tiled=True)

    mine, *rest = terms(where, tokens, others, grads)
    weight_grad, back = reduce_weight(mine, rest, got, finish, to_frames)
    input_grad = back.reshape(frames_dev, patches, cols)
    weight_grad = weight_grad * (1.0 / F)
    return (input_grad, weight_grad.reshape(w_qkv.shape))


def solution(mesh):
    fine = Mesh(mesh.devices.reshape(Z, Y, XH, C, MP), ("z", "y", "xh", "c", "mp"))
    in_specs = (P(FR, None, None), P(FR, None, "mp"), P(FR, None, "mp"))
    out_specs = (P(FR, None, "mp"), P(FR, None, "mp"))
    return jax.shard_map(
        on_device, mesh=fine, in_specs=in_specs, out_specs=out_specs, check_vma=False
    )
```

```python
import jax
import jax.numpy as jnp
from jax import lax
from jax.experimental import pallas as pl
from jax.experimental.pallas import tpu as pltpu
from jax.sharding import Mesh, PartitionSpec as P

HEAD_DIM = 64
Z, Y, XH, C, MP = 8, 4, 2, 2, 2
F = 128
ROWS = 12
VMEM_LIMIT = 32 * 2**20
bf16, f32 = jnp.bfloat16, jnp.float32
NT = (((1,), (1,)), ((), ()))
TN = (((0,), (0,)), ((), ()))


def dot(a, b, dims):
    return lax.dot_general(a, b, dims, preferred_element_type=f32)


def core_kernel(where_ref, t_ref, o_ref, *refs):
    pieces = refs[:16]
    give_ref, keep_ref, mine_ref, rest_ref, w_ref, s_ref, d_ref, g_ref = refs[16:]
    z, y, c, m = (where_ref[i] for i in range(4))
    unit = XH * C * ROWS

    @pl.loop(0, Z // 2)
    def _(t):
        for i in range(8):
            by, high = i // 2, i % 2
            a = pieces[i][t].astype(f32)
            b = pieces[i + 8][t].astype(f32)
            first = jnp.where(c == 0, a, b)
            second = jnp.where(c == 0, b, a)
            rows = [first[:ROWS], second[:ROWS], first[ROWS:], second[ROWS:]]
            to = lax.bitwise_xor(z, t + high * (Z // 2)) * Y + lax.rem(by + y, Y)
            to = pl.ds(pl.multiple_of(to * unit, unit), unit)
            w_ref[to, :] = jnp.concatenate(rows, 0).astype(bf16)

    part_cols = o_ref.shape[1]
    rows, half = t_ref.shape[0], t_ref.shape[1] - part_cols
    count = rows // F
    scale = HEAD_DIM ** (-0.5)
    pairs = half // 128
    near = pl.ds(pl.multiple_of(m * part_cols, part_cols), part_cols)
    away = pl.ds(pl.multiple_of((1 - m) * part_cols, part_cols), part_cols)
    for j in range(3):
        cols = slice(j * half, (j + 1) * half)
        part = jnp.dot(t_ref[:, :part_cols], w_ref[near, cols], preferred_element_type=f32)
        part += jnp.dot(o_ref[...], w_ref[away, cols], preferred_element_type=f32)
        part = part.astype(bf16)
        for pair in range(pairs):
            s_ref[j * pairs + pair] = part[:, pair * 128 : (pair + 1) * 128].astype(f32)
    for pair in range(pairs):
        at = part_cols + pair * 128
        s_ref[3 * pairs + pair] = t_ref[:, at : at + 128].astype(f32)
    low = lax.broadcasted_iota(jnp.int32, (F, 128), 1) < HEAD_DIM
    zero = jnp.zeros((F, 128), f32)

    def split(v):
        return jnp.concatenate([jnp.where(low, v, zero), jnp.where(low, zero, v)], 0).astype(bf16)

    @pl.loop(0, count)
    def _(p):
        at = pl.ds(p, F, stride=count)
        for pair in range(pairs):
            q, k, v, u = (s_ref[j * pairs + pair, at, :] for j in range(4))
            q2 = split(q * scale)
            u2 = split(u)
            k = k.astype(bf16)
            v = v.astype(bf16)
            weights = jnp.exp(dot(q2, k, NT))
            weights = weights / jnp.sum(weights, axis=-1, keepdims=True)
            dprobs = dot(u2, v, NT)
            center = jnp.sum(weights * dprobs, axis=-1, keepdims=True)
            dscores = (weights * (dprobs - center)).astype(bf16)
            dv = dot(weights.astype(bf16), u2, TN)
            dk = dot(dscores, q2, TN)
            both = jnp.dot(dscores, k, preferred_element_type=f32) * scale
            dq = jnp.where(low, both[:F], both[F:])
            for j, part in enumerate((dq, dk, dv)):
                d_ref[j * pairs + pair, at, :] = part
    g = jnp.concatenate([d_ref[i] for i in range(3 * pairs)], 1).astype(bf16)
    g_ref[...] = g
    give_ref[...] = dot(g, w_ref[away, :], NT).astype(bf16)
    keep_ref[...] = dot(g, w_ref[near, :], NT).astype(bf16)
    step = 384
    for ref, of in ((t_ref, m), (o_ref, 1 - m)):

        @pl.loop(0, part_cols // step)
        def _(i, ref=ref, of=of):
            total = dot(ref[:, pl.ds(pl.multiple_of(i * step, step), step)], g_ref[...], TN)
            for b in range(step // unit):
                quarters = [total[b * unit + r * ROWS :][:ROWS] for r in range(4)]
                first = jnp.concatenate([quarters[0], quarters[2]], 0)
                second = jnp.concatenate([quarters[1], quarters[3]], 0)
                by = lax.rem(b % Y + Y - y, Y)
                at = i * (step // unit // Y) + b // Y
                t = lax.bitwise_xor(of * (Z // MP) + at, z)
                mine_ref[by, t] = jnp.where(c == 0, first, second).astype(bf16)
                rest_ref[by, t] = jnp.where(c == 0, second, first).astype(bf16)


def core(where, tokens, others, mine, rest):
    rows, part_cols = others.shape
    half = tokens.shape[1] - part_cols
    width, n = MP * part_cols, 3 * half
    vm = pl.BlockSpec(memory_space=pltpu.VMEM)
    return pl.pallas_call(
        core_kernel,
        out_shape=(
            jax.ShapeDtypeStruct((rows, part_cols), bf16),
            jax.ShapeDtypeStruct((rows, part_cols), bf16),
            jax.ShapeDtypeStruct((Y, Z, XH * ROWS, n), bf16),
            jax.ShapeDtypeStruct((Y, Z, XH * ROWS, n), bf16),
        ),
        in_specs=[pl.BlockSpec(memory_space=pltpu.SMEM)] + [vm] * 18,
        out_specs=(vm,) * 4,
        scratch_shapes=[
            pltpu.VMEM((width, n), bf16),
            pltpu.VMEM((4 * half // 128, rows, 128), f32),
            pltpu.VMEM((3 * half // 128, rows, 128), f32),
            pltpu.VMEM((rows, n), bf16),
        ],
        compiler_params=pltpu.CompilerParams(vmem_limit_bytes=VMEM_LIMIT),
        cost_estimate=pl.CostEstimate(
            flops=6 * rows * width * n, bytes_accessed=8 * 2**20, transcendentals=0
        ),
        name="attention_core",
    )(where, tokens, others, *mine, *rest)


def combine_kernel(mine_ref, other_ref, *refs):
    own_ref, after_ref, before_ref, far_low, far_high, after_high, before_low = refs
    h = Z // 2

    def added(by, t):
        return mine_ref[by, t].astype(f32) + other_ref[by, t].astype(f32)

    @pl.loop(0, h)
    def _(t):
        far_low[t] = added(2, t).astype(bf16)
        far_high[t] = added(2, t + h).astype(bf16)
        own_ref[t] = added(0, t)
        own_ref[t + h] = added(0, t + h)
        after_ref[t] = added(1, t)
        after_high[t] = added(1, t + h).astype(bf16)
        before_low[t] = added(3, t).astype(bf16)
        before_ref[t] = added(3, t + h)


def combine(mine, other):
    vm = pl.BlockSpec(memory_space=pltpu.VMEM)
    block = mine.shape[2:]
    h = Z // 2
    return pl.pallas_call(
        combine_kernel,
        out_shape=[jax.ShapeDtypeStruct((n,) + block, f32) for n in (Z, h, h)]
        + [jax.ShapeDtypeStruct((h,) + block, bf16)] * 4,
        in_specs=[vm, vm],
        out_specs=[vm] * 7,
        compiler_params=pltpu.CompilerParams(vmem_limit_bytes=VMEM_LIMIT),
        cost_estimate=pl.CostEstimate(flops=0, bytes_accessed=2**20, transcendentals=0),
        name="combine_cores",
    )(mine, other)


FR = ("z", "y", "xh", "c")
PAIR = [(0, 1), (1, 0)]


def shift(x, axis, size, by):
    return lax.ppermute(x, axis, [(i, (i + by) % size) for i in range(size)])


def across(x, axis, size, by):
    return lax.ppermute(x, axis, [(i, i ^ by) for i in range(size)])


ZX = ("z", "xh")


def over_xh_and_pair(w):
    even = lax.axis_index("xh") == 0
    a, b, d = (across(w, ZX, Z * XH, by) for by in (1, 2, 3))
    first = jnp.concatenate([jnp.where(even, w, a), jnp.where(even, a, w)], 0)
    second = jnp.concatenate([jnp.where(even, b, d), jnp.where(even, d, b)], 0)
    return jnp.stack([first, second], 0)


def over_y(low, high):
    before_low = shift(low, "y", Y, 1)
    after_high = shift(high, "y", Y, Y - 1)
    before_high = shift(high, "y", Y, 1)
    after_low = shift(low, "y", Y, Y - 1)
    far_low = shift(before_low, "y", Y, 1)
    far_high = shift(after_high, "y", Y, Y - 1)
    return [low, high, after_low, after_high, far_low, far_high, before_low, before_high]


def reduce_weight(mine, rest, got, finish, late):
    even = lax.axis_index("xh") == 0
    other = lax.ppermute(rest, "c", PAIR)
    h = Z // 2
    own, after, before, far_low, far_high, after_high, before_low = combine(mine, other)
    up_far = shift(far_low, "y", Y, 1)
    down_far = shift(far_high, "y", Y, Y - 1)
    up_high = shift(after_high, "y", Y, 1)
    down_low = shift(before_low, "y", Y, Y - 1)
    up_far, down_far, got = lax.optimization_barrier((up_far, down_far, got))
    summed = finish(got)
    up_low = (after + up_far.astype(f32)).astype(bf16)
    down_high = (before + down_far.astype(f32)).astype(bf16)
    up_low, down_high, summed = lax.optimization_barrier((up_low, down_high, summed))
    up_low = shift(up_low, "y", Y, 1)
    down_high = shift(down_high, "y", Y, Y - 1)
    low = own[:h] + up_low.astype(f32) + down_low.astype(f32)
    high = own[h:] + up_high.astype(f32) + down_high.astype(f32)
    blocks = jnp.concatenate([low, high], 0)
    kept = jnp.where(even, blocks[:, :ROWS], blocks[:, ROWS:])
    sent = jnp.where(even, blocks[:, ROWS:], blocks[:, :ROWS])
    total = kept[0::2]
    for by, x in ((2, kept[1::2]), (1, sent[0::2]), (3, sent[1::2])):
        total = total + across(x.astype(bf16), ZX, Z * XH, by).astype(f32)
    back = late(summed)
    total, back = lax.optimization_barrier((total, back))
    result = total[0]
    for i in range(1, h):
        result = result + across(total[i].astype(bf16), "z", Z, 2 * i).astype(f32)
    return result, back


def on_device(normed, out_grad, w_qkv):
    frames_dev, patches, width = normed.shape
    half = out_grad.shape[2]
    cols = width // MP
    count = patches // F
    n = 3 * half
    where = jnp.stack([lax.axis_index(a) for a in ("z", "y", "c", "mp")]).astype(jnp.int32)
    m = lax.axis_index("mp")
    part = lax.dynamic_slice_in_dim(normed, m * cols, cols, 2)
    tokens = jnp.concatenate([part, out_grad], axis=2).reshape(F, count, cols + half)

    pair = over_xh_and_pair(w_qkv.reshape(w_qkv.shape[0], n))
    tokens, pair = lax.optimization_barrier((tokens, pair))
    tokens = lax.all_to_all(tokens, FR, 0, 0, tiled=True)
    two, four, six = (across(pair, "z", Z, 2 * i) for i in range(1, Z // 2))
    low, high = jnp.concatenate([pair, two], 0), jnp.concatenate([four, six], 0)
    part = tokens[:, :, :cols]
    low, high, part = lax.optimization_barrier((low, high, part))
    others = lax.ppermute(part, "mp", PAIR)
    mine = over_y(low, high)
    others = others.reshape(F * count, cols)
    tokens = tokens.reshape(F * count, cols + half)
    rest = {i: lax.ppermute(mine[i], "c", PAIR) for i in (0, 1, 2, 3, 6, 7)}
    mine, others, tokens = lax.optimization_barrier((mine, others, tokens))
    rest.update({i: lax.ppermute(mine[i], "c", PAIR) for i in (4, 5)})

    rest = [rest[i] for i in range(8)]
    give, keep, mine, rest = core(where, tokens, others, mine, rest)
    got = lax.ppermute(give, "mp", PAIR)

    def finish(got):
        return (keep.astype(f32) + got.astype(f32)).astype(bf16)

    def to_frames(x):
        return lax.all_to_all(x.reshape(F, count, cols), FR, 0, 0, tiled=True)

    weight_grad, back = reduce_weight(mine, rest, got, finish, to_frames)
    input_grad = back.reshape(frames_dev, patches, cols)
    weight_grad = weight_grad * (1.0 / F)
    return (input_grad, weight_grad.reshape(w_qkv.shape))


def solution(mesh):
    fine = Mesh(mesh.devices.reshape(Z, Y, XH, C, MP), ("z", "y", "xh", "c", "mp"))
    in_specs = (P(FR, None, None), P(FR, None, "mp"), P(FR, None, "mp"))
    out_specs = (P(FR, None, "mp"), P(FR, None, "mp"))
    return jax.shard_map(
        on_device, mesh=fine, in_specs=in_specs, out_specs=out_specs, check_vma=False
    )
```

```python
import jax
import jax.numpy as jnp
from jax import lax
from jax.experimental import pallas as pl
from jax.experimental.pallas import tpu as pltpu
from jax.sharding import Mesh, PartitionSpec as P

HEAD_DIM = 64
Z, Y, XH, C, MP = 8, 4, 2, 2, 2
F = 128
ROWS = 12
VMEM_LIMIT = 20 * 2**20
FIRST = 320
bf16, f32 = jnp.bfloat16, jnp.float32
NT = (((1,), (1,)), ((), ()))
TN = (((0,), (0,)), ((), ()))


def dot(a, b, dims):
    return lax.dot_general(a, b, dims, preferred_element_type=f32)


def core_kernel(where_ref, t_ref, o_ref, *refs):
    pieces = refs[:16]
    give_ref, keep_ref, mine_ref, rest_ref, w_ref, s_ref, d_ref, g_ref = refs[16:]
    z, y, c, m = (where_ref[i] for i in range(4))
    unit = XH * C * ROWS

    @pl.loop(0, Z // 2)
    def _(t):
        for i in range(8):
            by, high = i // 2, i % 2
            a = pieces[i][t].astype(f32)
            b = pieces[i + 8][t].astype(f32)
            first = jnp.where(c == 0, a, b)
            second = jnp.where(c == 0, b, a)
            rows = [first[:ROWS], second[:ROWS], first[ROWS:], second[ROWS:]]
            to = lax.bitwise_xor(z, t + high * (Z // 2)) * Y + lax.rem(by + y, Y)
            to = pl.ds(pl.multiple_of(to * unit, unit), unit)
            w_ref[to, :] = jnp.concatenate(rows, 0).astype(bf16)

    part_cols = o_ref.shape[1]
    rows, half = t_ref.shape[0], t_ref.shape[1] - part_cols
    count = rows // F
    scale = HEAD_DIM ** (-0.5)
    pairs = half // 128
    near = pl.ds(pl.multiple_of(m * part_cols, part_cols), part_cols)
    away = pl.ds(pl.multiple_of((1 - m) * part_cols, part_cols), part_cols)
    for j in range(3):
        cols = slice(j * half, (j + 1) * half)
        part = jnp.dot(t_ref[:, :part_cols], w_ref[near, cols], preferred_element_type=f32)
        part += jnp.dot(o_ref[...], w_ref[away, cols], preferred_element_type=f32)
        part = part.astype(bf16)
        for pair in range(pairs):
            s_ref[j * pairs + pair] = part[:, pair * 128 : (pair + 1) * 128].astype(f32)
    for pair in range(pairs):
        at = part_cols + pair * 128
        s_ref[3 * pairs + pair] = t_ref[:, at : at + 128].astype(f32)
    low = lax.broadcasted_iota(jnp.int32, (F, 128), 1) < HEAD_DIM
    zero = jnp.zeros((F, 128), f32)

    def split(v):
        return jnp.concatenate([jnp.where(low, v, zero), jnp.where(low, zero, v)], 0).astype(bf16)

    @pl.loop(0, count)
    def _(p):
        at = pl.ds(p, F, stride=count)
        for pair in range(pairs):
            q, k, v, u = (s_ref[j * pairs + pair, at, :] for j in range(4))
            q2 = split(q * scale)
            u2 = split(u)
            k = k.astype(bf16)
            v = v.astype(bf16)
            weights = jnp.exp(dot(q2, k, NT))
            weights = weights / jnp.sum(weights, axis=-1, keepdims=True)
            dprobs = dot(u2, v, NT)
            center = jnp.sum(weights * dprobs, axis=-1, keepdims=True)
            dscores = (weights * (dprobs - center)).astype(bf16)
            dv = dot(weights.astype(bf16), u2, TN)
            dk = dot(dscores, q2, TN)
            both = jnp.dot(dscores, k, preferred_element_type=f32) * scale
            dq = jnp.where(low, both[:F], both[F:])
            for j, part in enumerate((dq, dk, dv)):
                d_ref[j * pairs + pair, at, :] = part
    g = jnp.concatenate([d_ref[i] for i in range(3 * pairs)], 1).astype(bf16)
    g_ref[...] = g
    give_ref[...] = dot(g, w_ref[away, :], NT).astype(bf16)
    keep_ref[...] = dot(g, w_ref[near, :], NT).astype(bf16)
    step = 384
    for ref, of in ((t_ref, m), (o_ref, 1 - m)):

        @pl.loop(0, part_cols // step)
        def _(i, ref=ref, of=of):
            total = dot(ref[:, pl.ds(pl.multiple_of(i * step, step), step)], g_ref[...], TN)
            for b in range(step // unit):
                quarters = [total[b * unit + r * ROWS :][:ROWS] for r in range(4)]
                first = jnp.concatenate([quarters[0], quarters[2]], 0)
                second = jnp.concatenate([quarters[1], quarters[3]], 0)
                by = lax.rem(b % Y + Y - y, Y)
                at = i * (step // unit // Y) + b // Y
                t = lax.bitwise_xor(of * (Z // MP) + at, z)
                mine_ref[by, t] = jnp.where(c == 0, first, second).astype(bf16)
                rest_ref[by, t] = jnp.where(c == 0, second, first).astype(bf16)


def core(where, tokens, others, mine, rest):
    rows, part_cols = others.shape
    half = tokens.shape[1] - part_cols
    width, n = MP * part_cols, 3 * half
    vm = pl.BlockSpec(memory_space=pltpu.VMEM)
    return pl.pallas_call(
        core_kernel,
        out_shape=(
            jax.ShapeDtypeStruct((rows, part_cols), bf16),
            jax.ShapeDtypeStruct((rows, part_cols), bf16),
            jax.ShapeDtypeStruct((Y, Z, XH * ROWS, n), bf16),
            jax.ShapeDtypeStruct((Y, Z, XH * ROWS, n), bf16),
        ),
        in_specs=[pl.BlockSpec(memory_space=pltpu.SMEM)] + [vm] * 18,
        out_specs=(vm,) * 4,
        scratch_shapes=[
            pltpu.VMEM((width, n), bf16),
            pltpu.VMEM((4 * half // 128, rows, 128), f32),
            pltpu.VMEM((3 * half // 128, rows, 128), f32),
            pltpu.VMEM((rows, n), bf16),
        ],
        compiler_params=pltpu.CompilerParams(vmem_limit_bytes=VMEM_LIMIT),
        cost_estimate=pl.CostEstimate(
            flops=6 * rows * width * n, bytes_accessed=8 * 2**20, transcendentals=0
        ),
        name="attention_core",
    )(where, tokens, others, *mine, *rest)


def combine_kernel(mine_ref, other_ref, *refs):
    own_ref, after_ref, before_ref, far_low, far_high, after_high, before_low = refs
    h = Z // 2

    def added(by, t):
        return mine_ref[by, t].astype(f32) + other_ref[by, t].astype(f32)

    @pl.loop(0, h)
    def _(t):
        far_low[t] = added(2, t).astype(bf16)
        far_high[t] = added(2, t + h).astype(bf16)
        own_ref[t] = added(0, t)
        own_ref[t + h] = added(0, t + h)
        after_ref[t] = added(1, t)
        after_high[t] = added(1, t + h).astype(bf16)
        before_low[t] = added(3, t).astype(bf16)
        before_ref[t] = added(3, t + h)


def combine(mine, other):
    vm = pl.BlockSpec(memory_space=pltpu.VMEM)
    block = mine.shape[2:]
    h = Z // 2
    return pl.pallas_call(
        combine_kernel,
        out_shape=[jax.ShapeDtypeStruct((n,) + block, f32) for n in (Z, h, h)]
        + [jax.ShapeDtypeStruct((h,) + block, bf16)] * 4,
        in_specs=[vm, vm],
        out_specs=[vm] * 7,
        compiler_params=pltpu.CompilerParams(vmem_limit_bytes=VMEM_LIMIT),
        cost_estimate=pl.CostEstimate(flops=0, bytes_accessed=2**20, transcendentals=0),
        name="combine_cores",
    )(mine, other)


FR = ("z", "y", "xh", "c")
PAIR = [(0, 1), (1, 0)]


def shift(x, axis, size, by):
    return lax.ppermute(x, axis, [(i, (i + by) % size) for i in range(size)])


def across(x, axis, size, by):
    return lax.ppermute(x, axis, [(i, i ^ by) for i in range(size)])


ZX = ("z", "xh")


def over_xh_and_pair(w):
    even = lax.axis_index("xh") == 0
    a, b, d = (across(w, ZX, Z * XH, by) for by in (1, 2, 3))
    first = jnp.concatenate([jnp.where(even, w, a), jnp.where(even, a, w)], 0)
    second = jnp.concatenate([jnp.where(even, b, d), jnp.where(even, d, b)], 0)
    return jnp.stack([first, second], 0)


def swapped(*xs):
    return [lax.ppermute(x, "c", PAIR) for x in xs]


def reduce_weight(mine, rest, first, second, finish, to_frames):
    even = lax.axis_index("xh") == 0
    other = lax.ppermute(rest, "c", PAIR)
    first = lax.ppermute(first, "mp", PAIR)
    h = Z // 2
    own, after, before, far_low, far_high, after_high, before_low = combine(mine, other)
    up_far = shift(far_low, "y", Y, 1)
    down_far = shift(far_high, "y", Y, Y - 1)
    up_high = shift(after_high, "y", Y, 1)
    down_low = shift(before_low, "y", Y, Y - 1)
    up_far, down_far, first, second = lax.optimization_barrier((up_far, down_far, first, second))
    second = lax.ppermute(second, "mp", PAIR)
    up_low = shift((after + up_far.astype(f32)).astype(bf16), "y", Y, 1)
    down_high = shift((before + down_far.astype(f32)).astype(bf16), "y", Y, Y - 1)
    low = own[:h] + up_low.astype(f32) + down_low.astype(f32)
    high = own[h:] + up_high.astype(f32) + down_high.astype(f32)
    blocks = jnp.concatenate([low, high], 0)
    kept = jnp.where(even, blocks[:, :ROWS], blocks[:, ROWS:])
    sent = jnp.where(even, blocks[:, ROWS:], blocks[:, :ROWS])
    total = kept[0::2]
    for by, x in ((2, kept[1::2]), (1, sent[0::2]), (3, sent[1::2])):
        total = total + across(x.astype(bf16), ZX, Z * XH, by).astype(f32)
    summed = finish(first, second)
    total, summed = lax.optimization_barrier((total, summed))
    back = to_frames(summed)
    result = total[0]
    for i in range(1, h):
        result = result + across(total[i].astype(bf16), "z", Z, 2 * i).astype(f32)
    return result, back


def on_device(normed, out_grad, w_qkv):
    frames_dev, patches, width = normed.shape
    half = out_grad.shape[2]
    cols = width // MP
    count = patches // F
    n = 3 * half
    where = jnp.stack([lax.axis_index(a) for a in ("z", "y", "c", "mp")]).astype(jnp.int32)
    m = lax.axis_index("mp")
    part = lax.dynamic_slice_in_dim(normed, m * cols, cols, 2)
    tokens = jnp.concatenate([part, out_grad], axis=2).reshape(F, count, cols + half)

    pair = over_xh_and_pair(w_qkv.reshape(w_qkv.shape[0], n))
    tokens, pair = lax.optimization_barrier((tokens, pair))
    tokens = lax.all_to_all(tokens, FR, 0, 0, tiled=True)
    two, four, six = (across(pair, "z", Z, 2 * i) for i in range(1, Z // 2))
    low, high = jnp.concatenate([pair, two], 0), jnp.concatenate([four, six], 0)
    part = tokens[:, :, :cols]
    low, high, part = lax.optimization_barrier((low, high, part))
    others = lax.ppermute(part, "mp", PAIR)
    before_low = shift(low, "y", Y, 1)
    after_high = shift(high, "y", Y, Y - 1)
    before_high = shift(high, "y", Y, 1)
    after_low = shift(low, "y", Y, Y - 1)
    tokens = tokens.reshape(F * count, cols + half)
    own = swapped(low, high)
    before_low, after_high, tokens, own = lax.optimization_barrier(
        (before_low, after_high, tokens, own)
    )
    far_low = shift(before_low, "y", Y, 1)
    far_high = shift(after_high, "y", Y, Y - 1)
    near = swapped(after_low, after_high, before_low, before_high)
    far_low, far_high, near, others = lax.optimization_barrier((far_low, far_high, near, others))
    others = others.reshape(F * count, cols)
    mine = [low, high, after_low, after_high, far_low, far_high, before_low, before_high]
    rest = own + near[:2] + swapped(far_low, far_high) + near[2:]
    give, keep, mine, rest = core(where, tokens, others, mine, rest)
    first, second = give[:FIRST], give[FIRST:]

    def finish(first, second):
        got = jnp.concatenate([first, second], 0)
        return (keep.astype(f32) + got.astype(f32)).astype(bf16)

    def to_frames(x):
        return lax.all_to_all(x.reshape(F, count, cols), FR, 0, 0, tiled=True)

    weight_grad, back = reduce_weight(mine, rest, first, second, finish, to_frames)
    input_grad = back.reshape(frames_dev, patches, cols)
    weight_grad = weight_grad * (1.0 / F)
    return (input_grad, weight_grad.reshape(w_qkv.shape))


def solution(mesh):
    fine = Mesh(mesh.devices.reshape(Z, Y, XH, C, MP), ("z", "y", "xh", "c", "mp"))
    in_specs = (P(FR, None, None), P(FR, None, "mp"), P(FR, None, "mp"))
    out_specs = (P(FR, None, "mp"), P(FR, None, "mp"))
    return jax.shard_map(
        on_device, mesh=fine, in_specs=in_specs, out_specs=out_specs, check_vma=False
    )
```

```python
import jax
import jax.numpy as jnp
from jax import lax
from jax.experimental import pallas as pl
from jax.experimental.pallas import tpu as pltpu
from jax.sharding import Mesh, PartitionSpec as P

HEAD_DIM = 64
Z, Y, XH, C, MP = 8, 4, 2, 2, 2
F = 128
ROWS = 12
VMEM_LIMIT = 40 * 2**20
CUTS = (192,)
bf16, f32 = jnp.bfloat16, jnp.float32
NT = (((1,), (1,)), ((), ()))
TN = (((0,), (0,)), ((), ()))


def dot(a, b, dims):
    return lax.dot_general(a, b, dims, preferred_element_type=f32)


def core_kernel(where_ref, t_ref, o_ref, *refs):
    blocks = refs[:16]
    give_ref, keep_ref, mine_ref, rest_ref, w_ref, s_ref, d_ref, g_ref, pieces, sems = refs[16:]
    copies = [pltpu.make_async_copy(blocks[i], pieces.at[i], sems.at[i]) for i in range(16)]
    for copy in copies:
        copy.start()
    z, y, c, m = (where_ref[i] for i in range(4))
    unit = XH * C * ROWS
    for copy in copies:
        copy.wait()

    @pl.loop(0, Z // 2)
    def _(t):
        for i in range(8):
            by, high = i // 2, i % 2
            a = pieces[i, t].astype(f32)
            b = pieces[i + 8, t].astype(f32)
            first = jnp.where(c == 0, a, b)
            second = jnp.where(c == 0, b, a)
            rows = [first[:ROWS], second[:ROWS], first[ROWS:], second[ROWS:]]
            to = lax.bitwise_xor(z, t + high * (Z // 2)) * Y + lax.rem(by + y, Y)
            to = pl.ds(pl.multiple_of(to * unit, unit), unit)
            w_ref[to, :] = jnp.concatenate(rows, 0).astype(bf16)

    part_cols = o_ref.shape[1]
    rows, half = t_ref.shape[0], t_ref.shape[1] - part_cols
    count = rows // F
    scale = HEAD_DIM ** (-0.5)
    pairs = half // 128
    near = pl.ds(pl.multiple_of(m * part_cols, part_cols), part_cols)
    away = pl.ds(pl.multiple_of((1 - m) * part_cols, part_cols), part_cols)
    for j in range(3):
        cols = slice(j * half, (j + 1) * half)
        part = jnp.dot(t_ref[:, :part_cols], w_ref[near, cols], preferred_element_type=f32)
        part += jnp.dot(o_ref[...], w_ref[away, cols], preferred_element_type=f32)
        part = part.astype(bf16)
        for pair in range(pairs):
            s_ref[j * pairs + pair] = part[:, pair * 128 : (pair + 1) * 128].astype(f32)
    for pair in range(pairs):
        at = part_cols + pair * 128
        s_ref[3 * pairs + pair] = t_ref[:, at : at + 128].astype(f32)
    low = lax.broadcasted_iota(jnp.int32, (F, 128), 1) < HEAD_DIM
    zero = jnp.zeros((F, 128), f32)

    def split(v):
        return jnp.concatenate([jnp.where(low, v, zero), jnp.where(low, zero, v)], 0).astype(bf16)

    @pl.loop(0, count)
    def _(p):
        at = pl.ds(p, F, stride=count)
        for pair in range(pairs):
            q, k, v, u = (s_ref[j * pairs + pair, at, :] for j in range(4))
            q2 = split(q * scale)
            u2 = split(u)
            k = k.astype(bf16)
            v = v.astype(bf16)
            weights = jnp.exp(dot(q2, k, NT))
            weights = weights / jnp.sum(weights, axis=-1, keepdims=True)
            dprobs = dot(u2, v, NT)
            center = jnp.sum(weights * dprobs, axis=-1, keepdims=True)
            dscores = (weights * (dprobs - center)).astype(bf16)
            dv = dot(weights.astype(bf16), u2, TN)
            dk = dot(dscores, q2, TN)
            both = jnp.dot(dscores, k, preferred_element_type=f32) * scale
            dq = jnp.where(low, both[:F], both[F:])
            for j, part in enumerate((dq, dk, dv)):
                d_ref[j * pairs + pair, at, :] = part
    g = jnp.concatenate([d_ref[i] for i in range(3 * pairs)], 1).astype(bf16)
    g_ref[...] = g
    give_ref[...] = dot(g, w_ref[away, :], NT).astype(bf16)
    keep_ref[...] = dot(g, w_ref[near, :], NT).astype(bf16)
    step = 384
    for ref, of in ((t_ref, m), (o_ref, 1 - m)):

        @pl.loop(0, part_cols // step)
        def _(i, ref=ref, of=of):
            total = dot(ref[:, pl.ds(pl.multiple_of(i * step, step), step)], g_ref[...], TN)
            for b in range(step // unit):
                quarters = [total[b * unit + r * ROWS :][:ROWS] for r in range(4)]
                first = jnp.concatenate([quarters[0], quarters[2]], 0)
                second = jnp.concatenate([quarters[1], quarters[3]], 0)
                by = lax.rem(b % Y + Y - y, Y)
                at = i * (step // unit // Y) + b // Y
                t = lax.bitwise_xor(of * (Z // MP) + at, z)
                mine_ref[by, t] = jnp.where(c == 0, first, second).astype(bf16)
                rest_ref[by, t] = jnp.where(c == 0, second, first).astype(bf16)


def core(where, tokens, others, mine, rest):
    rows, part_cols = others.shape
    half = tokens.shape[1] - part_cols
    width, n = MP * part_cols, 3 * half
    vm = pl.BlockSpec(memory_space=pltpu.VMEM)
    return pl.pallas_call(
        core_kernel,
        out_shape=(
            jax.ShapeDtypeStruct((rows, part_cols), bf16),
            jax.ShapeDtypeStruct((rows, part_cols), bf16),
            jax.ShapeDtypeStruct((Y, Z, XH * ROWS, n), bf16),
            jax.ShapeDtypeStruct((Y, Z, XH * ROWS, n), bf16),
        ),
        in_specs=[pl.BlockSpec(memory_space=pltpu.SMEM), vm, vm]
        + [pl.BlockSpec(memory_space=pl.ANY)] * 16,
        out_specs=(vm,) * 4,
        scratch_shapes=[
            pltpu.VMEM((width, n), bf16),
            pltpu.VMEM((4 * half // 128, rows, 128), f32),
            pltpu.VMEM((3 * half // 128, rows, 128), f32),
            pltpu.VMEM((rows, n), bf16),
            pltpu.VMEM((16,) + mine[0].shape, bf16),
            pltpu.SemaphoreType.DMA((16,)),
        ],
        compiler_params=pltpu.CompilerParams(vmem_limit_bytes=VMEM_LIMIT),
        cost_estimate=pl.CostEstimate(
            flops=6 * rows * width * n, bytes_accessed=8 * 2**20, transcendentals=0
        ),
        name="attention_core",
    )(where, tokens, others, *mine, *rest)


def combine_kernel(mine_ref, other_ref, *refs):
    own_ref, after_ref, before_ref, far_low, far_high, after_high, before_low = refs
    h = Z // 2

    def added(by, t):
        return mine_ref[by, t].astype(f32) + other_ref[by, t].astype(f32)

    @pl.loop(0, h)
    def _(t):
        far_low[t] = added(2, t).astype(bf16)
        far_high[t] = added(2, t + h).astype(bf16)
        own_ref[t] = added(0, t)
        own_ref[t + h] = added(0, t + h)
        after_ref[t] = added(1, t)
        after_high[t] = added(1, t + h).astype(bf16)
        before_low[t] = added(3, t).astype(bf16)
        before_ref[t] = added(3, t + h)


def combine(mine, other):
    vm = pl.BlockSpec(memory_space=pltpu.VMEM)
    block = mine.shape[2:]
    h = Z // 2
    return pl.pallas_call(
        combine_kernel,
        out_shape=[jax.ShapeDtypeStruct((n,) + block, f32) for n in (Z, h, h)]
        + [jax.ShapeDtypeStruct((h,) + block, bf16)] * 4,
        in_specs=[vm, vm],
        out_specs=[vm] * 7,
        compiler_params=pltpu.CompilerParams(vmem_limit_bytes=VMEM_LIMIT),
        cost_estimate=pl.CostEstimate(flops=0, bytes_accessed=2**20, transcendentals=0),
        name="combine_cores",
    )(mine, other)


FR = ("z", "y", "xh", "c")
PAIR = [(0, 1), (1, 0)]


def shift(x, axis, size, by):
    return lax.ppermute(x, axis, [(i, (i + by) % size) for i in range(size)])


def across(x, axis, size, by):
    return lax.ppermute(x, axis, [(i, i ^ by) for i in range(size)])


ZX = ("z", "xh")


def over_xh_and_pair(w):
    even = lax.axis_index("xh") == 0
    a, b, d = (across(w, ZX, Z * XH, by) for by in (1, 2, 3))
    first = jnp.concatenate([jnp.where(even, w, a), jnp.where(even, a, w)], 0)
    second = jnp.concatenate([jnp.where(even, b, d), jnp.where(even, d, b)], 0)
    return jnp.stack([first, second], 0)


def swapped(*xs):
    return [lax.ppermute(x, "c", PAIR) for x in xs]


def reduce_weight(mine, rest, parts, finish, to_frames):
    first, second = parts
    even = lax.axis_index("xh") == 0
    other = lax.ppermute(rest, "c", PAIR)
    first = lax.ppermute(first, "mp", PAIR)
    h = Z // 2
    own, after, before, far_low, far_high, after_high, before_low = combine(mine, other)
    up_far = shift(far_low, "y", Y, 1)
    down_far = shift(far_high, "y", Y, Y - 1)
    up_high = shift(after_high, "y", Y, 1)
    down_low = shift(before_low, "y", Y, Y - 1)
    up_far, down_far, first, second = lax.optimization_barrier((up_far, down_far, first, second))
    second = lax.ppermute(second, "mp", PAIR)
    up_low = shift((after + up_far.astype(f32)).astype(bf16), "y", Y, 1)
    down_high = shift((before + down_far.astype(f32)).astype(bf16), "y", Y, Y - 1)
    low = own[:h] + up_low.astype(f32) + down_low.astype(f32)
    high = own[h:] + up_high.astype(f32) + down_high.astype(f32)
    blocks = jnp.concatenate([low, high], 0)
    kept = jnp.where(even, blocks[:, :ROWS], blocks[:, ROWS:])
    sent = jnp.where(even, blocks[:, ROWS:], blocks[:, :ROWS])
    total = kept[0::2]
    for by, x in ((2, kept[1::2]), (1, sent[0::2]), (3, sent[1::2])):
        total = total + across(x.astype(bf16), ZX, Z * XH, by).astype(f32)
    summed = finish(first, second)
    total, summed = lax.optimization_barrier((total, summed))
    back = to_frames(summed)
    result = total[0]
    for i in range(1, h):
        result = result + across(total[i].astype(bf16), "z", Z, 2 * i).astype(f32)
    return result, back


def on_device(normed, out_grad, w_qkv):
    frames_dev, patches, width = normed.shape
    half = out_grad.shape[2]
    cols = width // MP
    count = patches // F
    n = 3 * half
    where = jnp.stack([lax.axis_index(a) for a in ("z", "y", "c", "mp")]).astype(jnp.int32)
    m = lax.axis_index("mp")
    part = lax.dynamic_slice_in_dim(normed, m * cols, cols, 2)
    tokens = jnp.concatenate([part, out_grad], axis=2).reshape(F, count, cols + half)

    pair = over_xh_and_pair(w_qkv.reshape(w_qkv.shape[0], n))
    tokens, pair = lax.optimization_barrier((tokens, pair))
    tokens = lax.all_to_all(tokens, FR, 0, 0, tiled=True)
    two, four, six = (across(pair, "z", Z, 2 * i) for i in range(1, Z // 2))
    low, high = jnp.concatenate([pair, two], 0), jnp.concatenate([four, six], 0)
    part = tokens[:, :, :cols]
    low, high, part = lax.optimization_barrier((low, high, part))
    others = lax.ppermute(part, "mp", PAIR)
    before_low = shift(low, "y", Y, 1)
    after_high = shift(high, "y", Y, Y - 1)
    before_high = shift(high, "y", Y, 1)
    after_low = shift(low, "y", Y, Y - 1)
    far_low = shift(before_low, "y", Y, 1)
    far_high = shift(after_high, "y", Y, Y - 1)
    tokens = tokens.reshape(F * count, cols + half)
    own = swapped(low, high)
    near = [after_low, after_high, before_low, before_high]
    near, own, tokens = lax.optimization_barrier((near, own, tokens))
    near_rest = swapped(*near)
    far = [far_low, far_high]
    far, near_rest, others = lax.optimization_barrier((far, near_rest, others))
    others = others.reshape(F * count, cols)
    mine = [low, high] + near[:2] + far + near[2:]
    rest = own + near_rest[:2] + swapped(*far) + near_rest[2:]
    give, keep, mine, rest = core(where, tokens, others, mine, rest)
    parts = jnp.split(give, CUTS)

    def finish(*got):
        got = jnp.concatenate(got, 0)
        return (keep.astype(f32) + got.astype(f32)).astype(bf16)

    def to_frames(x):
        return lax.all_to_all(x.reshape(F, count, cols), FR, 0, 0, tiled=True)

    weight_grad, back = reduce_weight(mine, rest, parts, finish, to_frames)
    input_grad = back.reshape(frames_dev, patches, cols)
    weight_grad = weight_grad * (1.0 / F)
    return (input_grad, weight_grad.reshape(w_qkv.shape))


def solution(mesh):
    fine = Mesh(mesh.devices.reshape(Z, Y, XH, C, MP), ("z", "y", "xh", "c", "mp"))
    in_specs = (P(FR, None, None), P(FR, None, "mp"), P(FR, None, "mp"))
    out_specs = (P(FR, None, "mp"), P(FR, None, "mp"))
    return jax.shard_map(
        on_device, mesh=fine, in_specs=in_specs, out_specs=out_specs, check_vma=False
    )
```

```python
import jax
import jax.numpy as jnp
from jax import lax
from jax.experimental import pallas as pl
from jax.experimental.pallas import tpu as pltpu
from jax.sharding import Mesh, PartitionSpec as P

HEAD_DIM = 64
Z, Y, XH, C, MP = 8, 4, 2, 2, 2
F = 128
ROWS = 12
VMEM_LIMIT = 32 * 2**20
bf16, f32 = jnp.bfloat16, jnp.float32
NT = (((1,), (1,)), ((), ()))
TN = (((0,), (0,)), ((), ()))


def dot(a, b, dims):
    return lax.dot_general(a, b, dims, preferred_element_type=f32)


def core_kernel(where_ref, t_ref, o_ref, *refs):
    pieces = refs[:16]
    give_ref, keep_ref, mine_ref, rest_ref, w_ref, s_ref, d_ref, g_ref = refs[16:]
    z, y, c, m = (where_ref[i] for i in range(4))
    unit = XH * C * ROWS

    @pl.loop(0, Z // 2)
    def _(t):
        for i in range(8):
            by, high = i // 2, i % 2
            a = pieces[i][t].astype(f32)
            b = pieces[i + 8][t].astype(f32)
            first = jnp.where(c == 0, a, b)
            second = jnp.where(c == 0, b, a)
            rows = [first[:ROWS], second[:ROWS], first[ROWS:], second[ROWS:]]
            to = lax.bitwise_xor(z, t + high * (Z // 2)) * Y + lax.rem(by + y, Y)
            to = pl.ds(pl.multiple_of(to * unit, unit), unit)
            w_ref[to, :] = jnp.concatenate(rows, 0).astype(bf16)

    part_cols = o_ref.shape[1]
    rows, half = t_ref.shape[0], t_ref.shape[1] - part_cols
    count = rows // F
    scale = HEAD_DIM ** (-0.5)
    pairs = half // 128
    near = pl.ds(pl.multiple_of(m * part_cols, part_cols), part_cols)
    away = pl.ds(pl.multiple_of((1 - m) * part_cols, part_cols), part_cols)
    for j in range(3):
        cols = slice(j * half, (j + 1) * half)
        part = jnp.dot(t_ref[:, :part_cols], w_ref[near, cols], preferred_element_type=f32)
        part += jnp.dot(o_ref[...], w_ref[away, cols], preferred_element_type=f32)
        part = part.astype(bf16)
        for pair in range(pairs):
            s_ref[j * pairs + pair] = part[:, pair * 128 : (pair + 1) * 128].astype(f32)
    for pair in range(pairs):
        at = part_cols + pair * 128
        s_ref[3 * pairs + pair] = t_ref[:, at : at + 128].astype(f32)
    low = lax.broadcasted_iota(jnp.int32, (F, 128), 1) < HEAD_DIM
    zero = jnp.zeros((F, 128), f32)

    def split(v):
        return jnp.concatenate([jnp.where(low, v, zero), jnp.where(low, zero, v)], 0).astype(bf16)

    @pl.loop(0, count)
    def _(p):
        at = pl.ds(p, F, stride=count)
        for pair in range(pairs):
            q, k, v, u = (s_ref[j * pairs + pair, at, :] for j in range(4))
            q2 = split(q * scale)
            u2 = split(u)
            k = k.astype(bf16)
            v = v.astype(bf16)
            weights = jnp.exp(dot(q2, k, NT))
            weights = weights / jnp.sum(weights, axis=-1, keepdims=True)
            dprobs = dot(u2, v, NT)
            center = jnp.sum(weights * dprobs, axis=-1, keepdims=True)
            dscores = (weights * (dprobs - center)).astype(bf16)
            dv = dot(weights.astype(bf16), u2, TN)
            dk = dot(dscores, q2, TN)
            both = jnp.dot(dscores, k, preferred_element_type=f32) * scale
            dq = jnp.where(low, both[:F], both[F:])
            for j, part in enumerate((dq, dk, dv)):
                d_ref[j * pairs + pair, at, :] = part
    g = jnp.concatenate([d_ref[i] for i in range(3 * pairs)], 1).astype(bf16)
    g_ref[...] = g
    give_ref[...] = dot(g, w_ref[away, :], NT).astype(bf16)
    keep_ref[...] = dot(g, w_ref[near, :], NT).astype(bf16)
    step = 384
    for ref, of in ((t_ref, m), (o_ref, 1 - m)):

        @pl.loop(0, part_cols // step)
        def _(i, ref=ref, of=of):
            total = dot(ref[:, pl.ds(pl.multiple_of(i * step, step), step)], g_ref[...], TN)
            for b in range(step // unit):
                quarters = [total[b * unit + r * ROWS :][:ROWS] for r in range(4)]
                first = jnp.concatenate([quarters[0], quarters[2]], 0)
                second = jnp.concatenate([quarters[1], quarters[3]], 0)
                by = lax.rem(b % Y + Y - y, Y)
                at = i * (step // unit // Y) + b // Y
                t = lax.bitwise_xor(of * (Z // MP) + at, z)
                mine_ref[by, t] = jnp.where(c == 0, first, second).astype(bf16)
                rest_ref[by, t] = jnp.where(c == 0, second, first).astype(bf16)


def core(where, tokens, others, mine, rest):
    rows, part_cols = others.shape
    half = tokens.shape[1] - part_cols
    width, n = MP * part_cols, 3 * half
    vm = pl.BlockSpec(memory_space=pltpu.VMEM)
    return pl.pallas_call(
        core_kernel,
        out_shape=(
            jax.ShapeDtypeStruct((rows, part_cols), bf16),
            jax.ShapeDtypeStruct((rows, part_cols), bf16),
            jax.ShapeDtypeStruct((Y, Z, XH * ROWS, n), bf16),
            jax.ShapeDtypeStruct((Y, Z, XH * ROWS, n), bf16),
        ),
        in_specs=[pl.BlockSpec(memory_space=pltpu.SMEM)] + [vm] * 18,
        out_specs=(vm,) * 4,
        scratch_shapes=[
            pltpu.VMEM((width, n), bf16),
            pltpu.VMEM((4 * half // 128, rows, 128), f32),
            pltpu.VMEM((3 * half // 128, rows, 128), f32),
            pltpu.VMEM((rows, n), bf16),
        ],
        compiler_params=pltpu.CompilerParams(vmem_limit_bytes=VMEM_LIMIT),
        cost_estimate=pl.CostEstimate(
            flops=6 * rows * width * n, bytes_accessed=8 * 2**20, transcendentals=0
        ),
        name="attention_core",
    )(where, tokens, others, *mine, *rest)


def combine_kernel(mine_ref, other_ref, *refs):
    own_ref, after_ref, before_ref, far_low, far_high, after_high, before_low = refs
    h = Z // 2

    def added(by, t):
        return mine_ref[by, t].astype(f32) + other_ref[by, t].astype(f32)

    @pl.loop(0, h)
    def _(t):
        far_low[t] = added(2, t).astype(bf16)
        far_high[t] = added(2, t + h).astype(bf16)
        own_ref[t] = added(0, t)
        own_ref[t + h] = added(0, t + h)
        after_ref[t] = added(1, t)
        after_high[t] = added(1, t + h).astype(bf16)
        before_low[t] = added(3, t).astype(bf16)
        before_ref[t] = added(3, t + h)


def combine(mine, other):
    vm = pl.BlockSpec(memory_space=pltpu.VMEM)
    block = mine.shape[2:]
    h = Z // 2
    return pl.pallas_call(
        combine_kernel,
        out_shape=[jax.ShapeDtypeStruct((n,) + block, f32) for n in (Z, h, h)]
        + [jax.ShapeDtypeStruct((h,) + block, bf16)] * 4,
        in_specs=[vm, vm],
        out_specs=[vm] * 7,
        compiler_params=pltpu.CompilerParams(vmem_limit_bytes=VMEM_LIMIT),
        cost_estimate=pl.CostEstimate(flops=0, bytes_accessed=2**20, transcendentals=0),
        name="combine_cores",
    )(mine, other)


FR = ("z", "y", "xh", "c")
PAIR = [(0, 1), (1, 0)]


def shift(x, axis, size, by):
    return lax.ppermute(x, axis, [(i, (i + by) % size) for i in range(size)])


def across(x, axis, size, by):
    return lax.ppermute(x, axis, [(i, i ^ by) for i in range(size)])


ZX = ("z", "xh")


def over_xh_and_pair(w):
    even = lax.axis_index("xh") == 0
    a, b, d = (across(w, ZX, Z * XH, by) for by in (1, 2, 3))
    first = jnp.concatenate([jnp.where(even, w, a), jnp.where(even, a, w)], 0)
    second = jnp.concatenate([jnp.where(even, b, d), jnp.where(even, d, b)], 0)
    return jnp.stack([first, second], 0)


def over_y(low, high):
    before_low = shift(low, "y", Y, 1)
    after_high = shift(high, "y", Y, Y - 1)
    before_high = shift(high, "y", Y, 1)
    after_low = shift(low, "y", Y, Y - 1)
    far_low = shift(before_low, "y", Y, 1)
    far_high = shift(after_high, "y", Y, Y - 1)
    return [low, high, after_low, after_high, far_low, far_high, before_low, before_high]


def reduce_weight(mine, rest, got, finish, late):
    even = lax.axis_index("xh") == 0
    other = lax.ppermute(rest, "c", PAIR)
    h = Z // 2
    own, after, before, far_low, far_high, after_high, before_low = combine(mine, other)
    up_far = shift(far_low, "y", Y, 1)
    down_far = shift(far_high, "y", Y, Y - 1)
    up_high = shift(after_high, "y", Y, 1)
    down_low = shift(before_low, "y", Y, Y - 1)
    up_far, down_far, got = lax.optimization_barrier((up_far, down_far, got))
    summed = finish(got)
    up_low = (after + up_far.astype(f32)).astype(bf16)
    down_high = (before + down_far.astype(f32)).astype(bf16)
    up_low, down_high, summed = lax.optimization_barrier((up_low, down_high, summed))
    up_low = shift(up_low, "y", Y, 1)
    down_high = shift(down_high, "y", Y, Y - 1)
    low = own[:h] + up_low.astype(f32) + down_low.astype(f32)
    high = own[h:] + up_high.astype(f32) + down_high.astype(f32)
    blocks = jnp.concatenate([low, high], 0)
    pair = blocks[:2]
    for i in range(1, h):
        sent = blocks[2 * i : 2 * i + 2].astype(bf16)
        pair = pair + across(sent, "z", Z, 2 * i).astype(f32)
    back = late(summed)
    pair, back = lax.optimization_barrier((pair, back))
    kept = jnp.where(even, pair[:, :ROWS], pair[:, ROWS:])
    sent = jnp.where(even, pair[:, ROWS:], pair[:, :ROWS])
    result = kept[0]
    for by, x in ((1, sent[0]), (3, sent[1]), (2, kept[1])):
        result = result + across(x.astype(bf16), ZX, Z * XH, by).astype(f32)
    return result, back


def on_device(normed, out_grad, w_qkv):
    frames_dev, patches, width = normed.shape
    half = out_grad.shape[2]
    cols = width // MP
    count = patches // F
    n = 3 * half
    where = jnp.stack([lax.axis_index(a) for a in ("z", "y", "c", "mp")]).astype(jnp.int32)
    m = lax.axis_index("mp")
    part = lax.dynamic_slice_in_dim(normed, m * cols, cols, 2)
    tokens = jnp.concatenate([part, out_grad], axis=2).reshape(F, count, cols + half)

    pair = over_xh_and_pair(w_qkv.reshape(w_qkv.shape[0], n))
    tokens = lax.all_to_all(tokens, FR, 0, 0, tiled=True)
    two, four, six = (across(pair, "z", Z, 2 * i) for i in range(1, Z // 2))
    low, high = jnp.concatenate([pair, two], 0), jnp.concatenate([four, six], 0)
    part = tokens[:, :, :cols]
    low, high, part = lax.optimization_barrier((low, high, part))
    others = lax.ppermute(part, "mp", PAIR)
    mine = over_y(low, high)
    others = others.reshape(F * count, cols)
    tokens = tokens.reshape(F * count, cols + half)
    mine[2], mine[7], tokens = lax.optimization_barrier((mine[2], mine[7], tokens))
    rest = {i: lax.ppermute(mine[i], "c", PAIR) for i in (0, 1, 2, 3, 6, 7)}
    mine, others, tokens = lax.optimization_barrier((mine, others, tokens))
    rest.update({i: lax.ppermute(mine[i], "c", PAIR) for i in (4, 5)})

    rest = [rest[i] for i in range(8)]
    give, keep, mine, rest = core(where, tokens, others, mine, rest)
    got = lax.ppermute(give, "mp", PAIR)

    def finish(got):
        return (keep.astype(f32) + got.astype(f32)).astype(bf16)

    def to_frames(x):
        return lax.all_to_all(x.reshape(F, count, cols), FR, 0, 0, tiled=True)

    weight_grad, back = reduce_weight(mine, rest, got, finish, to_frames)
    input_grad = back.reshape(frames_dev, patches, cols)
    weight_grad = weight_grad * (1.0 / F)
    return (input_grad, weight_grad.reshape(w_qkv.shape))


def solution(mesh):
    fine = Mesh(mesh.devices.reshape(Z, Y, XH, C, MP), ("z", "y", "xh", "c", "mp"))
    in_specs = (P(FR, None, None), P(FR, None, "mp"), P(FR, None, "mp"))
    out_specs = (P(FR, None, "mp"), P(FR, None, "mp"))
    return jax.shard_map(
        on_device, mesh=fine, in_specs=in_specs, out_specs=out_specs, check_vma=False
    )
```

```python
import jax
import jax.numpy as jnp
from jax import lax
from jax.experimental import pallas as pl
from jax.experimental.pallas import tpu as pltpu
from jax.sharding import Mesh, PartitionSpec as P

HEAD_DIM = 64
Z, Y, XH, C, MP = 8, 4, 2, 2, 2
F = 128
ROWS = 12
VMEM_LIMIT = 32 * 2**20
bf16, f32 = jnp.bfloat16, jnp.float32
NT = (((1,), (1,)), ((), ()))
TN = (((0,), (0,)), ((), ()))


def dot(a, b, dims):
    return lax.dot_general(a, b, dims, preferred_element_type=f32)


def core_kernel(where_ref, t_ref, o_ref, *refs):
    own_ref, other_ref = refs[:2]
    give_ref, keep_ref, mine_ref, rest_ref, w_ref, s_ref, d_ref, g_ref = refs[2:]
    z, y, c, m = (where_ref[i] for i in range(4))
    unit = XH * C * ROWS

    @pl.loop(0, Z)
    def _(t):
        for i in range(Y):
            a = own_ref[i, t].astype(f32)
            b = other_ref[i, t].astype(f32)
            first = jnp.where(c == 0, a, b)
            second = jnp.where(c == 0, b, a)
            rows = [first[:ROWS], second[:ROWS], first[ROWS:], second[ROWS:]]
            to = pl.ds(pl.multiple_of((lax.bitwise_xor(z, t) * Y + i) * unit, unit), unit)
            w_ref[to, :] = jnp.concatenate(rows, 0).astype(bf16)

    part_cols = o_ref.shape[1]
    rows, half = t_ref.shape[0], t_ref.shape[1] - part_cols
    count = rows // F
    scale = HEAD_DIM ** (-0.5)
    pairs = half // 128
    near = pl.ds(pl.multiple_of(m * part_cols, part_cols), part_cols)
    away = pl.ds(pl.multiple_of((1 - m) * part_cols, part_cols), part_cols)
    part = jnp.dot(t_ref[:, :part_cols], w_ref[near, :], preferred_element_type=f32)
    part += jnp.dot(o_ref[...], w_ref[away, :], preferred_element_type=f32)
    part = part.astype(bf16)
    for i in range(3 * pairs):
        s_ref[i] = part[:, i * 128 : (i + 1) * 128].astype(f32)
    for pair in range(pairs):
        at = part_cols + pair * 128
        s_ref[3 * pairs + pair] = t_ref[:, at : at + 128].astype(f32)
    low = lax.broadcasted_iota(jnp.int32, (F, 128), 1) < HEAD_DIM
    zero = jnp.zeros((F, 128), f32)

    def split(v):
        return jnp.concatenate([jnp.where(low, v, zero), jnp.where(low, zero, v)], 0).astype(bf16)

    @pl.loop(0, count)
    def _(p):
        at = pl.ds(p, F, stride=count)
        for pair in range(pairs):
            q, k, v, u = (s_ref[j * pairs + pair, at, :] for j in range(4))
            q2 = split(q * scale)
            u2 = split(u)
            k = k.astype(bf16)
            v = v.astype(bf16)
            weights = jnp.exp(dot(q2, k, NT))
            weights = weights / jnp.sum(weights, axis=-1, keepdims=True)
            dprobs = dot(u2, v, NT)
            center = jnp.sum(weights * dprobs, axis=-1, keepdims=True)
            dscores = (weights * (dprobs - center)).astype(bf16)
            dv = dot(weights.astype(bf16), u2, TN)
            dk = dot(dscores, q2, TN)
            both = jnp.dot(dscores, k, preferred_element_type=f32) * scale
            dq = jnp.where(low, both[:F], both[F:])
            for j, part in enumerate((dq, dk, dv)):
                d_ref[j * pairs + pair, at, :] = part
    g = jnp.concatenate([d_ref[i] for i in range(3 * pairs)], 1).astype(bf16)
    g_ref[...] = g
    give_ref[...] = dot(g, w_ref[away, :], NT).astype(bf16)
    keep_ref[...] = dot(g, w_ref[near, :], NT).astype(bf16)
    step = 384
    for ref, of in ((t_ref, m), (o_ref, 1 - m)):
        for i in range(part_cols // step):
            total = dot(ref[:, i * step : (i + 1) * step], g_ref[...], TN)
            for b in range(step // unit):
                quarters = [total[b * unit + r * ROWS :][:ROWS] for r in range(4)]
                first = jnp.concatenate([quarters[0], quarters[2]], 0)
                second = jnp.concatenate([quarters[1], quarters[3]], 0)
                by = lax.rem(b % Y + Y - y, Y)
                at = i * (step // unit // Y) + b // Y
                t = lax.bitwise_xor(of * (Z // MP) + at, z)
                mine_ref[by, t] = jnp.where(c == 0, first, second).astype(bf16)
                rest_ref[by, t] = jnp.where(c == 0, second, first).astype(bf16)


def core(where, tokens, others, own, other):
    rows, part_cols = others.shape
    half = tokens.shape[1] - part_cols
    width, n = MP * part_cols, 3 * half
    vm = pl.BlockSpec(memory_space=pltpu.VMEM)
    return pl.pallas_call(
        core_kernel,
        out_shape=(
            jax.ShapeDtypeStruct((rows, part_cols), bf16),
            jax.ShapeDtypeStruct((rows, part_cols), bf16),
            jax.ShapeDtypeStruct((Y, Z, XH * ROWS, n), bf16),
            jax.ShapeDtypeStruct((Y, Z, XH * ROWS, n), bf16),
        ),
        in_specs=[pl.BlockSpec(memory_space=pltpu.SMEM)] + [vm] * 4,
        out_specs=(vm,) * 4,
        scratch_shapes=[
            pltpu.VMEM((width, n), bf16),
            pltpu.VMEM((4 * half // 128, rows, 128), f32),
            pltpu.VMEM((3 * half // 128, rows, 128), f32),
            pltpu.VMEM((rows, n), bf16),
        ],
        compiler_params=pltpu.CompilerParams(vmem_limit_bytes=VMEM_LIMIT),
        cost_estimate=pl.CostEstimate(
            flops=6 * rows * width * n, bytes_accessed=8 * 2**20, transcendentals=0
        ),
        name="attention_core",
    )(where, tokens, others, own, other)


def combine_kernel(mine_ref, other_ref, *refs):
    own_ref, after_ref, before_ref, far_low, far_high, after_high, before_low = refs
    h = Z // 2

    def added(by, t):
        return mine_ref[by, t].astype(f32) + other_ref[by, t].astype(f32)

    @pl.loop(0, h)
    def _(t):
        far_low[t] = added(2, t).astype(bf16)
        far_high[t] = added(2, t + h).astype(bf16)
        own_ref[t] = added(0, t)
        own_ref[t + h] = added(0, t + h)
        after_ref[t] = added(1, t)
        after_high[t] = added(1, t + h).astype(bf16)
        before_low[t] = added(3, t).astype(bf16)
        before_ref[t] = added(3, t + h)


def combine(mine, other):
    vm = pl.BlockSpec(memory_space=pltpu.VMEM)
    block = mine.shape[2:]
    h = Z // 2
    return pl.pallas_call(
        combine_kernel,
        out_shape=[jax.ShapeDtypeStruct((n,) + block, f32) for n in (Z, h, h)]
        + [jax.ShapeDtypeStruct((h,) + block, bf16)] * 4,
        in_specs=[vm, vm],
        out_specs=[vm] * 7,
        compiler_params=pltpu.CompilerParams(vmem_limit_bytes=VMEM_LIMIT),
        cost_estimate=pl.CostEstimate(flops=0, bytes_accessed=2**20, transcendentals=0),
        name="combine_cores",
    )(mine, other)


FR = ("z", "y", "xh", "c")
PAIR = [(0, 1), (1, 0)]


def shift(x, axis, size, by):
    return lax.ppermute(x, axis, [(i, (i + by) % size) for i in range(size)])


def across(x, axis, size, by):
    return lax.ppermute(x, axis, [(i, i ^ by) for i in range(size)])


ZX = ("z", "xh")


def over_z(w):
    even = lax.axis_index("xh") == 0
    own = jnp.stack([w] + [across(w, "z", Z, 2 * i) for i in range(1, Z // 2)], 0)
    a, b, d = (across(own, ZX, Z * XH, by) for by in (1, 2, 3))
    first = jnp.concatenate([jnp.where(even, own, a), jnp.where(even, a, own)], 1)
    second = jnp.concatenate([jnp.where(even, b, d), jnp.where(even, d, b)], 1)
    return jnp.stack([first, second], 1).reshape(Z, XH * ROWS, w.shape[1])


def reduce_weight(mine, rest, got, finish, late):
    even = lax.axis_index("xh") == 0
    other = lax.ppermute(rest, "c", PAIR)
    h = Z // 2
    own, after, before, far_low, far_high, after_high, before_low = combine(mine, other)
    up_far = shift(far_low, "y", Y, 1)
    down_far = shift(far_high, "y", Y, Y - 1)
    up_high = shift(after_high, "y", Y, 1)
    down_low = shift(before_low, "y", Y, Y - 1)
    up_far, down_far, got = lax.optimization_barrier((up_far, down_far, got))
    summed = finish(got)
    up_low = (after + up_far.astype(f32)).astype(bf16)
    down_high = (before + down_far.astype(f32)).astype(bf16)
    up_low, down_high, summed = lax.optimization_barrier((up_low, down_high, summed))
    up_low = shift(up_low, "y", Y, 1)
    down_high = shift(down_high, "y", Y, Y - 1)
    low = own[:h] + up_low.astype(f32) + down_low.astype(f32)
    high = own[h:] + up_high.astype(f32) + down_high.astype(f32)
    blocks = jnp.concatenate([low, high], 0)
    kept = jnp.where(even, blocks[:, :ROWS], blocks[:, ROWS:])
    sent = jnp.where(even, blocks[:, ROWS:], blocks[:, :ROWS])
    total = kept[0::2]
    for by, x in ((2, kept[1::2]), (1, sent[0::2]), (3, sent[1::2])):
        total = total + across(x.astype(bf16), ZX, Z * XH, by).astype(f32)
    back = late(summed)
    total, back = lax.optimization_barrier((total, back))
    result = total[0]
    for i in range(1, h):
        result = result + across(total[i].astype(bf16), "z", Z, 2 * i).astype(f32)
    return result, back


def on_device(normed, out_grad, w_qkv):
    frames_dev, patches, width = normed.shape
    half = out_grad.shape[2]
    cols = width // MP
    count = patches // F
    n = 3 * half
    where = jnp.stack([lax.axis_index(a) for a in ("z", "y", "c", "mp")]).astype(jnp.int32)
    m = lax.axis_index("mp")
    part = lax.dynamic_slice_in_dim(normed, m * cols, cols, 2)
    tokens = jnp.concatenate([part, out_grad], axis=2).reshape(F, count, cols + half)

    own = over_z(w_qkv.reshape(w_qkv.shape[0], n))
    tokens = lax.all_to_all(tokens, FR, 0, 0, tiled=True)
    part = tokens[:, :, :cols]
    own, part = lax.optimization_barrier((own, part))
    others = lax.ppermute(part, "mp", PAIR)
    own = lax.all_to_all(jnp.broadcast_to(own[None], (Y,) + own.shape), "y", 0, 0, tiled=True)
    tokens = tokens.reshape(F * count, cols + half)
    own, tokens, others = lax.optimization_barrier((own, tokens, others))
    others = others.reshape(F * count, cols)
    other = lax.ppermute(own, "c", PAIR)
    give, keep, mine, rest = core(where, tokens, others, own, other)
    got = lax.ppermute(give, "mp", PAIR)

    def finish(got):
        return (keep.astype(f32) + got.astype(f32)).astype(bf16)

    def to_frames(x):
        return lax.all_to_all(x.reshape(F, count, cols), FR, 0, 0, tiled=True)

    weight_grad, back = reduce_weight(mine, rest, got, finish, to_frames)
    input_grad = back.reshape(frames_dev, patches, cols)
    weight_grad = weight_grad * (1.0 / F)
    return (input_grad, weight_grad.reshape(w_qkv.shape))


def solution(mesh):
    fine = Mesh(mesh.devices.reshape(Z, Y, XH, C, MP), ("z", "y", "xh", "c", "mp"))
    in_specs = (P(FR, None, None), P(FR, None, "mp"), P(FR, None, "mp"))
    out_specs = (P(FR, None, "mp"), P(FR, None, "mp"))
    return jax.shard_map(
        on_device, mesh=fine, in_specs=in_specs, out_specs=out_specs, check_vma=False
    )
```

```python
import jax
import jax.numpy as jnp
from jax import lax
from jax.experimental import pallas as pl
from jax.experimental.pallas import tpu as pltpu
from jax.sharding import Mesh, PartitionSpec as P

HEAD_DIM = 64
Z, Y, XH, C, MP = 8, 4, 2, 2, 2
F = 128
ROWS = 12
VMEM_LIMIT = 32 * 2**20
bf16, f32 = jnp.bfloat16, jnp.float32
NT = (((1,), (1,)), ((), ()))
TN = (((0,), (0,)), ((), ()))


def dot(a, b, dims):
    return lax.dot_general(a, b, dims, preferred_element_type=f32)


def core_kernel(where_ref, t_ref, *refs):
    parts, pieces = refs[:2], refs[2:18]
    give_ref, keep_ref, mine_ref, rest_ref, w_ref, s_ref, d_ref, g_ref, o_ref = refs[18:]
    for i, part in enumerate(parts):
        o_ref[i * part.shape[0] : (i + 1) * part.shape[0]] = part[...]
    z, y, c, m = (where_ref[i] for i in range(4))
    unit = XH * C * ROWS

    @pl.loop(0, Z // 2)
    def _(t):
        for i in range(8):
            by, high = i // 2, i % 2
            a = pieces[i][t].astype(f32)
            b = pieces[i + 8][t].astype(f32)
            first = jnp.where(c == 0, a, b)
            second = jnp.where(c == 0, b, a)
            rows = [first[:ROWS], second[:ROWS], first[ROWS:], second[ROWS:]]
            to = lax.bitwise_xor(z, t + high * (Z // 2)) * Y + lax.rem(by + y, Y)
            to = pl.ds(pl.multiple_of(to * unit, unit), unit)
            w_ref[to, :] = jnp.concatenate(rows, 0).astype(bf16)

    part_cols = o_ref.shape[1]
    rows, half = t_ref.shape[0], t_ref.shape[1] - part_cols
    count = rows // F
    scale = HEAD_DIM ** (-0.5)
    pairs = half // 128
    near = pl.ds(pl.multiple_of(m * part_cols, part_cols), part_cols)
    away = pl.ds(pl.multiple_of((1 - m) * part_cols, part_cols), part_cols)
    part = jnp.dot(t_ref[:, :part_cols], w_ref[near, :], preferred_element_type=f32)
    part += jnp.dot(o_ref[...], w_ref[away, :], preferred_element_type=f32)
    part = part.astype(bf16)
    for i in range(3 * pairs):
        s_ref[i] = part[:, i * 128 : (i + 1) * 128].astype(f32)
    for pair in range(pairs):
        at = part_cols + pair * 128
        s_ref[3 * pairs + pair] = t_ref[:, at : at + 128].astype(f32)
    low = lax.broadcasted_iota(jnp.int32, (F, 128), 1) < HEAD_DIM
    zero = jnp.zeros((F, 128), f32)

    def split(v):
        return jnp.concatenate([jnp.where(low, v, zero), jnp.where(low, zero, v)], 0).astype(bf16)

    @pl.loop(0, count)
    def _(p):
        at = pl.ds(p, F, stride=count)
        for pair in range(pairs):
            q, k, v, u = (s_ref[j * pairs + pair, at, :] for j in range(4))
            q2 = split(q * scale)
            u2 = split(u)
            k = k.astype(bf16)
            v = v.astype(bf16)
            weights = jnp.exp(dot(q2, k, NT))
            weights = weights / jnp.sum(weights, axis=-1, keepdims=True)
            dprobs = dot(u2, v, NT)
            center = jnp.sum(weights * dprobs, axis=-1, keepdims=True)
            dscores = (weights * (dprobs - center)).astype(bf16)
            dv = dot(weights.astype(bf16), u2, TN)
            dk = dot(dscores, q2, TN)
            both = jnp.dot(dscores, k, preferred_element_type=f32) * scale
            dq = jnp.where(low, both[:F], both[F:])
            for j, part in enumerate((dq, dk, dv)):
                d_ref[j * pairs + pair, at, :] = part
    g = jnp.concatenate([d_ref[i] for i in range(3 * pairs)], 1).astype(bf16)
    g_ref[...] = g
    give_ref[...] = dot(g, w_ref[away, :], NT).astype(bf16)
    keep_ref[...] = dot(g, w_ref[near, :], NT).astype(bf16)
    step = 384
    for ref, of in ((t_ref, m), (o_ref, 1 - m)):

        @pl.loop(0, part_cols // step)
        def _(i, ref=ref, of=of):
            total = dot(ref[:, pl.ds(pl.multiple_of(i * step, step), step)], g_ref[...], TN)
            for b in range(step // unit):
                quarters = [total[b * unit + r * ROWS :][:ROWS] for r in range(4)]
                first = jnp.concatenate([quarters[0], quarters[2]], 0)
                second = jnp.concatenate([quarters[1], quarters[3]], 0)
                by = lax.rem(b % Y + Y - y, Y)
                at = i * (step // unit // Y) + b // Y
                t = lax.bitwise_xor(of * (Z // MP) + at, z)
                mine_ref[by, t] = jnp.where(c == 0, first, second).astype(bf16)
                rest_ref[by, t] = jnp.where(c == 0, second, first).astype(bf16)


def core(where, tokens, others, own, other):
    rows, part_cols = tokens.shape[0], others[0].shape[1]
    half = tokens.shape[1] - part_cols
    width, n = MP * part_cols, 3 * half
    vm = pl.BlockSpec(memory_space=pltpu.VMEM)
    return pl.pallas_call(
        core_kernel,
        out_shape=(
            jax.ShapeDtypeStruct((rows, part_cols), bf16),
            jax.ShapeDtypeStruct((rows, part_cols), bf16),
            jax.ShapeDtypeStruct((Y, Z, XH * ROWS, n), bf16),
            jax.ShapeDtypeStruct((Y, Z, XH * ROWS, n), bf16),
        ),
        in_specs=[pl.BlockSpec(memory_space=pltpu.SMEM)] + [vm] * 19,
        out_specs=(vm,) * 4,
        scratch_shapes=[
            pltpu.VMEM((width, n), bf16),
            pltpu.VMEM((4 * half // 128, rows, 128), f32),
            pltpu.VMEM((3 * half // 128, rows, 128), f32),
            pltpu.VMEM((rows, n), bf16),
            pltpu.VMEM((rows, part_cols), bf16),
        ],
        compiler_params=pltpu.CompilerParams(vmem_limit_bytes=VMEM_LIMIT),
        cost_estimate=pl.CostEstimate(
            flops=6 * rows * width * n, bytes_accessed=8 * 2**20, transcendentals=0
        ),
        name="attention_core",
    )(where, tokens, *others, *own, *other)


def combine_kernel(mine_ref, other_ref, *refs):
    own_ref, after_ref, before_ref, far_low, far_high, after_high, before_low = refs
    h = Z // 2

    def added(by, t):
        return mine_ref[by, t].astype(f32) + other_ref[by, t].astype(f32)

    @pl.loop(0, h)
    def _(t):
        far_low[t] = added(2, t).astype(bf16)
        far_high[t] = added(2, t + h).astype(bf16)
        own_ref[t] = added(0, t)
        own_ref[t + h] = added(0, t + h)
        after_ref[t] = added(1, t)
        after_high[t] = added(1, t + h).astype(bf16)
        before_low[t] = added(3, t).astype(bf16)
        before_ref[t] = added(3, t + h)


def combine(mine, other):
    vm = pl.BlockSpec(memory_space=pltpu.VMEM)
    block = mine.shape[2:]
    h = Z // 2
    return pl.pallas_call(
        combine_kernel,
        out_shape=[jax.ShapeDtypeStruct((n,) + block, f32) for n in (Z, h, h)]
        + [jax.ShapeDtypeStruct((h,) + block, bf16)] * 4,
        in_specs=[vm, vm],
        out_specs=[vm] * 7,
        compiler_params=pltpu.CompilerParams(vmem_limit_bytes=VMEM_LIMIT),
        cost_estimate=pl.CostEstimate(flops=0, bytes_accessed=2**20, transcendentals=0),
        name="combine_cores",
    )(mine, other)


FR = ("z", "y", "xh", "c")
PAIR = [(0, 1), (1, 0)]


def shift(x, axis, size, by):
    return lax.ppermute(x, axis, [(i, (i + by) % size) for i in range(size)])


def across(x, axis, size, by):
    return lax.ppermute(x, axis, [(i, i ^ by) for i in range(size)])


ZX = ("z", "xh")


def over_z(w):
    even = lax.axis_index("xh") == 0
    own = jnp.stack([w] + [across(w, "z", Z, 2 * i) for i in range(1, Z // 2)], 0)
    a, b, d = (across(own, ZX, Z * XH, by) for by in (1, 2, 3))

    def part(at):
        first = jnp.concatenate([jnp.where(even, own, a)[at], jnp.where(even, a, own)[at]], 1)
        second = jnp.concatenate([jnp.where(even, b, d)[at], jnp.where(even, d, b)[at]], 1)
        return jnp.stack([first, second], 1).reshape(Z // 2, XH * ROWS, w.shape[1])

    return part(slice(0, 2)), part(slice(2, 4))


def reduce_weight(mine, rest, got, finish, late):
    even = lax.axis_index("xh") == 0
    other = lax.ppermute(rest, "c", PAIR)
    h = Z // 2
    own, after, before, far_low, far_high, after_high, before_low = combine(mine, other)
    up_far = shift(far_low, "y", Y, 1)
    down_far = shift(far_high, "y", Y, Y - 1)
    up_high = shift(after_high, "y", Y, 1)
    down_low = shift(before_low, "y", Y, Y - 1)
    up_far, down_far, got = lax.optimization_barrier((up_far, down_far, got))
    summed = finish(got)
    up_low = (after + up_far.astype(f32)).astype(bf16)
    down_high = (before + down_far.astype(f32)).astype(bf16)
    up_low, down_high, summed = lax.optimization_barrier((up_low, down_high, summed))
    up_low = shift(up_low, "y", Y, 1)
    down_high = shift(down_high, "y", Y, Y - 1)
    low = own[:h] + up_low.astype(f32) + down_low.astype(f32)
    high = own[h:] + up_high.astype(f32) + down_high.astype(f32)
    blocks = jnp.concatenate([low, high], 0)
    kept = jnp.where(even, blocks[:, :ROWS], blocks[:, ROWS:])
    sent = jnp.where(even, blocks[:, ROWS:], blocks[:, :ROWS])
    total = kept[0::2]
    for by, x in ((2, kept[1::2]), (1, sent[0::2]), (3, sent[1::2])):
        total = total + across(x.astype(bf16), ZX, Z * XH, by).astype(f32)
    back = late(summed)
    total, back = lax.optimization_barrier((total, back))
    result = total[0]
    for i in range(1, h):
        result = result + across(total[i].astype(bf16), "z", Z, 2 * i).astype(f32)
    return result, back


def on_device(normed, out_grad, w_qkv):
    frames_dev, patches, width = normed.shape
    half = out_grad.shape[2]
    cols = width // MP
    count = patches // F
    n = 3 * half
    where = jnp.stack([lax.axis_index(a) for a in ("z", "y", "c", "mp")]).astype(jnp.int32)
    m = lax.axis_index("mp")
    part = lax.dynamic_slice_in_dim(normed, m * cols, cols, 2)
    tokens = jnp.concatenate([part, out_grad], axis=2).reshape(F, count, cols + half)

    low, high = over_z(w_qkv.reshape(w_qkv.shape[0], n))
    tokens = lax.all_to_all(tokens, FR, 0, 0, tiled=True)
    first, second = tokens[: F // 2, :, :cols], tokens[F // 2 :, :, :cols]
    first = lax.ppermute(first, "mp", PAIR)
    low, high, first, second = lax.optimization_barrier((low, high, first, second))
    second = lax.ppermute(second, "mp", PAIR)
    before_low = shift(low, "y", Y, 1)
    after_high = shift(high, "y", Y, Y - 1)
    before_high = shift(high, "y", Y, 1)
    after_low = shift(low, "y", Y, Y - 1)
    tokens = tokens.reshape(F * count, cols + half)
    before_low, after_high, tokens = lax.optimization_barrier((before_low, after_high, tokens))
    far_low = shift(before_low, "y", Y, 1)
    far_high = shift(after_high, "y", Y, Y - 1)
    far_low, far_high, second = lax.optimization_barrier((far_low, far_high, second))
    others = [x.reshape(F // 2 * count, cols) for x in (first, second)]
    own = [low, high, after_low, after_high, far_low, far_high, before_low, before_high]
    other = [lax.ppermute(x, "c", PAIR) for x in own]
    give, keep, mine, rest = core(where, tokens, others, own, other)
    got = lax.ppermute(give, "mp", PAIR)

    def finish(got):
        return (keep.astype(f32) + got.astype(f32)).astype(bf16)

    def to_frames(x):
        return lax.all_to_all(x.reshape(F, count, cols), FR, 0, 0, tiled=True)

    weight_grad, back = reduce_weight(mine, rest, got, finish, to_frames)
    input_grad = back.reshape(frames_dev, patches, cols)
    weight_grad = weight_grad * (1.0 / F)
    return (input_grad, weight_grad.reshape(w_qkv.shape))


def solution(mesh):
    fine = Mesh(mesh.devices.reshape(Z, Y, XH, C, MP), ("z", "y", "xh", "c", "mp"))
    in_specs = (P(FR, None, None), P(FR, None, "mp"), P(FR, None, "mp"))
    out_specs = (P(FR, None, "mp"), P(FR, None, "mp"))
    return jax.shard_map(
        on_device, mesh=fine, in_specs=in_specs, out_specs=out_specs, check_vma=False
    )
```

```python
import jax
import jax.numpy as jnp
from jax import lax
from jax.experimental import pallas as pl
from jax.experimental.pallas import tpu as pltpu
from jax.sharding import Mesh, PartitionSpec as P

HEAD_DIM = 64
Z, Y, XH, C, MP = 8, 4, 2, 2, 2
F = 128
ROWS = 12
VMEM_LIMIT = 32 * 2**20
bf16, f32 = jnp.bfloat16, jnp.float32
NT = (((1,), (1,)), ((), ()))
TN = (((0,), (0,)), ((), ()))


def dot(a, b, dims):
    return lax.dot_general(a, b, dims, preferred_element_type=f32)


def core_kernel(where_ref, t_ref, o_ref, *refs):
    pieces = refs[:16]
    give_ref, keep_ref, mine_ref, rest_ref, w_ref, s_ref, d_ref, g_ref = refs[16:]
    z, y, c, m = (where_ref[i] for i in range(4))
    unit = XH * C * ROWS

    @pl.loop(0, Z // 2)
    def _(t):
        for i in range(8):
            by, high = i // 2, i % 2
            a = pieces[i][t].astype(f32)
            b = pieces[i + 8][t].astype(f32)
            first = jnp.where(c == 0, a, b)
            second = jnp.where(c == 0, b, a)
            rows = [first[:ROWS], second[:ROWS], first[ROWS:], second[ROWS:]]
            to = lax.bitwise_xor(z, t + high * (Z // 2)) * Y + lax.rem(by + y, Y)
            to = pl.ds(pl.multiple_of(to * unit, unit), unit)
            w_ref[to, :] = jnp.concatenate(rows, 0).astype(bf16)

    part_cols = o_ref.shape[1]
    rows, half = t_ref.shape[0], t_ref.shape[1] - part_cols
    count = rows // F
    scale = HEAD_DIM ** (-0.5)
    pairs = half // 128
    near = pl.ds(pl.multiple_of(m * part_cols, part_cols), part_cols)
    away = pl.ds(pl.multiple_of((1 - m) * part_cols, part_cols), part_cols)
    part = jnp.dot(t_ref[:, :part_cols], w_ref[near, :], preferred_element_type=f32)
    part += jnp.dot(o_ref[...], w_ref[away, :], preferred_element_type=f32)
    part = part.astype(bf16)
    for i in range(3 * pairs):
        s_ref[i] = part[:, i * 128 : (i + 1) * 128].astype(f32)
    for pair in range(pairs):
        at = part_cols + pair * 128
        s_ref[3 * pairs + pair] = t_ref[:, at : at + 128].astype(f32)
    low = lax.broadcasted_iota(jnp.int32, (F, 128), 1) < HEAD_DIM
    zero = jnp.zeros((F, 128), f32)

    def split(v):
        return jnp.concatenate([jnp.where(low, v, zero), jnp.where(low, zero, v)], 0).astype(bf16)

    @pl.loop(0, count)
    def _(p):
        at = pl.ds(p, F, stride=count)
        for pair in range(pairs):
            q, k, v, u = (s_ref[j * pairs + pair, at, :] for j in range(4))
            q2 = split(q * scale)
            u2 = split(u)
            k = k.astype(bf16)
            v = v.astype(bf16)
            weights = jnp.exp(dot(q2, k, NT))
            weights = weights / jnp.sum(weights, axis=-1, keepdims=True)
            dprobs = dot(u2, v, NT)
            center = jnp.sum(weights * dprobs, axis=-1, keepdims=True)
            dscores = (weights * (dprobs - center)).astype(bf16)
            dv = dot(weights.astype(bf16), u2, TN)
            dk = dot(dscores, q2, TN)
            both = jnp.dot(dscores, k, preferred_element_type=f32) * scale
            dq = jnp.where(low, both[:F], both[F:])
            for j, part in enumerate((dq, dk, dv)):
                d_ref[j * pairs + pair, at, :] = part
    g = jnp.concatenate([d_ref[i] for i in range(3 * pairs)], 1).astype(bf16)
    g_ref[...] = g
    give_ref[...] = dot(g, w_ref[away, :], NT).astype(bf16)
    keep_ref[...] = dot(g, w_ref[near, :], NT).astype(bf16)
    step = 384
    for ref, of in ((t_ref, m), (o_ref, 1 - m)):

        @pl.loop(0, part_cols // step)
        def _(i, ref=ref, of=of):
            total = dot(ref[:, pl.ds(pl.multiple_of(i * step, step), step)], g_ref[...], TN)
            for b in range(step // unit):
                quarters = [total[b * unit + r * ROWS :][:ROWS] for r in range(4)]
                first = jnp.concatenate([quarters[0], quarters[2]], 0)
                second = jnp.concatenate([quarters[1], quarters[3]], 0)
                by = lax.rem(b % Y + Y - y, Y)
                at = i * (step // unit // Y) + b // Y
                t = lax.bitwise_xor(of * (Z // MP) + at, z)
                mine_ref[by, t] = jnp.where(c == 0, first, second).astype(bf16)
                rest_ref[by, t] = jnp.where(c == 0, second, first).astype(bf16)


def core(where, tokens, others, mine, rest):
    rows, part_cols = others.shape
    half = tokens.shape[1] - part_cols
    width, n = MP * part_cols, 3 * half
    vm = pl.BlockSpec(memory_space=pltpu.VMEM)
    return pl.pallas_call(
        core_kernel,
        out_shape=(
            jax.ShapeDtypeStruct((rows, part_cols), bf16),
            jax.ShapeDtypeStruct((rows, part_cols), bf16),
            jax.ShapeDtypeStruct((Y, Z, XH * ROWS, n), bf16),
            jax.ShapeDtypeStruct((Y, Z, XH * ROWS, n), bf16),
        ),
        in_specs=[pl.BlockSpec(memory_space=pltpu.SMEM)] + [vm] * 18,
        out_specs=(vm,) * 4,
        scratch_shapes=[
            pltpu.VMEM((width, n), bf16),
            pltpu.VMEM((4 * half // 128, rows, 128), f32),
            pltpu.VMEM((3 * half // 128, rows, 128), f32),
            pltpu.VMEM((rows, n), bf16),
        ],
        compiler_params=pltpu.CompilerParams(vmem_limit_bytes=VMEM_LIMIT),
        cost_estimate=pl.CostEstimate(
            flops=6 * rows * width * n, bytes_accessed=8 * 2**20, transcendentals=0
        ),
        name="attention_core",
    )(where, tokens, others, *mine, *rest)


def combine_kernel(mine_ref, other_ref, *refs):
    own_ref, after_ref, before_ref, far_low, far_high, after_high, before_low = refs
    h = Z // 2

    def added(by, t):
        return mine_ref[by, t].astype(f32) + other_ref[by, t].astype(f32)

    @pl.loop(0, h)
    def _(t):
        far_low[t] = added(2, t).astype(bf16)
        far_high[t] = added(2, t + h).astype(bf16)
        own_ref[t] = added(0, t)
        own_ref[t + h] = added(0, t + h)
        after_ref[t] = added(1, t)
        after_high[t] = added(1, t + h).astype(bf16)
        before_low[t] = added(3, t).astype(bf16)
        before_ref[t] = added(3, t + h)


def combine(mine, other):
    vm = pl.BlockSpec(memory_space=pltpu.VMEM)
    block = mine.shape[2:]
    h = Z // 2
    return pl.pallas_call(
        combine_kernel,
        out_shape=[jax.ShapeDtypeStruct((n,) + block, f32) for n in (Z, h, h)]
        + [jax.ShapeDtypeStruct((h,) + block, bf16)] * 4,
        in_specs=[vm, vm],
        out_specs=[vm] * 7,
        compiler_params=pltpu.CompilerParams(vmem_limit_bytes=VMEM_LIMIT),
        cost_estimate=pl.CostEstimate(flops=0, bytes_accessed=2**20, transcendentals=0),
        name="combine_cores",
    )(mine, other)


def add_kernel(a_ref, b_ref, o_ref):
    total = a_ref[...].astype(f32) + b_ref[...].astype(f32)
    o_ref[...] = total.reshape(o_ref.shape).astype(bf16)


def add_parts(a, b):
    rows, cols = a.shape
    vm = pl.BlockSpec(memory_space=pltpu.VMEM)
    return pl.pallas_call(
        add_kernel,
        out_shape=jax.ShapeDtypeStruct((F, rows // F, cols), bf16),
        in_specs=[vm, vm],
        out_specs=vm,
        compiler_params=pltpu.CompilerParams(vmem_limit_bytes=16 * 2**20),
        cost_estimate=pl.CostEstimate(flops=0, bytes_accessed=2**20, transcendentals=0),
        name="add_parts",
    )(a, b)


FR = ("z", "y", "xh", "c")
PAIR = [(0, 1), (1, 0)]


def shift(x, axis, size, by):
    return lax.ppermute(x, axis, [(i, (i + by) % size) for i in range(size)])


def across(x, axis, size, by):
    return lax.ppermute(x, axis, [(i, i ^ by) for i in range(size)])


ZX = ("z", "xh")


def far_z(w):
    return jnp.stack([w] + [across(w, "z", Z, 2 * i) for i in range(1, Z // 2)], 0)


def near_zx(own):
    even = lax.axis_index("xh") == 0
    a, b, d = (across(own, ZX, Z * XH, by) for by in (1, 2, 3))

    def part(at):
        first = jnp.concatenate([jnp.where(even, own, a)[at], jnp.where(even, a, own)[at]], 1)
        second = jnp.concatenate([jnp.where(even, b, d)[at], jnp.where(even, d, b)[at]], 1)
        return jnp.stack([first, second], 1).reshape(Z // 2, XH * ROWS, own.shape[2])

    return part(slice(0, 2)), part(slice(2, 4))


def reduce_weight(mine, rest, got, finish, late):
    even = lax.axis_index("xh") == 0
    other = lax.ppermute(rest, "c", PAIR)
    h = Z // 2
    own, after, before, far_low, far_high, after_high, before_low = combine(mine, other)
    up_far = shift(far_low, "y", Y, 1)
    down_far = shift(far_high, "y", Y, Y - 1)
    up_high = shift(after_high, "y", Y, 1)
    down_low = shift(before_low, "y", Y, Y - 1)
    up_far, down_far, got = lax.optimization_barrier((up_far, down_far, got))
    summed = finish(got)
    up_low = (after + up_far.astype(f32)).astype(bf16)
    down_high = (before + down_far.astype(f32)).astype(bf16)
    up_low, down_high, summed = lax.optimization_barrier((up_low, down_high, summed))
    up_low = shift(up_low, "y", Y, 1)
    down_high = shift(down_high, "y", Y, Y - 1)
    low = own[:h] + up_low.astype(f32) + down_low.astype(f32)
    high = own[h:] + up_high.astype(f32) + down_high.astype(f32)
    blocks = jnp.concatenate([low, high], 0)
    kept = jnp.where(even, blocks[:, :ROWS], blocks[:, ROWS:])
    sent = jnp.where(even, blocks[:, ROWS:], blocks[:, :ROWS])
    total = kept[0::2]
    for by, x in ((2, kept[1::2]), (1, sent[0::2]), (3, sent[1::2])):
        total = total + across(x.astype(bf16), ZX, Z * XH, by).astype(f32)
    back = late(summed)
    total, back = lax.optimization_barrier((total, back))
    result = total[0]
    for i in range(1, h):
        result = result + across(total[i].astype(bf16), "z", Z, 2 * i).astype(f32)
    return result, back


def on_device(normed, out_grad, w_qkv):
    frames_dev, patches, width = normed.shape
    half = out_grad.shape[2]
    cols = width // MP
    count = patches // F
    n = 3 * half
    where = jnp.stack([lax.axis_index(a) for a in ("z", "y", "c", "mp")]).astype(jnp.int32)
    m = lax.axis_index("mp")
    part = lax.dynamic_slice_in_dim(normed, m * cols, cols, 2)
    tokens = jnp.concatenate([part, out_grad], axis=2).reshape(F, count, cols + half)

    rows = far_z(w_qkv.reshape(w_qkv.shape[0], n))
    tokens, rows = lax.optimization_barrier((tokens, rows))
    tokens = lax.all_to_all(tokens, FR, 0, 0, tiled=True)
    low, high = near_zx(rows)
    part = tokens[:, :, :cols]
    low, high, part = lax.optimization_barrier((low, high, part))
    others = lax.ppermute(part, "mp", PAIR)
    before_low = shift(low, "y", Y, 1)
    after_high = shift(high, "y", Y, Y - 1)
    before_high = shift(high, "y", Y, 1)
    after_low = shift(low, "y", Y, Y - 1)
    tokens = tokens.reshape(F * count, cols + half)
    before_low, after_high, tokens = lax.optimization_barrier((before_low, after_high, tokens))
    far_low = shift(before_low, "y", Y, 1)
    far_high = shift(after_high, "y", Y, Y - 1)
    mine = [low, high, after_low, after_high, far_low, far_high, before_low, before_high]
    others = others.reshape(F * count, cols)
    rest = {i: lax.ppermute(mine[i], "c", PAIR) for i in (0, 1, 2, 3, 6, 7)}
    mine, others = lax.optimization_barrier((mine, others))
    rest.update({i: lax.ppermute(mine[i], "c", PAIR) for i in (4, 5)})

    rest = [rest[i] for i in range(8)]
    give, keep, mine, rest = core(where, tokens, others, mine, rest)
    got = lax.ppermute(give, "mp", PAIR)

    def finish(got):
        return add_parts(keep, got)

    def to_frames(x):
        return lax.all_to_all(x, FR, 0, 0, tiled=True)

    weight_grad, back = reduce_weight(mine, rest, got, finish, to_frames)
    input_grad = back.reshape(frames_dev, patches, cols)
    weight_grad = weight_grad * (1.0 / F)
    return (input_grad, weight_grad.reshape(w_qkv.shape))


def solution(mesh):
    fine = Mesh(mesh.devices.reshape(Z, Y, XH, C, MP), ("z", "y", "xh", "c", "mp"))
    in_specs = (P(FR, None, None), P(FR, None, "mp"), P(FR, None, "mp"))
    out_specs = (P(FR, None, "mp"), P(FR, None, "mp"))
    return jax.shard_map(
        on_device, mesh=fine, in_specs=in_specs, out_specs=out_specs, check_vma=False
    )
```

```python
import jax
import jax.numpy as jnp
from jax import lax
from jax.experimental import pallas as pl
from jax.experimental.pallas import tpu as pltpu
from jax.sharding import Mesh, PartitionSpec as P

HEAD_DIM = 64
Z, Y, XH, C, MP = 8, 4, 2, 2, 2
F = 128
ROWS = 12
VMEM_LIMIT = 32 * 2**20
ROWS_COST = 20 * 10**9
bf16, f32 = jnp.bfloat16, jnp.float32
NT = (((1,), (1,)), ((), ()))
TN = (((0,), (0,)), ((), ()))


def dot(a, b, dims):
    return lax.dot_general(a, b, dims, preferred_element_type=f32)


def core_kernel(where_ref, t_ref, o_ref, *refs):
    pieces = refs[:16]
    give_ref, keep_ref, mine_ref, rest_ref, w_ref, s_ref, d_ref, g_ref = refs[16:]
    z, y, c, m = (where_ref[i] for i in range(4))
    unit = XH * C * ROWS

    @pl.loop(0, Z // 2)
    def _(t):
        for i in range(8):
            by, high = i // 2, i % 2
            a = pieces[i][t].astype(f32)
            b = pieces[i + 8][t].astype(f32)
            first = jnp.where(c == 0, a, b)
            second = jnp.where(c == 0, b, a)
            rows = [first[:ROWS], second[:ROWS], first[ROWS:], second[ROWS:]]
            to = lax.bitwise_xor(z, t + high * (Z // 2)) * Y + lax.rem(by + y, Y)
            to = pl.ds(pl.multiple_of(to * unit, unit), unit)
            w_ref[to, :] = jnp.concatenate(rows, 0).astype(bf16)

    part_cols = o_ref.shape[1]
    rows, half = t_ref.shape[0], t_ref.shape[1] - part_cols
    count = rows // F
    scale = HEAD_DIM ** (-0.5)
    pairs = half // 128
    near = pl.ds(pl.multiple_of(m * part_cols, part_cols), part_cols)
    away = pl.ds(pl.multiple_of((1 - m) * part_cols, part_cols), part_cols)
    part = jnp.dot(t_ref[:, :part_cols], w_ref[near, :], preferred_element_type=f32)
    part += jnp.dot(o_ref[...], w_ref[away, :], preferred_element_type=f32)
    part = part.astype(bf16)
    for i in range(3 * pairs):
        s_ref[i] = part[:, i * 128 : (i + 1) * 128].astype(f32)
    for pair in range(pairs):
        at = part_cols + pair * 128
        s_ref[3 * pairs + pair] = t_ref[:, at : at + 128].astype(f32)
    low = lax.broadcasted_iota(jnp.int32, (F, 128), 1) < HEAD_DIM
    zero = jnp.zeros((F, 128), f32)

    def split(v):
        return jnp.concatenate([jnp.where(low, v, zero), jnp.where(low, zero, v)], 0).astype(bf16)

    @pl.loop(0, count)
    def _(p):
        at = pl.ds(p, F, stride=count)
        for pair in range(pairs):
            q, k, v, u = (s_ref[j * pairs + pair, at, :] for j in range(4))
            q2 = split(q * scale)
            u2 = split(u)
            k = k.astype(bf16)
            v = v.astype(bf16)
            weights = jnp.exp(dot(q2, k, NT))
            weights = weights / jnp.sum(weights, axis=-1, keepdims=True)
            dprobs = dot(u2, v, NT)
            center = jnp.sum(weights * dprobs, axis=-1, keepdims=True)
            dscores = (weights * (dprobs - center)).astype(bf16)
            dv = dot(weights.astype(bf16), u2, TN)
            dk = dot(dscores, q2, TN)
            both = jnp.dot(dscores, k, preferred_element_type=f32) * scale
            dq = jnp.where(low, both[:F], both[F:])
            for j, part in enumerate((dq, dk, dv)):
                d_ref[j * pairs + pair, at, :] = part
    g = jnp.concatenate([d_ref[i] for i in range(3 * pairs)], 1).astype(bf16)
    g_ref[...] = g
    give_ref[...] = dot(g, w_ref[away, :], NT).astype(bf16)
    keep_ref[...] = dot(g, w_ref[near, :], NT).astype(bf16)
    step = 384
    for ref, of in ((t_ref, m), (o_ref, 1 - m)):

        @pl.loop(0, part_cols // step)
        def _(i, ref=ref, of=of):
            total = dot(ref[:, pl.ds(pl.multiple_of(i * step, step), step)], g_ref[...], TN)
            for b in range(step // unit):
                quarters = [total[b * unit + r * ROWS :][:ROWS] for r in range(4)]
                first = jnp.concatenate([quarters[0], quarters[2]], 0)
                second = jnp.concatenate([quarters[1], quarters[3]], 0)
                by = lax.rem(b % Y + Y - y, Y)
                at = i * (step // unit // Y) + b // Y
                t = lax.bitwise_xor(of * (Z // MP) + at, z)
                mine_ref[by, t] = jnp.where(c == 0, first, second).astype(bf16)
                rest_ref[by, t] = jnp.where(c == 0, second, first).astype(bf16)


def core(where, tokens, others, mine, rest):
    rows, part_cols = others.shape
    half = tokens.shape[1] - part_cols
    width, n = MP * part_cols, 3 * half
    vm = pl.BlockSpec(memory_space=pltpu.VMEM)
    return pl.pallas_call(
        core_kernel,
        out_shape=(
            jax.ShapeDtypeStruct((rows, part_cols), bf16),
            jax.ShapeDtypeStruct((rows, part_cols), bf16),
            jax.ShapeDtypeStruct((Y, Z, XH * ROWS, n), bf16),
            jax.ShapeDtypeStruct((Y, Z, XH * ROWS, n), bf16),
        ),
        in_specs=[pl.BlockSpec(memory_space=pltpu.SMEM)] + [vm] * 18,
        out_specs=(vm,) * 4,
        scratch_shapes=[
            pltpu.VMEM((width, n), bf16),
            pltpu.VMEM((4 * half // 128, rows, 128), f32),
            pltpu.VMEM((3 * half // 128, rows, 128), f32),
            pltpu.VMEM((rows, n), bf16),
        ],
        compiler_params=pltpu.CompilerParams(vmem_limit_bytes=VMEM_LIMIT),
        cost_estimate=pl.CostEstimate(
            flops=6 * rows * width * n, bytes_accessed=8 * 2**20, transcendentals=0
        ),
        name="attention_core",
    )(where, tokens, others, *mine, *rest)


def combine_kernel(mine_ref, other_ref, *refs):
    own_ref, after_ref, before_ref, far_low, far_high, after_high, before_low = refs
    h = Z // 2

    def added(by, t):
        return mine_ref[by, t].astype(f32) + other_ref[by, t].astype(f32)

    @pl.loop(0, h)
    def _(t):
        far_low[t] = added(2, t).astype(bf16)
        far_high[t] = added(2, t + h).astype(bf16)
        own_ref[t] = added(0, t)
        own_ref[t + h] = added(0, t + h)
        after_ref[t] = added(1, t)
        after_high[t] = added(1, t + h).astype(bf16)
        before_low[t] = added(3, t).astype(bf16)
        before_ref[t] = added(3, t + h)


def combine(mine, other):
    vm = pl.BlockSpec(memory_space=pltpu.VMEM)
    block = mine.shape[2:]
    h = Z // 2
    return pl.pallas_call(
        combine_kernel,
        out_shape=[jax.ShapeDtypeStruct((n,) + block, f32) for n in (Z, h, h)]
        + [jax.ShapeDtypeStruct((h,) + block, bf16)] * 4,
        in_specs=[vm, vm],
        out_specs=[vm] * 7,
        compiler_params=pltpu.CompilerParams(vmem_limit_bytes=VMEM_LIMIT),
        cost_estimate=pl.CostEstimate(flops=0, bytes_accessed=2**20, transcendentals=0),
        name="combine_cores",
    )(mine, other)


def add_kernel(a_ref, b_ref, o_ref):
    total = a_ref[...].astype(f32) + b_ref[...].astype(f32)
    o_ref[...] = total.reshape(o_ref.shape).astype(bf16)


def add_parts(a, b):
    rows, cols = a.shape
    vm = pl.BlockSpec(memory_space=pltpu.VMEM)
    return pl.pallas_call(
        add_kernel,
        out_shape=jax.ShapeDtypeStruct((F, rows // F, cols), bf16),
        in_specs=[vm, vm],
        out_specs=vm,
        compiler_params=pltpu.CompilerParams(vmem_limit_bytes=16 * 2**20),
        cost_estimate=pl.CostEstimate(flops=0, bytes_accessed=2**20, transcendentals=0),
        name="add_parts",
    )(a, b)


def rows_kernel(x_ref, all_ref, part_ref):
    rows = x_ref[...].astype(f32).reshape(all_ref.shape).astype(bf16)
    all_ref[...] = rows
    part_ref[...] = rows[:, : part_ref.shape[1]]


def to_rows(x, part_cols):
    rows, n = x.shape[0] * x.shape[1], x.shape[2]
    vm = pl.BlockSpec(memory_space=pltpu.VMEM)
    return pl.pallas_call(
        rows_kernel,
        out_shape=(
            jax.ShapeDtypeStruct((rows, n), bf16),
            jax.ShapeDtypeStruct((rows, part_cols), bf16),
        ),
        in_specs=[vm],
        out_specs=(vm, vm),
        compiler_params=pltpu.CompilerParams(vmem_limit_bytes=24 * 2**20),
        cost_estimate=pl.CostEstimate(flops=ROWS_COST, bytes_accessed=2**20, transcendentals=0),
        name="to_rows",
    )(x)


FR = ("z", "y", "xh", "c")
PAIR = [(0, 1), (1, 0)]


def shift(x, axis, size, by):
    return lax.ppermute(x, axis, [(i, (i + by) % size) for i in range(size)])


def across(x, axis, size, by):
    return lax.ppermute(x, axis, [(i, i ^ by) for i in range(size)])


ZX = ("z", "xh")


def far_z(w):
    return jnp.stack([w] + [across(w, "z", Z, 2 * i) for i in range(1, Z // 2)], 0)


def near_zx(own):
    even = lax.axis_index("xh") == 0
    a, b, d = (across(own, ZX, Z * XH, by) for by in (1, 2, 3))

    def part(at):
        first = jnp.concatenate([jnp.where(even, own, a)[at], jnp.where(even, a, own)[at]], 1)
        second = jnp.concatenate([jnp.where(even, b, d)[at], jnp.where(even, d, b)[at]], 1)
        return jnp.stack([first, second], 1).reshape(Z // 2, XH * ROWS, own.shape[2])

    return part(slice(0, 2)), part(slice(2, 4))


def reduce_weight(mine, rest, got, finish, late):
    even = lax.axis_index("xh") == 0
    other = lax.ppermute(rest, "c", PAIR)
    h = Z // 2
    own, after, before, far_low, far_high, after_high, before_low = combine(mine, other)
    up_far = shift(far_low, "y", Y, 1)
    down_far = shift(far_high, "y", Y, Y - 1)
    up_high = shift(after_high, "y", Y, 1)
    down_low = shift(before_low, "y", Y, Y - 1)
    up_far, down_far, got = lax.optimization_barrier((up_far, down_far, got))
    summed = finish(got)
    up_low = (after + up_far.astype(f32)).astype(bf16)
    down_high = (before + down_far.astype(f32)).astype(bf16)
    up_low, down_high, summed = lax.optimization_barrier((up_low, down_high, summed))
    up_low = shift(up_low, "y", Y, 1)
    down_high = shift(down_high, "y", Y, Y - 1)
    low = own[:h] + up_low.astype(f32) + down_low.astype(f32)
    high = own[h:] + up_high.astype(f32) + down_high.astype(f32)
    blocks = jnp.concatenate([low, high], 0)
    kept = jnp.where(even, blocks[:, :ROWS], blocks[:, ROWS:])
    sent = jnp.where(even, blocks[:, ROWS:], blocks[:, :ROWS])
    total = kept[0::2]
    for by, x in ((2, kept[1::2]), (1, sent[0::2]), (3, sent[1::2])):
        total = total + across(x.astype(bf16), ZX, Z * XH, by).astype(f32)
    back = late(summed)
    total, back = lax.optimization_barrier((total, back))
    result = total[0]
    for i in range(1, h):
        result = result + across(total[i].astype(bf16), "z", Z, 2 * i).astype(f32)
    return result, back


def on_device(normed, out_grad, w_qkv):
    frames_dev, patches, width = normed.shape
    half = out_grad.shape[2]
    cols = width // MP
    count = patches // F
    n = 3 * half
    where = jnp.stack([lax.axis_index(a) for a in ("z", "y", "c", "mp")]).astype(jnp.int32)
    m = lax.axis_index("mp")
    part = lax.dynamic_slice_in_dim(normed, m * cols, cols, 2)
    tokens = jnp.concatenate([part, out_grad], axis=2).reshape(F, count, cols + half)

    rows = far_z(w_qkv.reshape(w_qkv.shape[0], n))
    tokens, rows = lax.optimization_barrier((tokens, rows))
    tokens = lax.all_to_all(tokens, FR, 0, 0, tiled=True)
    low, high = near_zx(rows)
    tokens, part = to_rows(tokens, cols)
    low, high, part = lax.optimization_barrier((low, high, part))
    others = lax.ppermute(part, "mp", PAIR)
    before_low = shift(low, "y", Y, 1)
    after_high = shift(high, "y", Y, Y - 1)
    before_high = shift(high, "y", Y, 1)
    after_low = shift(low, "y", Y, Y - 1)
    far_low = shift(before_low, "y", Y, 1)
    far_high = shift(after_high, "y", Y, Y - 1)
    mine = [low, high, after_low, after_high, far_low, far_high, before_low, before_high]
    rest = {i: lax.ppermute(mine[i], "c", PAIR) for i in (0, 1, 2, 3, 6, 7)}
    mine, others = lax.optimization_barrier((mine, others))
    rest.update({i: lax.ppermute(mine[i], "c", PAIR) for i in (4, 5)})

    rest = [rest[i] for i in range(8)]
    give, keep, mine, rest = core(where, tokens, others, mine, rest)
    got = lax.ppermute(give, "mp", PAIR)

    def finish(got):
        return add_parts(keep, got)

    def to_frames(x):
        return lax.all_to_all(x, FR, 0, 0, tiled=True)

    weight_grad, back = reduce_weight(mine, rest, got, finish, to_frames)
    input_grad = back.reshape(frames_dev, patches, cols)
    weight_grad = weight_grad * (1.0 / F)
    return (input_grad, weight_grad.reshape(w_qkv.shape))


def solution(mesh):
    fine = Mesh(mesh.devices.reshape(Z, Y, XH, C, MP), ("z", "y", "xh", "c", "mp"))
    in_specs = (P(FR, None, None), P(FR, None, "mp"), P(FR, None, "mp"))
    out_specs = (P(FR, None, "mp"), P(FR, None, "mp"))
    return jax.shard_map(
        on_device, mesh=fine, in_specs=in_specs, out_specs=out_specs, check_vma=False
    )
```

```python
import jax
import jax.numpy as jnp
from jax import lax
from jax.experimental import pallas as pl
from jax.experimental.pallas import tpu as pltpu
from jax.sharding import Mesh, PartitionSpec as P

HEAD_DIM = 64
Z, Y, XH, C, MP = 8, 4, 2, 2, 2
F = 128
ROWS = 12
VMEM_LIMIT = 32 * 2**20
bf16, f32 = jnp.bfloat16, jnp.float32
NT = (((1,), (1,)), ((), ()))
TN = (((0,), (0,)), ((), ()))


def dot(a, b, dims):
    return lax.dot_general(a, b, dims, preferred_element_type=f32)


def core_kernel(where_ref, t_ref, o_ref, *refs):
    blocks = refs[:16]
    give_ref, keep_ref, mine_ref, rest_ref, w_ref, s_ref, d_ref, g_ref, pieces, sems = refs[16:]
    copies = [pltpu.make_async_copy(blocks[i], pieces.at[i], sems.at[i]) for i in range(16)]
    for i in range(8):
        copies[i].start()
        copies[i + 8].start()
    z, y, c, m = (where_ref[i] for i in range(4))
    unit = XH * C * ROWS

    for i in range(8):
        by, high = i // 2, i % 2
        copies[i].wait()
        copies[i + 8].wait()

        @pl.loop(0, Z // 2)
        def _(t, i=i, by=by, high=high):
            a = pieces[i, t].astype(f32)
            b = pieces[i + 8, t].astype(f32)
            first = jnp.where(c == 0, a, b)
            second = jnp.where(c == 0, b, a)
            rows = [first[:ROWS], second[:ROWS], first[ROWS:], second[ROWS:]]
            to = lax.bitwise_xor(z, t + high * (Z // 2)) * Y + lax.rem(by + y, Y)
            to = pl.ds(pl.multiple_of(to * unit, unit), unit)
            w_ref[to, :] = jnp.concatenate(rows, 0).astype(bf16)

    part_cols = o_ref.shape[1]
    rows, half = t_ref.shape[0], t_ref.shape[1] - part_cols
    count = rows // F
    scale = HEAD_DIM ** (-0.5)
    pairs = half // 128
    near = pl.ds(pl.multiple_of(m * part_cols, part_cols), part_cols)
    away = pl.ds(pl.multiple_of((1 - m) * part_cols, part_cols), part_cols)
    part = jnp.dot(t_ref[:, :part_cols], w_ref[near, :], preferred_element_type=f32)
    part += jnp.dot(o_ref[...], w_ref[away, :], preferred_element_type=f32)
    part = part.astype(bf16)
    for i in range(3 * pairs):
        s_ref[i] = part[:, i * 128 : (i + 1) * 128].astype(f32)
    for pair in range(pairs):
        at = part_cols + pair * 128
        s_ref[3 * pairs + pair] = t_ref[:, at : at + 128].astype(f32)
    low = lax.broadcasted_iota(jnp.int32, (F, 128), 1) < HEAD_DIM
    zero = jnp.zeros((F, 128), f32)

    def split(v):
        return jnp.concatenate([jnp.where(low, v, zero), jnp.where(low, zero, v)], 0).astype(bf16)

    @pl.loop(0, count)
    def _(p):
        at = pl.ds(p, F, stride=count)
        for pair in range(pairs):
            q, k, v, u = (s_ref[j * pairs + pair, at, :] for j in range(4))
            q2 = split(q * scale)
            u2 = split(u)
            k = k.astype(bf16)
            v = v.astype(bf16)
            weights = jnp.exp(dot(q2, k, NT))
            weights = weights / jnp.sum(weights, axis=-1, keepdims=True)
            dprobs = dot(u2, v, NT)
            center = jnp.sum(weights * dprobs, axis=-1, keepdims=True)
            dscores = (weights * (dprobs - center)).astype(bf16)
            dv = dot(weights.astype(bf16), u2, TN)
            dk = dot(dscores, q2, TN)
            both = jnp.dot(dscores, k, preferred_element_type=f32) * scale
            dq = jnp.where(low, both[:F], both[F:])
            for j, part in enumerate((dq, dk, dv)):
                d_ref[j * pairs + pair, at, :] = part
    g = jnp.concatenate([d_ref[i] for i in range(3 * pairs)], 1).astype(bf16)
    g_ref[...] = g
    give_ref[...] = dot(g, w_ref[away, :], NT).astype(bf16)
    keep_ref[...] = dot(g, w_ref[near, :], NT).astype(bf16)
    step = 384
    for ref, of in ((t_ref, m), (o_ref, 1 - m)):

        @pl.loop(0, part_cols // step)
        def _(i, ref=ref, of=of):
            total = dot(ref[:, pl.ds(pl.multiple_of(i * step, step), step)], g_ref[...], TN)
            for b in range(step // unit):
                quarters = [total[b * unit + r * ROWS :][:ROWS] for r in range(4)]
                first = jnp.concatenate([quarters[0], quarters[2]], 0)
                second = jnp.concatenate([quarters[1], quarters[3]], 0)
                by = lax.rem(b % Y + Y - y, Y)
                at = i * (step // unit // Y) + b // Y
                t = lax.bitwise_xor(of * (Z // MP) + at, z)
                mine_ref[by, t] = jnp.where(c == 0, first, second).astype(bf16)
                rest_ref[by, t] = jnp.where(c == 0, second, first).astype(bf16)


def core(where, tokens, others, mine, rest):
    rows, part_cols = others.shape
    half = tokens.shape[1] - part_cols
    width, n = MP * part_cols, 3 * half
    vm = pl.BlockSpec(memory_space=pltpu.VMEM)
    return pl.pallas_call(
        core_kernel,
        out_shape=(
            jax.ShapeDtypeStruct((rows, part_cols), bf16),
            jax.ShapeDtypeStruct((rows, part_cols), bf16),
            jax.ShapeDtypeStruct((Y, Z, XH * ROWS, n), bf16),
            jax.ShapeDtypeStruct((Y, Z, XH * ROWS, n), bf16),
        ),
        in_specs=[pl.BlockSpec(memory_space=pltpu.SMEM), vm, vm]
        + [pl.BlockSpec(memory_space=pltpu.HBM)] * 16,
        out_specs=(vm,) * 4,
        scratch_shapes=[
            pltpu.VMEM((width, n), bf16),
            pltpu.VMEM((4 * half // 128, rows, 128), f32),
            pltpu.VMEM((3 * half // 128, rows, 128), f32),
            pltpu.VMEM((rows, n), bf16),
            pltpu.VMEM((16,) + mine[0].shape, bf16),
            pltpu.SemaphoreType.DMA((16,)),
        ],
        compiler_params=pltpu.CompilerParams(vmem_limit_bytes=VMEM_LIMIT),
        cost_estimate=pl.CostEstimate(
            flops=6 * rows * width * n, bytes_accessed=8 * 2**20, transcendentals=0
        ),
        name="attention_core",
    )(where, tokens, others, *mine, *rest)


def combine_kernel(mine_ref, other_ref, *refs):
    own_ref, after_ref, before_ref, far_low, far_high, after_high, before_low = refs
    h = Z // 2

    def added(by, t):
        return mine_ref[by, t].astype(f32) + other_ref[by, t].astype(f32)

    @pl.loop(0, h)
    def _(t):
        far_low[t] = added(2, t).astype(bf16)
        far_high[t] = added(2, t + h).astype(bf16)
        own_ref[t] = added(0, t)
        own_ref[t + h] = added(0, t + h)
        after_ref[t] = added(1, t)
        after_high[t] = added(1, t + h).astype(bf16)
        before_low[t] = added(3, t).astype(bf16)
        before_ref[t] = added(3, t + h)


def combine(mine, other):
    vm = pl.BlockSpec(memory_space=pltpu.VMEM)
    block = mine.shape[2:]
    h = Z // 2
    return pl.pallas_call(
        combine_kernel,
        out_shape=[jax.ShapeDtypeStruct((n,) + block, f32) for n in (Z, h, h)]
        + [jax.ShapeDtypeStruct((h,) + block, bf16)] * 4,
        in_specs=[vm, vm],
        out_specs=[vm] * 7,
        compiler_params=pltpu.CompilerParams(vmem_limit_bytes=VMEM_LIMIT),
        cost_estimate=pl.CostEstimate(flops=0, bytes_accessed=2**20, transcendentals=0),
        name="combine_cores",
    )(mine, other)


def add_kernel(a_ref, b_ref, o_ref):
    total = a_ref[...].astype(f32) + b_ref[...].astype(f32)
    o_ref[...] = total.reshape(o_ref.shape).astype(bf16)


def add_parts(a, b):
    rows, cols = a.shape
    vm = pl.BlockSpec(memory_space=pltpu.VMEM)
    return pl.pallas_call(
        add_kernel,
        out_shape=jax.ShapeDtypeStruct((F, rows // F, cols), bf16),
        in_specs=[vm, vm],
        out_specs=vm,
        compiler_params=pltpu.CompilerParams(vmem_limit_bytes=16 * 2**20),
        cost_estimate=pl.CostEstimate(flops=0, bytes_accessed=2**20, transcendentals=0),
        name="add_parts",
    )(a, b)


def rows_kernel(x_ref, all_ref, part_ref):
    rows = x_ref[...].astype(f32).reshape(all_ref.shape).astype(bf16)
    all_ref[...] = rows
    part_ref[...] = rows[:, : part_ref.shape[1]]


def to_rows(x, part_cols):
    rows, n = x.shape[0] * x.shape[1], x.shape[2]
    vm = pl.BlockSpec(memory_space=pltpu.VMEM)
    return pl.pallas_call(
        rows_kernel,
        out_shape=(
            jax.ShapeDtypeStruct((rows, n), bf16),
            jax.ShapeDtypeStruct((rows, part_cols), bf16),
        ),
        in_specs=[vm],
        out_specs=(vm, vm),
        compiler_params=pltpu.CompilerParams(vmem_limit_bytes=24 * 2**20),
        cost_estimate=pl.CostEstimate(flops=0, bytes_accessed=2**20, transcendentals=0),
        name="to_rows",
    )(x)


FR = ("z", "y", "xh", "c")
PAIR = [(0, 1), (1, 0)]


def shift(x, axis, size, by):
    return lax.ppermute(x, axis, [(i, (i + by) % size) for i in range(size)])


def across(x, axis, size, by):
    return lax.ppermute(x, axis, [(i, i ^ by) for i in range(size)])


ZX = ("z", "xh")


def far_z(w):
    return jnp.stack([w] + [across(w, "z", Z, 2 * i) for i in range(1, Z // 2)], 0)


def near_zx(own):
    even = lax.axis_index("xh") == 0
    a, b, d = (across(own, ZX, Z * XH, by) for by in (1, 2, 3))

    def part(at):
        first = jnp.concatenate([jnp.where(even, own, a)[at], jnp.where(even, a, own)[at]], 1)
        second = jnp.concatenate([jnp.where(even, b, d)[at], jnp.where(even, d, b)[at]], 1)
        return jnp.stack([first, second], 1).reshape(Z // 2, XH * ROWS, own.shape[2])

    return part(slice(0, 2)), part(slice(2, 4))


def reduce_weight(mine, rest, got, finish, late):
    even = lax.axis_index("xh") == 0
    other = lax.ppermute(rest, "c", PAIR)
    h = Z // 2
    own, after, before, far_low, far_high, after_high, before_low = combine(mine, other)
    up_far = shift(far_low, "y", Y, 1)
    down_far = shift(far_high, "y", Y, Y - 1)
    up_high = shift(after_high, "y", Y, 1)
    down_low = shift(before_low, "y", Y, Y - 1)
    up_far, down_far, got = lax.optimization_barrier((up_far, down_far, got))
    summed = finish(got)
    up_low = (after + up_far.astype(f32)).astype(bf16)
    down_high = (before + down_far.astype(f32)).astype(bf16)
    up_low, down_high, summed = lax.optimization_barrier((up_low, down_high, summed))
    up_low = shift(up_low, "y", Y, 1)
    down_high = shift(down_high, "y", Y, Y - 1)
    low = own[:h] + up_low.astype(f32) + down_low.astype(f32)
    high = own[h:] + up_high.astype(f32) + down_high.astype(f32)
    blocks = jnp.concatenate([low, high], 0)
    kept = jnp.where(even, blocks[:, :ROWS], blocks[:, ROWS:])
    sent = jnp.where(even, blocks[:, ROWS:], blocks[:, :ROWS])
    total = kept[0::2]
    for by, x in ((2, kept[1::2]), (1, sent[0::2]), (3, sent[1::2])):
        total = total + across(x.astype(bf16), ZX, Z * XH, by).astype(f32)
    back = late(summed)
    total, back = lax.optimization_barrier((total, back))
    result = total[0]
    for i in range(1, h):
        result = result + across(total[i].astype(bf16), "z", Z, 2 * i).astype(f32)
    return result, back


def on_device(normed, out_grad, w_qkv):
    frames_dev, patches, width = normed.shape
    half = out_grad.shape[2]
    cols = width // MP
    count = patches // F
    n = 3 * half
    where = jnp.stack([lax.axis_index(a) for a in ("z", "y", "c", "mp")]).astype(jnp.int32)
    m = lax.axis_index("mp")
    part = lax.dynamic_slice_in_dim(normed, m * cols, cols, 2)
    tokens = jnp.concatenate([part, out_grad], axis=2).reshape(F, count, cols + half)

    rows = far_z(w_qkv.reshape(w_qkv.shape[0], n))
    tokens, rows = lax.optimization_barrier((tokens, rows))
    tokens = lax.all_to_all(tokens, FR, 0, 0, tiled=True)
    low, high = near_zx(rows)
    tokens, part = to_rows(tokens, cols)
    low, high, part = lax.optimization_barrier((low, high, part))
    others = lax.ppermute(part, "mp", PAIR)
    before_low = shift(low, "y", Y, 1)
    after_high = shift(high, "y", Y, Y - 1)
    before_high = shift(high, "y", Y, 1)
    after_low = shift(low, "y", Y, Y - 1)
    far_low = shift(before_low, "y", Y, 1)
    far_high = shift(after_high, "y", Y, Y - 1)
    mine = [low, high, after_low, after_high, far_low, far_high, before_low, before_high]
    rest = {i: lax.ppermute(mine[i], "c", PAIR) for i in (0, 1, 2, 3, 6, 7)}
    mine, others = lax.optimization_barrier((mine, others))
    rest.update({i: lax.ppermute(mine[i], "c", PAIR) for i in (4, 5)})

    rest = [rest[i] for i in range(8)]
    give, keep, mine, rest = core(where, tokens, others, mine, rest)
    got = lax.ppermute(give, "mp", PAIR)

    def finish(got):
        return add_parts(keep, got)

    def to_frames(x):
        return lax.all_to_all(x, FR, 0, 0, tiled=True)

    weight_grad, back = reduce_weight(mine, rest, got, finish, to_frames)
    input_grad = back.reshape(frames_dev, patches, cols)
    weight_grad = weight_grad * (1.0 / F)
    return (input_grad, weight_grad.reshape(w_qkv.shape))


def solution(mesh):
    fine = Mesh(mesh.devices.reshape(Z, Y, XH, C, MP), ("z", "y", "xh", "c", "mp"))
    in_specs = (P(FR, None, None), P(FR, None, "mp"), P(FR, None, "mp"))
    out_specs = (P(FR, None, "mp"), P(FR, None, "mp"))
    return jax.shard_map(
        on_device, mesh=fine, in_specs=in_specs, out_specs=out_specs, check_vma=False
    )
```

```python
import jax
import jax.numpy as jnp
from jax import lax
from jax.experimental import pallas as pl
from jax.experimental.pallas import tpu as pltpu
from jax.sharding import Mesh, PartitionSpec as P

HEAD_DIM = 64
Z, Y, XH, C, MP = 8, 4, 2, 2, 2
F = 128
ROWS = 12
VMEM_LIMIT = 32 * 2**20
bf16, f32 = jnp.bfloat16, jnp.float32
NT = (((1,), (1,)), ((), ()))
TN = (((0,), (0,)), ((), ()))


def dot(a, b, dims):
    return lax.dot_general(a, b, dims, preferred_element_type=f32)


def core_kernel(where_ref, x_ref, o_ref, *refs):
    pieces = refs[:16]
    give_ref, keep_ref, mine_ref, rest_ref, w_ref, s_ref, d_ref, g_ref, t_ref = refs[16:]
    t_ref[...] = x_ref[...].astype(f32).reshape(t_ref.shape).astype(bf16)
    z, y, c, m = (where_ref[i] for i in range(4))
    unit = XH * C * ROWS

    @pl.loop(0, Z // 2)
    def _(t):
        for i in range(8):
            by, high = i // 2, i % 2
            a = pieces[i][t].astype(f32)
            b = pieces[i + 8][t].astype(f32)
            first = jnp.where(c == 0, a, b)
            second = jnp.where(c == 0, b, a)
            rows = [first[:ROWS], second[:ROWS], first[ROWS:], second[ROWS:]]
            to = lax.bitwise_xor(z, t + high * (Z // 2)) * Y + lax.rem(by + y, Y)
            to = pl.ds(pl.multiple_of(to * unit, unit), unit)
            w_ref[to, :] = jnp.concatenate(rows, 0).astype(bf16)

    part_cols = o_ref.shape[1]
    rows, half = t_ref.shape[0], t_ref.shape[1] - part_cols
    count = rows // F
    scale = HEAD_DIM ** (-0.5)
    pairs = half // 128
    near = pl.ds(pl.multiple_of(m * part_cols, part_cols), part_cols)
    away = pl.ds(pl.multiple_of((1 - m) * part_cols, part_cols), part_cols)
    part = jnp.dot(t_ref[:, :part_cols], w_ref[near, :], preferred_element_type=f32)
    part += jnp.dot(o_ref[...], w_ref[away, :], preferred_element_type=f32)
    part = part.astype(bf16)
    for i in range(3 * pairs):
        s_ref[i] = part[:, i * 128 : (i + 1) * 128].astype(f32)
    for pair in range(pairs):
        at = part_cols + pair * 128
        s_ref[3 * pairs + pair] = t_ref[:, at : at + 128].astype(f32)
    low = lax.broadcasted_iota(jnp.int32, (F, 128), 1) < HEAD_DIM
    zero = jnp.zeros((F, 128), f32)

    def split(v):
        return jnp.concatenate([jnp.where(low, v, zero), jnp.where(low, zero, v)], 0).astype(bf16)

    @pl.loop(0, count)
    def _(p):
        at = pl.ds(p, F, stride=count)
        for pair in range(pairs):
            q, k, v, u = (s_ref[j * pairs + pair, at, :] for j in range(4))
            q2 = split(q * scale)
            u2 = split(u)
            k = k.astype(bf16)
            v = v.astype(bf16)
            weights = jnp.exp(dot(q2, k, NT))
            weights = weights / jnp.sum(weights, axis=-1, keepdims=True)
            dprobs = dot(u2, v, NT)
            center = jnp.sum(weights * dprobs, axis=-1, keepdims=True)
            dscores = (weights * (dprobs - center)).astype(bf16)
            dv = dot(weights.astype(bf16), u2, TN)
            dk = dot(dscores, q2, TN)
            both = jnp.dot(dscores, k, preferred_element_type=f32) * scale
            dq = jnp.where(low, both[:F], both[F:])
            for j, part in enumerate((dq, dk, dv)):
                d_ref[j * pairs + pair, at, :] = part
    g = jnp.concatenate([d_ref[i] for i in range(3 * pairs)], 1).astype(bf16)
    g_ref[...] = g
    give_ref[...] = dot(g, w_ref[away, :], NT).astype(bf16)
    keep_ref[...] = dot(g, w_ref[near, :], NT).astype(bf16)
    step = 384
    for ref, of in ((t_ref, m), (o_ref, 1 - m)):
        for i in range(part_cols // step):
            total = dot(ref[:, i * step : (i + 1) * step], g_ref[...], TN)
            for b in range(step // unit):
                quarters = [total[b * unit + r * ROWS :][:ROWS] for r in range(4)]
                first = jnp.concatenate([quarters[0], quarters[2]], 0)
                second = jnp.concatenate([quarters[1], quarters[3]], 0)
                by = lax.rem(b % Y + Y - y, Y)
                at = i * (step // unit // Y) + b // Y
                t = lax.bitwise_xor(of * (Z // MP) + at, z)
                mine_ref[by, t] = jnp.where(c == 0, first, second).astype(bf16)
                rest_ref[by, t] = jnp.where(c == 0, second, first).astype(bf16)


def core(where, tokens, others, mine, rest):
    rows, part_cols = others.shape
    half = tokens.shape[2] - part_cols
    width, n = MP * part_cols, 3 * half
    vm = pl.BlockSpec(memory_space=pltpu.VMEM)
    return pl.pallas_call(
        core_kernel,
        out_shape=(
            jax.ShapeDtypeStruct((rows, part_cols), bf16),
            jax.ShapeDtypeStruct((rows, part_cols), bf16),
            jax.ShapeDtypeStruct((Y, Z, XH * ROWS, n), bf16),
            jax.ShapeDtypeStruct((Y, Z, XH * ROWS, n), bf16),
        ),
        in_specs=[pl.BlockSpec(memory_space=pltpu.SMEM)] + [vm] * 18,
        out_specs=(vm,) * 4,
        scratch_shapes=[
            pltpu.VMEM((width, n), bf16),
            pltpu.VMEM((4 * half // 128, rows, 128), f32),
            pltpu.VMEM((3 * half // 128, rows, 128), f32),
            pltpu.VMEM((rows, n), bf16),
            pltpu.VMEM((rows, part_cols + half), bf16),
        ],
        compiler_params=pltpu.CompilerParams(vmem_limit_bytes=VMEM_LIMIT),
        cost_estimate=pl.CostEstimate(
            flops=6 * rows * width * n, bytes_accessed=8 * 2**20, transcendentals=0
        ),
        name="attention_core",
    )(where, tokens, others, *mine, *rest)


def combine_kernel(mine_ref, other_ref, *refs):
    own_ref, after_ref, before_ref, far_low, far_high, after_high, before_low = refs
    h = Z // 2

    def added(by, t):
        return mine_ref[by, t].astype(f32) + other_ref[by, t].astype(f32)

    @pl.loop(0, h)
    def _(t):
        far_low[t] = added(2, t).astype(bf16)
        far_high[t] = added(2, t + h).astype(bf16)
        own_ref[t] = added(0, t)
        own_ref[t + h] = added(0, t + h)
        after_ref[t] = added(1, t)
        after_high[t] = added(1, t + h).astype(bf16)
        before_low[t] = added(3, t).astype(bf16)
        before_ref[t] = added(3, t + h)


def combine(mine, other):
    vm = pl.BlockSpec(memory_space=pltpu.VMEM)
    block = mine.shape[2:]
    h = Z // 2
    return pl.pallas_call(
        combine_kernel,
        out_shape=[jax.ShapeDtypeStruct((n,) + block, f32) for n in (Z, h, h)]
        + [jax.ShapeDtypeStruct((h,) + block, bf16)] * 4,
        in_specs=[vm, vm],
        out_specs=[vm] * 7,
        compiler_params=pltpu.CompilerParams(vmem_limit_bytes=VMEM_LIMIT),
        cost_estimate=pl.CostEstimate(flops=0, bytes_accessed=2**20, transcendentals=0),
        name="combine_cores",
    )(mine, other)


def add_kernel(a_ref, b_ref, o_ref):
    total = a_ref[...].astype(f32) + b_ref[...].astype(f32)
    o_ref[...] = total.reshape(o_ref.shape).astype(bf16)


def add_parts(a, b):
    rows, cols = a.shape
    vm = pl.BlockSpec(memory_space=pltpu.VMEM)
    return pl.pallas_call(
        add_kernel,
        out_shape=jax.ShapeDtypeStruct((F, rows // F, cols), bf16),
        in_specs=[vm, vm],
        out_specs=vm,
        compiler_params=pltpu.CompilerParams(vmem_limit_bytes=16 * 2**20),
        cost_estimate=pl.CostEstimate(flops=0, bytes_accessed=2**20, transcendentals=0),
        name="add_parts",
    )(a, b)


def rows_kernel(x_ref, part_ref):
    cols = part_ref.shape[1]
    part_ref[...] = x_ref[:, :, :cols].astype(f32).reshape(part_ref.shape).astype(bf16)


def part_rows(x, part_cols):
    vm = pl.BlockSpec(memory_space=pltpu.VMEM)
    return pl.pallas_call(
        rows_kernel,
        out_shape=jax.ShapeDtypeStruct((x.shape[0] * x.shape[1], part_cols), bf16),
        in_specs=[vm],
        out_specs=vm,
        compiler_params=pltpu.CompilerParams(vmem_limit_bytes=16 * 2**20),
        cost_estimate=pl.CostEstimate(flops=0, bytes_accessed=2**20, transcendentals=0),
        name="part_rows",
    )(x)


FR = ("z", "y", "xh", "c")
PAIR = [(0, 1), (1, 0)]


def shift(x, axis, size, by):
    return lax.ppermute(x, axis, [(i, (i + by) % size) for i in range(size)])


def across(x, axis, size, by):
    return lax.ppermute(x, axis, [(i, i ^ by) for i in range(size)])


ZX = ("z", "xh")


def far_z(w):
    return jnp.stack([w] + [across(w, "z", Z, 2 * i) for i in range(1, Z // 2)], 0)


def near_zx(own):
    even = lax.axis_index("xh") == 0
    a, b, d = (across(own, ZX, Z * XH, by) for by in (1, 2, 3))

    def part(at):
        first = jnp.concatenate([jnp.where(even, own, a)[at], jnp.where(even, a, own)[at]], 1)
        second = jnp.concatenate([jnp.where(even, b, d)[at], jnp.where(even, d, b)[at]], 1)
        return jnp.stack([first, second], 1).reshape(Z // 2, XH * ROWS, own.shape[2])

    return part(slice(0, 2)), part(slice(2, 4))


def reduce_weight(mine, rest, got, finish, late):
    even = lax.axis_index("xh") == 0
    other = lax.ppermute(rest, "c", PAIR)
    h = Z // 2
    own, after, before, far_low, far_high, after_high, before_low = combine(mine, other)
    up_far = shift(far_low, "y", Y, 1)
    down_far = shift(far_high, "y", Y, Y - 1)
    up_high = shift(after_high, "y", Y, 1)
    down_low = shift(before_low, "y", Y, Y - 1)
    up_far, down_far, got = lax.optimization_barrier((up_far, down_far, got))
    summed = finish(got)
    up_low = (after + up_far.astype(f32)).astype(bf16)
    down_high = (before + down_far.astype(f32)).astype(bf16)
    up_low, down_high, summed = lax.optimization_barrier((up_low, down_high, summed))
    up_low = shift(up_low, "y", Y, 1)
    down_high = shift(down_high, "y", Y, Y - 1)
    low = own[:h] + up_low.astype(f32) + down_low.astype(f32)
    high = own[h:] + up_high.astype(f32) + down_high.astype(f32)
    blocks = jnp.concatenate([low, high], 0)
    kept = jnp.where(even, blocks[:, :ROWS], blocks[:, ROWS:])
    sent = jnp.where(even, blocks[:, ROWS:], blocks[:, :ROWS])
    total = kept[0::2]
    for by, x in ((2, kept[1::2]), (1, sent[0::2]), (3, sent[1::2])):
        total = total + across(x.astype(bf16), ZX, Z * XH, by).astype(f32)
    back = late(summed)
    total, back = lax.optimization_barrier((total, back))
    result = total[0]
    for i in range(1, h):
        result = result + across(total[i].astype(bf16), "z", Z, 2 * i).astype(f32)
    return result, back


def on_device(normed, out_grad, w_qkv):
    frames_dev, patches, width = normed.shape
    half = out_grad.shape[2]
    cols = width // MP
    count = patches // F
    n = 3 * half
    where = jnp.stack([lax.axis_index(a) for a in ("z", "y", "c", "mp")]).astype(jnp.int32)
    m = lax.axis_index("mp")
    part = lax.dynamic_slice_in_dim(normed, m * cols, cols, 2)
    tokens = jnp.concatenate([part, out_grad], axis=2).reshape(F, count, cols + half)

    rows = far_z(w_qkv.reshape(w_qkv.shape[0], n))
    tokens, rows = lax.optimization_barrier((tokens, rows))
    tokens = lax.all_to_all(tokens, FR, 0, 0, tiled=True)
    low, high = near_zx(rows)
    part = part_rows(tokens, cols)
    low, high, part = lax.optimization_barrier((low, high, part))
    others = lax.ppermute(part, "mp", PAIR)
    before_low = shift(low, "y", Y, 1)
    after_high = shift(high, "y", Y, Y - 1)
    before_high = shift(high, "y", Y, 1)
    after_low = shift(low, "y", Y, Y - 1)
    far_low = shift(before_low, "y", Y, 1)
    far_high = shift(after_high, "y", Y, Y - 1)
    mine = [low, high, after_low, after_high, far_low, far_high, before_low, before_high]
    rest = {i: lax.ppermute(mine[i], "c", PAIR) for i in (0, 1, 2, 3, 6, 7)}
    mine, others = lax.optimization_barrier((mine, others))
    rest.update({i: lax.ppermute(mine[i], "c", PAIR) for i in (4, 5)})

    rest = [rest[i] for i in range(8)]
    give, keep, mine, rest = core(where, tokens, others, mine, rest)
    got = lax.ppermute(give, "mp", PAIR)

    def finish(got):
        return add_parts(keep, got)

    def to_frames(x):
        return lax.all_to_all(x, FR, 0, 0, tiled=True)

    weight_grad, back = reduce_weight(mine, rest, got, finish, to_frames)
    input_grad = back.reshape(frames_dev, patches, cols)
    weight_grad = weight_grad * (1.0 / F)
    return (input_grad, weight_grad.reshape(w_qkv.shape))


def solution(mesh):
    fine = Mesh(mesh.devices.reshape(Z, Y, XH, C, MP), ("z", "y", "xh", "c", "mp"))
    in_specs = (P(FR, None, None), P(FR, None, "mp"), P(FR, None, "mp"))
    out_specs = (P(FR, None, "mp"), P(FR, None, "mp"))
    return jax.shard_map(
        on_device, mesh=fine, in_specs=in_specs, out_specs=out_specs, check_vma=False
    )
```

```python
import jax
import jax.numpy as jnp
from jax import lax
from jax.experimental import pallas as pl
from jax.experimental.pallas import tpu as pltpu
from jax.sharding import Mesh, PartitionSpec as P

HEAD_DIM = 64
Z, Y, XH, C, MP = 8, 4, 2, 2, 2
F = 128
ROWS = 12
VMEM_LIMIT = 16 * 2**20
CORE_LIMIT = 56 * 2**20
bf16, f32 = jnp.bfloat16, jnp.float32
NT = (((1,), (1,)), ((), ()))
TN = (((0,), (0,)), ((), ()))


def dot(a, b, dims):
    return lax.dot_general(a, b, dims, preferred_element_type=f32)


def core_kernel(where_ref, x_ref, o_ref, *refs):
    pieces = refs[:16]
    give_ref, keep_ref, mine_ref, rest_ref, w_ref, s_ref, d_ref, g_ref, t_ref = refs[16:]
    t_ref[...] = x_ref[...].astype(f32).reshape(t_ref.shape).astype(bf16)
    z, y, c, m = (where_ref[i] for i in range(4))
    unit = XH * C * ROWS

    @pl.loop(0, Z // 2)
    def _(t):
        for i in range(8):
            by, high = i // 2, i % 2
            a = pieces[i][t].astype(f32)
            b = pieces[i + 8][t].astype(f32)
            first = jnp.where(c == 0, a, b)
            second = jnp.where(c == 0, b, a)
            rows = [first[:ROWS], second[:ROWS], first[ROWS:], second[ROWS:]]
            to = lax.bitwise_xor(z, t + high * (Z // 2)) * Y + lax.rem(by + y, Y)
            to = pl.ds(pl.multiple_of(to * unit, unit), unit)
            w_ref[to, :] = jnp.concatenate(rows, 0).astype(bf16)

    part_cols = o_ref.shape[1]
    rows, half = t_ref.shape[0], t_ref.shape[1] - part_cols
    count = rows // F
    scale = HEAD_DIM ** (-0.5)
    pairs = half // 128
    near = pl.ds(pl.multiple_of(m * part_cols, part_cols), part_cols)
    away = pl.ds(pl.multiple_of((1 - m) * part_cols, part_cols), part_cols)
    part = jnp.dot(t_ref[:, :part_cols], w_ref[near, :], preferred_element_type=f32)
    part += jnp.dot(o_ref[...], w_ref[away, :], preferred_element_type=f32)
    part = part.astype(bf16)
    for i in range(3 * pairs):
        s_ref[i] = part[:, i * 128 : (i + 1) * 128].astype(f32)
    for pair in range(pairs):
        at = part_cols + pair * 128
        s_ref[3 * pairs + pair] = t_ref[:, at : at + 128].astype(f32)
    low = lax.broadcasted_iota(jnp.int32, (F, 128), 1) < HEAD_DIM
    zero = jnp.zeros((F, 128), f32)

    def split(v):
        return jnp.concatenate([jnp.where(low, v, zero), jnp.where(low, zero, v)], 0).astype(bf16)

    @pl.loop(0, count)
    def _(p):
        at = pl.ds(p, F, stride=count)
        for pair in range(pairs):
            q, k, v, u = (s_ref[j * pairs + pair, at, :] for j in range(4))
            q2 = split(q * scale)
            u2 = split(u)
            k = k.astype(bf16)
            v = v.astype(bf16)
            weights = jnp.exp(dot(q2, k, NT))
            weights = weights / jnp.sum(weights, axis=-1, keepdims=True)
            dprobs = dot(u2, v, NT)
            center = jnp.sum(weights * dprobs, axis=-1, keepdims=True)
            dscores = (weights * (dprobs - center)).astype(bf16)
            dv = dot(weights.astype(bf16), u2, TN)
            dk = dot(dscores, q2, TN)
            both = jnp.dot(dscores, k, preferred_element_type=f32) * scale
            dq = jnp.where(low, both[:F], both[F:])
            for j, part in enumerate((dq, dk, dv)):
                d_ref[j * pairs + pair, at, :] = part
    g = jnp.concatenate([d_ref[i] for i in range(3 * pairs)], 1).astype(bf16)
    g_ref[...] = g
    give_ref[...] = dot(g, w_ref[away, :], NT).astype(bf16)
    keep_ref[...] = dot(g, w_ref[near, :], NT).astype(bf16)
    step = 384
    for ref, of in ((t_ref, m), (o_ref, 1 - m)):
        for i in range(part_cols // step):
            total = dot(ref[:, i * step : (i + 1) * step], g_ref[...], TN)
            for b in range(step // unit):
                quarters = [total[b * unit + r * ROWS :][:ROWS] for r in range(4)]
                first = jnp.concatenate([quarters[0], quarters[2]], 0)
                second = jnp.concatenate([quarters[1], quarters[3]], 0)
                by = lax.rem(b % Y + Y - y, Y)
                at = i * (step // unit // Y) + b // Y
                t = lax.bitwise_xor(of * (Z // MP) + at, z)
                mine_ref[by, t] = jnp.where(c == 0, first, second).astype(bf16)
                rest_ref[by, t] = jnp.where(c == 0, second, first).astype(bf16)


def core(where, tokens, others, mine, rest):
    rows, part_cols = others.shape
    half = tokens.shape[2] - part_cols
    width, n = MP * part_cols, 3 * half
    vm = pl.BlockSpec(memory_space=pltpu.VMEM)
    return pl.pallas_call(
        core_kernel,
        out_shape=(
            jax.ShapeDtypeStruct((rows, part_cols), bf16),
            jax.ShapeDtypeStruct((rows, part_cols), bf16),
            jax.ShapeDtypeStruct((Y, Z, XH * ROWS, n), bf16),
            jax.ShapeDtypeStruct((Y, Z, XH * ROWS, n), bf16),
        ),
        in_specs=[pl.BlockSpec(memory_space=pltpu.SMEM)] + [vm] * 18,
        out_specs=(vm,) * 4,
        scratch_shapes=[
            pltpu.VMEM((width, n), bf16),
            pltpu.VMEM((4 * half // 128, rows, 128), f32),
            pltpu.VMEM((3 * half // 128, rows, 128), f32),
            pltpu.VMEM((rows, n), bf16),
            pltpu.VMEM((rows, part_cols + half), bf16),
        ],
        compiler_params=pltpu.CompilerParams(vmem_limit_bytes=CORE_LIMIT),
        cost_estimate=pl.CostEstimate(
            flops=6 * rows * width * n, bytes_accessed=8 * 2**20, transcendentals=0
        ),
        name="attention_core",
    )(where, tokens, others, *mine, *rest)


def combine_kernel(mine_ref, other_ref, *refs):
    own_ref, after_ref, before_ref, far_low, far_high, after_high, before_low = refs
    h = Z // 2

    def added(by, t):
        return mine_ref[by, t].astype(f32) + other_ref[by, t].astype(f32)

    @pl.loop(0, h)
    def _(t):
        far_low[t] = added(2, t).astype(bf16)
        far_high[t] = added(2, t + h).astype(bf16)
        own_ref[t] = added(0, t)
        own_ref[t + h] = added(0, t + h)
        after_ref[t] = added(1, t)
        after_high[t] = added(1, t + h).astype(bf16)
        before_low[t] = added(3, t).astype(bf16)
        before_ref[t] = added(3, t + h)


def combine(mine, other):
    vm = pl.BlockSpec(memory_space=pltpu.VMEM)
    block = mine.shape[2:]
    h = Z // 2
    return pl.pallas_call(
        combine_kernel,
        out_shape=[jax.ShapeDtypeStruct((n,) + block, f32) for n in (Z, h, h)]
        + [jax.ShapeDtypeStruct((h,) + block, bf16)] * 4,
        in_specs=[vm, vm],
        out_specs=[vm] * 7,
        compiler_params=pltpu.CompilerParams(vmem_limit_bytes=VMEM_LIMIT),
        cost_estimate=pl.CostEstimate(flops=0, bytes_accessed=2**20, transcendentals=0),
        name="combine_cores",
    )(mine, other)


def add_kernel(a_ref, b_ref, o_ref):
    total = a_ref[...].astype(f32) + b_ref[...].astype(f32)
    o_ref[...] = total.reshape(o_ref.shape).astype(bf16)


def add_parts(a, b):
    rows, cols = a.shape
    vm = pl.BlockSpec(memory_space=pltpu.VMEM)
    return pl.pallas_call(
        add_kernel,
        out_shape=jax.ShapeDtypeStruct((F, rows // F, cols), bf16),
        in_specs=[vm, vm],
        out_specs=vm,
        compiler_params=pltpu.CompilerParams(vmem_limit_bytes=16 * 2**20),
        cost_estimate=pl.CostEstimate(flops=0, bytes_accessed=2**20, transcendentals=0),
        name="add_parts",
    )(a, b)


def rows_kernel(x_ref, part_ref):
    cols = part_ref.shape[1]
    part_ref[...] = x_ref[:, :, :cols].astype(f32).reshape(part_ref.shape).astype(bf16)


def part_rows(x, part_cols):
    vm = pl.BlockSpec(memory_space=pltpu.VMEM)
    return pl.pallas_call(
        rows_kernel,
        out_shape=jax.ShapeDtypeStruct((x.shape[0] * x.shape[1], part_cols), bf16),
        in_specs=[vm],
        out_specs=vm,
        compiler_params=pltpu.CompilerParams(vmem_limit_bytes=16 * 2**20),
        cost_estimate=pl.CostEstimate(flops=0, bytes_accessed=2**20, transcendentals=0),
        name="part_rows",
    )(x)


FR = ("z", "y", "xh", "c")
PAIR = [(0, 1), (1, 0)]


def shift(x, axis, size, by):
    return lax.ppermute(x, axis, [(i, (i + by) % size) for i in range(size)])


def across(x, axis, size, by):
    return lax.ppermute(x, axis, [(i, i ^ by) for i in range(size)])


ZX = ("z", "xh")


def far_z(w):
    return jnp.stack([w] + [across(w, "z", Z, 2 * i) for i in range(1, Z // 2)], 0)


def near_zx(own):
    even = lax.axis_index("xh") == 0
    a, b, d = (across(own, ZX, Z * XH, by) for by in (1, 2, 3))

    def part(at):
        first = jnp.concatenate([jnp.where(even, own, a)[at], jnp.where(even, a, own)[at]], 1)
        second = jnp.concatenate([jnp.where(even, b, d)[at], jnp.where(even, d, b)[at]], 1)
        return jnp.stack([first, second], 1).reshape(Z // 2, XH * ROWS, own.shape[2])

    return part(slice(0, 2)), part(slice(2, 4))


def reduce_weight(mine, rest, got, finish, late):
    even = lax.axis_index("xh") == 0
    other = lax.ppermute(rest, "c", PAIR)
    h = Z // 2
    own, after, before, far_low, far_high, after_high, before_low = combine(mine, other)
    up_far = shift(far_low, "y", Y, 1)
    down_far = shift(far_high, "y", Y, Y - 1)
    up_high = shift(after_high, "y", Y, 1)
    down_low = shift(before_low, "y", Y, Y - 1)
    up_far, down_far, got = lax.optimization_barrier((up_far, down_far, got))
    summed = finish(got)
    up_low = (after + up_far.astype(f32)).astype(bf16)
    down_high = (before + down_far.astype(f32)).astype(bf16)
    up_low, down_high, summed = lax.optimization_barrier((up_low, down_high, summed))
    up_low = shift(up_low, "y", Y, 1)
    down_high = shift(down_high, "y", Y, Y - 1)
    low = own[:h] + up_low.astype(f32) + down_low.astype(f32)
    high = own[h:] + up_high.astype(f32) + down_high.astype(f32)
    blocks = jnp.concatenate([low, high], 0)
    kept = jnp.where(even, blocks[:, :ROWS], blocks[:, ROWS:])
    sent = jnp.where(even, blocks[:, ROWS:], blocks[:, :ROWS])
    total = kept[0::2]
    for by, x in ((2, kept[1::2]), (1, sent[0::2]), (3, sent[1::2])):
        total = total + across(x.astype(bf16), ZX, Z * XH, by).astype(f32)
    back = late(summed)
    total, back = lax.optimization_barrier((total, back))
    result = total[0]
    for i in range(1, h):
        result = result + across(total[i].astype(bf16), "z", Z, 2 * i).astype(f32)
    return result, back


def on_device(normed, out_grad, w_qkv):
    frames_dev, patches, width = normed.shape
    half = out_grad.shape[2]
    cols = width // MP
    count = patches // F
    n = 3 * half
    where = jnp.stack([lax.axis_index(a) for a in ("z", "y", "c", "mp")]).astype(jnp.int32)
    m = lax.axis_index("mp")
    part = lax.dynamic_slice_in_dim(normed, m * cols, cols, 2)
    tokens = jnp.concatenate([part, out_grad], axis=2).reshape(F, count, cols + half)

    rows = far_z(w_qkv.reshape(w_qkv.shape[0], n))
    tokens, rows = lax.optimization_barrier((tokens, rows))
    tokens = lax.all_to_all(tokens, FR, 0, 0, tiled=True)
    low, high = near_zx(rows)
    part = part_rows(tokens, cols)
    low, high, part = lax.optimization_barrier((low, high, part))
    others = lax.ppermute(part, "mp", PAIR)
    before_low = shift(low, "y", Y, 1)
    after_high = shift(high, "y", Y, Y - 1)
    before_high = shift(high, "y", Y, 1)
    after_low = shift(low, "y", Y, Y - 1)
    far_low = shift(before_low, "y", Y, 1)
    far_high = shift(after_high, "y", Y, Y - 1)
    mine = [low, high, after_low, after_high, far_low, far_high, before_low, before_high]
    rest = {i: lax.ppermute(mine[i], "c", PAIR) for i in (0, 1, 2, 3, 6, 7)}
    mine, others = lax.optimization_barrier((mine, others))
    rest.update({i: lax.ppermute(mine[i], "c", PAIR) for i in (4, 5)})

    rest = [rest[i] for i in range(8)]
    give, keep, mine, rest = core(where, tokens, others, mine, rest)
    got = lax.ppermute(give, "mp", PAIR)

    def finish(got):
        return add_parts(keep, got)

    def to_frames(x):
        return lax.all_to_all(x, FR, 0, 0, tiled=True)

    weight_grad, back = reduce_weight(mine, rest, got, finish, to_frames)
    input_grad = back.reshape(frames_dev, patches, cols)
    weight_grad = weight_grad * (1.0 / F)
    return (input_grad, weight_grad.reshape(w_qkv.shape))


def solution(mesh):
    fine = Mesh(mesh.devices.reshape(Z, Y, XH, C, MP), ("z", "y", "xh", "c", "mp"))
    in_specs = (P(FR, None, None), P(FR, None, "mp"), P(FR, None, "mp"))
    out_specs = (P(FR, None, "mp"), P(FR, None, "mp"))
    return jax.shard_map(
        on_device, mesh=fine, in_specs=in_specs, out_specs=out_specs, check_vma=False
    )
```

```python
import jax
import jax.numpy as jnp
from jax import lax
from jax.experimental import pallas as pl
from jax.experimental.pallas import tpu as pltpu
from jax.sharding import Mesh, PartitionSpec as P

HEAD_DIM = 64
Z, Y, XH, C, MP = 8, 4, 2, 2, 2
F = 128
ROWS = 12
VMEM_LIMIT = 16 * 2**20
CORE_LIMIT = 56 * 2**20
bf16, f32 = jnp.bfloat16, jnp.float32
NT = (((1,), (1,)), ((), ()))
TN = (((0,), (0,)), ((), ()))


def dot(a, b, dims):
    return lax.dot_general(a, b, dims, preferred_element_type=f32)


def core_kernel(where_ref, x_hbm, o_hbm, *refs):
    blocks = refs[:16]
    give_ref, keep_ref, mine_ref, rest_ref, w_ref, s_ref, d_ref, g_ref, t_ref = refs[16:25]
    x_ref, o_ref, pieces, sems = refs[25:]
    copies = [pltpu.make_async_copy(blocks[i], pieces.at[i], sems.at[i]) for i in range(16)]
    copy_x = pltpu.make_async_copy(x_hbm, x_ref, sems.at[16])
    copy_o = pltpu.make_async_copy(o_hbm, o_ref, sems.at[17])
    for i in range(8):
        copies[i].start()
        copies[i + 8].start()
    copy_x.start()
    copy_o.start()
    z, y, c, m = (where_ref[i] for i in range(4))
    unit = XH * C * ROWS

    for i in range(8):
        by, high = i // 2, i % 2
        copies[i].wait()
        copies[i + 8].wait()

        @pl.loop(0, Z // 2)
        def _(t, i=i, by=by, high=high):
            a = pieces[i, t].astype(f32)
            b = pieces[i + 8, t].astype(f32)
            first = jnp.where(c == 0, a, b)
            second = jnp.where(c == 0, b, a)
            rows = [first[:ROWS], second[:ROWS], first[ROWS:], second[ROWS:]]
            to = lax.bitwise_xor(z, t + high * (Z // 2)) * Y + lax.rem(by + y, Y)
            to = pl.ds(pl.multiple_of(to * unit, unit), unit)
            w_ref[to, :] = jnp.concatenate(rows, 0).astype(bf16)

    copy_x.wait()
    t_ref[...] = x_ref[...].astype(f32).reshape(t_ref.shape).astype(bf16)
    copy_o.wait()
    part_cols = o_ref.shape[1]
    rows, half = t_ref.shape[0], t_ref.shape[1] - part_cols
    count = rows // F
    scale = HEAD_DIM ** (-0.5)
    pairs = half // 128
    near = pl.ds(pl.multiple_of(m * part_cols, part_cols), part_cols)
    away = pl.ds(pl.multiple_of((1 - m) * part_cols, part_cols), part_cols)
    part = jnp.dot(t_ref[:, :part_cols], w_ref[near, :], preferred_element_type=f32)
    part += jnp.dot(o_ref[...], w_ref[away, :], preferred_element_type=f32)
    part = part.astype(bf16)
    for i in range(3 * pairs):
        s_ref[i] = part[:, i * 128 : (i + 1) * 128].astype(f32)
    for pair in range(pairs):
        at = part_cols + pair * 128
        s_ref[3 * pairs + pair] = t_ref[:, at : at + 128].astype(f32)
    low = lax.broadcasted_iota(jnp.int32, (F, 128), 1) < HEAD_DIM
    zero = jnp.zeros((F, 128), f32)

    def split(v):
        return jnp.concatenate([jnp.where(low, v, zero), jnp.where(low, zero, v)], 0).astype(bf16)

    @pl.loop(0, count)
    def _(p):
        at = pl.ds(p, F, stride=count)
        for pair in range(pairs):
            q, k, v, u = (s_ref[j * pairs + pair, at, :] for j in range(4))
            q2 = split(q * scale)
            u2 = split(u)
            k = k.astype(bf16)
            v = v.astype(bf16)
            weights = jnp.exp(dot(q2, k, NT))
            weights = weights / jnp.sum(weights, axis=-1, keepdims=True)
            dprobs = dot(u2, v, NT)
            center = jnp.sum(weights * dprobs, axis=-1, keepdims=True)
            dscores = (weights * (dprobs - center)).astype(bf16)
            dv = dot(weights.astype(bf16), u2, TN)
            dk = dot(dscores, q2, TN)
            both = jnp.dot(dscores, k, preferred_element_type=f32) * scale
            dq = jnp.where(low, both[:F], both[F:])
            for j, part in enumerate((dq, dk, dv)):
                d_ref[j * pairs + pair, at, :] = part
    g = jnp.concatenate([d_ref[i] for i in range(3 * pairs)], 1).astype(bf16)
    g_ref[...] = g
    give_ref[...] = dot(g, w_ref[away, :], NT).astype(bf16)
    keep_ref[...] = dot(g, w_ref[near, :], NT).astype(bf16)
    step = 384
    for ref, of in ((t_ref, m), (o_ref, 1 - m)):
        for i in range(part_cols // step):
            total = dot(ref[:, i * step : (i + 1) * step], g_ref[...], TN)
            for b in range(step // unit):
                quarters = [total[b * unit + r * ROWS :][:ROWS] for r in range(4)]
                first = jnp.concatenate([quarters[0], quarters[2]], 0)
                second = jnp.concatenate([quarters[1], quarters[3]], 0)
                by = lax.rem(b % Y + Y - y, Y)
                at = i * (step // unit // Y) + b // Y
                t = lax.bitwise_xor(of * (Z // MP) + at, z)
                mine_ref[by, t] = jnp.where(c == 0, first, second).astype(bf16)
                rest_ref[by, t] = jnp.where(c == 0, second, first).astype(bf16)


def core(where, tokens, others, mine, rest):
    rows, part_cols = others.shape
    half = tokens.shape[2] - part_cols
    width, n = MP * part_cols, 3 * half
    vm = pl.BlockSpec(memory_space=pltpu.VMEM)
    return pl.pallas_call(
        core_kernel,
        out_shape=(
            jax.ShapeDtypeStruct((rows, part_cols), bf16),
            jax.ShapeDtypeStruct((rows, part_cols), bf16),
            jax.ShapeDtypeStruct((Y, Z, XH * ROWS, n), bf16),
            jax.ShapeDtypeStruct((Y, Z, XH * ROWS, n), bf16),
        ),
        in_specs=[pl.BlockSpec(memory_space=pltpu.SMEM)]
        + [pl.BlockSpec(memory_space=pl.ANY)] * 18,
        out_specs=(vm,) * 4,
        scratch_shapes=[
            pltpu.VMEM((width, n), bf16),
            pltpu.VMEM((4 * half // 128, rows, 128), f32),
            pltpu.VMEM((3 * half // 128, rows, 128), f32),
            pltpu.VMEM((rows, n), bf16),
            pltpu.VMEM((rows, part_cols + half), bf16),
            pltpu.VMEM(tokens.shape, bf16),
            pltpu.VMEM(others.shape, bf16),
            pltpu.VMEM((16,) + mine[0].shape, bf16),
            pltpu.SemaphoreType.DMA((18,)),
        ],
        compiler_params=pltpu.CompilerParams(vmem_limit_bytes=CORE_LIMIT),
        cost_estimate=pl.CostEstimate(
            flops=6 * rows * width * n, bytes_accessed=8 * 2**20, transcendentals=0
        ),
        name="attention_core",
    )(where, tokens, others, *mine, *rest)


def combine_kernel(mine_ref, other_ref, *refs):
    own_ref, after_ref, before_ref, far_low, far_high, after_high, before_low = refs
    h = Z // 2

    def added(by, t):
        return mine_ref[by, t].astype(f32) + other_ref[by, t].astype(f32)

    @pl.loop(0, h)
    def _(t):
        far_low[t] = added(2, t).astype(bf16)
        far_high[t] = added(2, t + h).astype(bf16)
        own_ref[t] = added(0, t)
        own_ref[t + h] = added(0, t + h)
        after_ref[t] = added(1, t)
        after_high[t] = added(1, t + h).astype(bf16)
        before_low[t] = added(3, t).astype(bf16)
        before_ref[t] = added(3, t + h)


def combine(mine, other):
    vm = pl.BlockSpec(memory_space=pltpu.VMEM)
    block = mine.shape[2:]
    h = Z // 2
    return pl.pallas_call(
        combine_kernel,
        out_shape=[jax.ShapeDtypeStruct((n,) + block, f32) for n in (Z, h, h)]
        + [jax.ShapeDtypeStruct((h,) + block, bf16)] * 4,
        in_specs=[vm, vm],
        out_specs=[vm] * 7,
        compiler_params=pltpu.CompilerParams(vmem_limit_bytes=VMEM_LIMIT),
        cost_estimate=pl.CostEstimate(flops=0, bytes_accessed=2**20, transcendentals=0),
        name="combine_cores",
    )(mine, other)


def add_kernel(a_ref, b_ref, o_ref):
    total = a_ref[...].astype(f32) + b_ref[...].astype(f32)
    o_ref[...] = total.reshape(o_ref.shape).astype(bf16)


def add_parts(a, b):
    rows, cols = a.shape
    vm = pl.BlockSpec(memory_space=pltpu.VMEM)
    return pl.pallas_call(
        add_kernel,
        out_shape=jax.ShapeDtypeStruct((F, rows // F, cols), bf16),
        in_specs=[vm, vm],
        out_specs=vm,
        compiler_params=pltpu.CompilerParams(vmem_limit_bytes=16 * 2**20),
        cost_estimate=pl.CostEstimate(flops=0, bytes_accessed=2**20, transcendentals=0),
        name="add_parts",
    )(a, b)


def rows_kernel(x_ref, part_ref):
    cols = part_ref.shape[1]
    part_ref[...] = x_ref[:, :, :cols].astype(f32).reshape(part_ref.shape).astype(bf16)


def part_rows(x, part_cols):
    vm = pl.BlockSpec(memory_space=pltpu.VMEM)
    return pl.pallas_call(
        rows_kernel,
        out_shape=jax.ShapeDtypeStruct((x.shape[0] * x.shape[1], part_cols), bf16),
        in_specs=[vm],
        out_specs=vm,
        compiler_params=pltpu.CompilerParams(vmem_limit_bytes=16 * 2**20),
        cost_estimate=pl.CostEstimate(flops=0, bytes_accessed=2**20, transcendentals=0),
        name="part_rows",
    )(x)


FR = ("z", "y", "xh", "c")
PAIR = [(0, 1), (1, 0)]


def shift(x, axis, size, by):
    return lax.ppermute(x, axis, [(i, (i + by) % size) for i in range(size)])


def across(x, axis, size, by):
    return lax.ppermute(x, axis, [(i, i ^ by) for i in range(size)])


ZX = ("z", "xh")


def far_z(w):
    return jnp.stack([w] + [across(w, "z", Z, 2 * i) for i in range(1, Z // 2)], 0)


def near_zx(own):
    even = lax.axis_index("xh") == 0
    a, b, d = (across(own, ZX, Z * XH, by) for by in (1, 2, 3))

    def part(at):
        first = jnp.concatenate([jnp.where(even, own, a)[at], jnp.where(even, a, own)[at]], 1)
        second = jnp.concatenate([jnp.where(even, b, d)[at], jnp.where(even, d, b)[at]], 1)
        return jnp.stack([first, second], 1).reshape(Z // 2, XH * ROWS, own.shape[2])

    return part(slice(0, 2)), part(slice(2, 4))


def reduce_weight(mine, rest, got, finish, late):
    even = lax.axis_index("xh") == 0
    other = lax.ppermute(rest, "c", PAIR)
    h = Z // 2
    own, after, before, far_low, far_high, after_high, before_low = combine(mine, other)
    up_far = shift(far_low, "y", Y, 1)
    down_far = shift(far_high, "y", Y, Y - 1)
    up_high = shift(after_high, "y", Y, 1)
    down_low = shift(before_low, "y", Y, Y - 1)
    up_far, down_far, got = lax.optimization_barrier((up_far, down_far, got))
    summed = finish(got)
    up_low = (after + up_far.astype(f32)).astype(bf16)
    down_high = (before + down_far.astype(f32)).astype(bf16)
    up_low, down_high, summed = lax.optimization_barrier((up_low, down_high, summed))
    up_low = shift(up_low, "y", Y, 1)
    down_high = shift(down_high, "y", Y, Y - 1)
    low = own[:h] + up_low.astype(f32) + down_low.astype(f32)
    high = own[h:] + up_high.astype(f32) + down_high.astype(f32)
    blocks = jnp.concatenate([low, high], 0)
    kept = jnp.where(even, blocks[:, :ROWS], blocks[:, ROWS:])
    sent = jnp.where(even, blocks[:, ROWS:], blocks[:, :ROWS])
    total = kept[0::2]
    for by, x in ((2, kept[1::2]), (1, sent[0::2]), (3, sent[1::2])):
        total = total + across(x.astype(bf16), ZX, Z * XH, by).astype(f32)
    back = late(summed)
    total, back = lax.optimization_barrier((total, back))
    result = total[0]
    for i in range(1, h):
        result = result + across(total[i].astype(bf16), "z", Z, 2 * i).astype(f32)
    return result, back


def on_device(normed, out_grad, w_qkv):
    frames_dev, patches, width = normed.shape
    half = out_grad.shape[2]
    cols = width // MP
    count = patches // F
    n = 3 * half
    where = jnp.stack([lax.axis_index(a) for a in ("z", "y", "c", "mp")]).astype(jnp.int32)
    m = lax.axis_index("mp")
    part = lax.dynamic_slice_in_dim(normed, m * cols, cols, 2)
    tokens = jnp.concatenate([part, out_grad], axis=2).reshape(F, count, cols + half)

    rows = far_z(w_qkv.reshape(w_qkv.shape[0], n))
    tokens, rows = lax.optimization_barrier((tokens, rows))
    tokens = lax.all_to_all(tokens, FR, 0, 0, tiled=True)
    low, high = near_zx(rows)
    part = part_rows(tokens, cols)
    low, high, part = lax.optimization_barrier((low, high, part))
    others = lax.ppermute(part, "mp", PAIR)
    before_low = shift(low, "y", Y, 1)
    after_high = shift(high, "y", Y, Y - 1)
    before_high = shift(high, "y", Y, 1)
    after_low = shift(low, "y", Y, Y - 1)
    far_low = shift(before_low, "y", Y, 1)
    far_high = shift(after_high, "y", Y, Y - 1)
    mine = [low, high, after_low, after_high, far_low, far_high, before_low, before_high]
    rest = {i: lax.ppermute(mine[i], "c", PAIR) for i in (0, 1, 2, 3, 6, 7)}
    mine, others = lax.optimization_barrier((mine, others))
    rest.update({i: lax.ppermute(mine[i], "c", PAIR) for i in (4, 5)})

    rest = [rest[i] for i in range(8)]
    give, keep, mine, rest = core(where, tokens, others, mine, rest)
    got = lax.ppermute(give, "mp", PAIR)

    def finish(got):
        return add_parts(keep, got)

    def to_frames(x):
        return lax.all_to_all(x, FR, 0, 0, tiled=True)

    weight_grad, back = reduce_weight(mine, rest, got, finish, to_frames)
    input_grad = back.reshape(frames_dev, patches, cols)
    weight_grad = weight_grad * (1.0 / F)
    return (input_grad, weight_grad.reshape(w_qkv.shape))


def solution(mesh):
    fine = Mesh(mesh.devices.reshape(Z, Y, XH, C, MP), ("z", "y", "xh", "c", "mp"))
    in_specs = (P(FR, None, None), P(FR, None, "mp"), P(FR, None, "mp"))
    out_specs = (P(FR, None, "mp"), P(FR, None, "mp"))
    return jax.shard_map(
        on_device, mesh=fine, in_specs=in_specs, out_specs=out_specs, check_vma=False
    )
```

```python
import jax
import jax.numpy as jnp
from jax import lax
from jax.experimental import pallas as pl
from jax.experimental.pallas import tpu as pltpu
from jax.sharding import Mesh, PartitionSpec as P

HEAD_DIM = 64
Z, Y, XH, C, MP = 8, 4, 2, 2, 2
F = 128
ROWS = 12
VMEM_LIMIT = 16 * 2**20
CORE_LIMIT = 48 * 2**20
bf16, f32 = jnp.bfloat16, jnp.float32
NT = (((1,), (1,)), ((), ()))
TN = (((0,), (0,)), ((), ()))


def dot(a, b, dims):
    return lax.dot_general(a, b, dims, preferred_element_type=f32)


def core_kernel(where_ref, x_hbm, o_hbm, *refs):
    blocks = refs[:16]
    give_ref, keep_ref, mine_ref, rest_ref, w_ref, s_ref, d_ref, g_ref, t_ref = refs[16:25]
    x_ref, o_ref, pieces, sems = refs[25:]
    copies = [pltpu.make_async_copy(blocks[i], pieces.at[i], sems.at[i]) for i in range(16)]
    copy_x = pltpu.make_async_copy(x_hbm, x_ref, sems.at[16])
    copy_o = pltpu.make_async_copy(o_hbm, o_ref, sems.at[17])
    for i in range(8):
        copies[i].start()
        copies[i + 8].start()
    copy_x.start()
    copy_o.start()
    z, y, c, m = (where_ref[i] for i in range(4))
    unit = XH * C * ROWS

    for i in range(8):
        by, high = i // 2, i % 2
        copies[i].wait()
        copies[i + 8].wait()

        @pl.loop(0, Z // 2)
        def _(t, i=i, by=by, high=high):
            a = pieces[i, t].astype(f32)
            b = pieces[i + 8, t].astype(f32)
            first = jnp.where(c == 0, a, b)
            second = jnp.where(c == 0, b, a)
            rows = [first[:ROWS], second[:ROWS], first[ROWS:], second[ROWS:]]
            to = lax.bitwise_xor(z, t + high * (Z // 2)) * Y + lax.rem(by + y, Y)
            to = pl.ds(pl.multiple_of(to * unit, unit), unit)
            w_ref[to, :] = jnp.concatenate(rows, 0).astype(bf16)

    copy_x.wait()
    t_ref[...] = x_ref[...].astype(f32).reshape(t_ref.shape).astype(bf16)
    copy_o.wait()
    part_cols = o_ref.shape[1]
    rows, half = t_ref.shape[0], t_ref.shape[1] - part_cols
    count = rows // F
    scale = HEAD_DIM ** (-0.5)
    pairs = half // 128
    near = pl.ds(pl.multiple_of(m * part_cols, part_cols), part_cols)
    away = pl.ds(pl.multiple_of((1 - m) * part_cols, part_cols), part_cols)
    part = jnp.dot(t_ref[:, :part_cols], w_ref[near, :], preferred_element_type=f32)
    part += jnp.dot(o_ref[...], w_ref[away, :], preferred_element_type=f32)
    part = part.astype(bf16)
    for i in range(3 * pairs):
        s_ref[i] = part[:, i * 128 : (i + 1) * 128].astype(f32)
    for pair in range(pairs):
        at = part_cols + pair * 128
        s_ref[3 * pairs + pair] = t_ref[:, at : at + 128].astype(f32)
    low = lax.broadcasted_iota(jnp.int32, (F, 128), 1) < HEAD_DIM
    zero = jnp.zeros((F, 128), f32)

    def split(v):
        return jnp.concatenate([jnp.where(low, v, zero), jnp.where(low, zero, v)], 0).astype(bf16)

    @pl.loop(0, count)
    def _(p):
        at = pl.ds(p, F, stride=count)
        for pair in range(pairs):
            q, k, v, u = (s_ref[j * pairs + pair, at, :] for j in range(4))
            q2 = split(q * scale)
            u2 = split(u)
            k = k.astype(bf16)
            v = v.astype(bf16)
            weights = jnp.exp(dot(q2, k, NT))
            weights = weights / jnp.sum(weights, axis=-1, keepdims=True)
            dprobs = dot(u2, v, NT)
            center = jnp.sum(weights * dprobs, axis=-1, keepdims=True)
            dscores = (weights * (dprobs - center)).astype(bf16)
            dv = dot(weights.astype(bf16), u2, TN)
            dk = dot(dscores, q2, TN)
            both = jnp.dot(dscores, k, preferred_element_type=f32) * scale
            dq = jnp.where(low, both[:F], both[F:])
            for j, part in enumerate((dq, dk, dv)):
                d_ref[j * pairs + pair, at, :] = part
    g = jnp.concatenate([d_ref[i] for i in range(3 * pairs)], 1).astype(bf16)
    g_ref[...] = g
    give_ref[...] = dot(g, w_ref[away, :], NT).astype(bf16)
    keep_ref[...] = dot(g, w_ref[near, :], NT).astype(bf16)
    step = 384
    for ref, of in ((t_ref, m), (o_ref, 1 - m)):
        for i in range(part_cols // step):
            total = dot(ref[:, i * step : (i + 1) * step], g_ref[...], TN)
            for b in range(step // unit):
                quarters = [total[b * unit + r * ROWS :][:ROWS] for r in range(4)]
                first = jnp.concatenate([quarters[0], quarters[2]], 0)
                second = jnp.concatenate([quarters[1], quarters[3]], 0)
                by = lax.rem(b % Y + Y - y, Y)
                at = i * (step // unit // Y) + b // Y
                t = lax.bitwise_xor(of * (Z // MP) + at, z)
                mine_ref[by, t] = jnp.where(c == 0, first, second).astype(bf16)
                rest_ref[by, t] = jnp.where(c == 0, second, first).astype(bf16)


def core(where, tokens, others, mine, rest):
    rows, part_cols = others.shape
    half = tokens.shape[2] - part_cols
    width, n = MP * part_cols, 3 * half
    vm = pl.BlockSpec(memory_space=pltpu.VMEM)
    return pl.pallas_call(
        core_kernel,
        out_shape=(
            jax.ShapeDtypeStruct((rows, part_cols), bf16),
            jax.ShapeDtypeStruct((rows, part_cols), bf16),
            jax.ShapeDtypeStruct((Y, Z, XH * ROWS, n), bf16),
            jax.ShapeDtypeStruct((Y, Z, XH * ROWS, n), bf16),
        ),
        in_specs=[pl.BlockSpec(memory_space=pltpu.SMEM)]
        + [pl.BlockSpec(memory_space=pl.ANY)] * 18,
        out_specs=(vm,) * 4,
        scratch_shapes=[
            pltpu.VMEM((width, n), bf16),
            pltpu.VMEM((4 * half // 128, rows, 128), f32),
            pltpu.VMEM((3 * half // 128, rows, 128), f32),
            pltpu.VMEM((rows, n), bf16),
            pltpu.VMEM((rows, part_cols + half), bf16),
            pltpu.VMEM(tokens.shape, bf16),
            pltpu.VMEM(others.shape, bf16),
            pltpu.VMEM((16,) + mine[0].shape, bf16),
            pltpu.SemaphoreType.DMA((18,)),
        ],
        compiler_params=pltpu.CompilerParams(vmem_limit_bytes=CORE_LIMIT),
        cost_estimate=pl.CostEstimate(
            flops=6 * rows * width * n, bytes_accessed=8 * 2**20, transcendentals=0
        ),
        name="attention_core",
    )(where, tokens, others, *mine, *rest)


def combine_kernel(mine_ref, other_ref, *refs):
    own_ref, after_ref, before_ref, far_low, far_high, after_high, before_low = refs
    h = Z // 2

    def added(by, t):
        return mine_ref[by, t].astype(f32) + other_ref[by, t].astype(f32)

    @pl.loop(0, h)
    def _(t):
        far_low[t] = added(2, t).astype(bf16)
        far_high[t] = added(2, t + h).astype(bf16)
        own_ref[t] = added(0, t)
        own_ref[t + h] = added(0, t + h)
        after_ref[t] = added(1, t)
        after_high[t] = added(1, t + h).astype(bf16)
        before_low[t] = added(3, t).astype(bf16)
        before_ref[t] = added(3, t + h)


def combine(mine, other):
    vm = pl.BlockSpec(memory_space=pltpu.VMEM)
    block = mine.shape[2:]
    h = Z // 2
    return pl.pallas_call(
        combine_kernel,
        out_shape=[jax.ShapeDtypeStruct((n,) + block, f32) for n in (Z, h, h)]
        + [jax.ShapeDtypeStruct((h,) + block, bf16)] * 4,
        in_specs=[vm, vm],
        out_specs=[vm] * 7,
        compiler_params=pltpu.CompilerParams(vmem_limit_bytes=VMEM_LIMIT),
        cost_estimate=pl.CostEstimate(flops=0, bytes_accessed=2**20, transcendentals=0),
        name="combine_cores",
    )(mine, other)


def add_kernel(a_ref, b_ref, o_ref):
    total = a_ref[...].astype(f32) + b_ref[...].astype(f32)
    o_ref[...] = total.reshape(o_ref.shape).astype(bf16)


def add_parts(a, b):
    rows, cols = a.shape
    vm = pl.BlockSpec(memory_space=pltpu.VMEM)
    return pl.pallas_call(
        add_kernel,
        out_shape=jax.ShapeDtypeStruct((F, rows // F, cols), bf16),
        in_specs=[vm, vm],
        out_specs=vm,
        compiler_params=pltpu.CompilerParams(vmem_limit_bytes=16 * 2**20),
        cost_estimate=pl.CostEstimate(flops=0, bytes_accessed=2**20, transcendentals=0),
        name="add_parts",
    )(a, b)


def rows_kernel(x_ref, part_ref):
    cols = part_ref.shape[1]
    part_ref[...] = x_ref[:, :, :cols].astype(f32).reshape(part_ref.shape).astype(bf16)


def part_rows(x, part_cols):
    vm = pl.BlockSpec(memory_space=pltpu.VMEM)
    return pl.pallas_call(
        rows_kernel,
        out_shape=jax.ShapeDtypeStruct((x.shape[0] * x.shape[1], part_cols), bf16),
        in_specs=[vm],
        out_specs=vm,
        compiler_params=pltpu.CompilerParams(vmem_limit_bytes=16 * 2**20),
        cost_estimate=pl.CostEstimate(flops=0, bytes_accessed=2**20, transcendentals=0),
        name="part_rows",
    )(x)


FR = ("z", "y", "xh", "c")
PAIR = [(0, 1), (1, 0)]


def shift(x, axis, size, by):
    return lax.ppermute(x, axis, [(i, (i + by) % size) for i in range(size)])


def across(x, axis, size, by):
    return lax.ppermute(x, axis, [(i, i ^ by) for i in range(size)])


ZX = ("z", "xh")


def far_z(w):
    return jnp.stack([w] + [across(w, "z", Z, 2 * i) for i in range(1, Z // 2)], 0)


def near_zx(own):
    even = lax.axis_index("xh") == 0
    a, b, d = (across(own, ZX, Z * XH, by) for by in (1, 2, 3))

    def part(at):
        first = jnp.concatenate([jnp.where(even, own, a)[at], jnp.where(even, a, own)[at]], 1)
        second = jnp.concatenate([jnp.where(even, b, d)[at], jnp.where(even, d, b)[at]], 1)
        return jnp.stack([first, second], 1).reshape(Z // 2, XH * ROWS, own.shape[2])

    return part(slice(0, 2)), part(slice(2, 4))


def reduce_weight(mine, rest, got, finish, late):
    even = lax.axis_index("xh") == 0
    other = lax.ppermute(rest, "c", PAIR)
    h = Z // 2
    own, after, before, far_low, far_high, after_high, before_low = combine(mine, other)
    up_far = shift(far_low, "y", Y, 1)
    down_far = shift(far_high, "y", Y, Y - 1)
    up_high = shift(after_high, "y", Y, 1)
    down_low = shift(before_low, "y", Y, Y - 1)
    up_far, down_far, got = lax.optimization_barrier((up_far, down_far, got))
    summed = finish(got)
    up_low = (after + up_far.astype(f32)).astype(bf16)
    down_high = (before + down_far.astype(f32)).astype(bf16)
    up_low, down_high, summed = lax.optimization_barrier((up_low, down_high, summed))
    up_low = shift(up_low, "y", Y, 1)
    down_high = shift(down_high, "y", Y, Y - 1)
    low = own[:h] + up_low.astype(f32) + down_low.astype(f32)
    high = own[h:] + up_high.astype(f32) + down_high.astype(f32)
    blocks = jnp.concatenate([low, high], 0)
    kept = jnp.where(even, blocks[:, :ROWS], blocks[:, ROWS:])
    sent = jnp.where(even, blocks[:, ROWS:], blocks[:, :ROWS])
    total = kept[0::2]
    for by, x in ((2, kept[1::2]), (1, sent[0::2]), (3, sent[1::2])):
        total = total + across(x.astype(bf16), ZX, Z * XH, by).astype(f32)
    back = late(summed)
    total, back = lax.optimization_barrier((total, back))
    result = total[0]
    for i in range(1, h):
        result = result + across(total[i].astype(bf16), "z", Z, 2 * i).astype(f32)
    return result, back


def on_device(normed, out_grad, w_qkv):
    frames_dev, patches, width = normed.shape
    half = out_grad.shape[2]
    cols = width // MP
    count = patches // F
    n = 3 * half
    where = jnp.stack([lax.axis_index(a) for a in ("z", "y", "c", "mp")]).astype(jnp.int32)
    m = lax.axis_index("mp")
    part = lax.dynamic_slice_in_dim(normed, m * cols, cols, 2)
    tokens = jnp.concatenate([part, out_grad], axis=2).reshape(F, count, cols + half)

    rows = far_z(w_qkv.reshape(w_qkv.shape[0], n))
    tokens, rows = lax.optimization_barrier((tokens, rows))
    tokens = lax.all_to_all(tokens, FR, 0, 0, tiled=True)
    low, high = near_zx(rows)
    part = part_rows(tokens, cols)
    low, high, part = lax.optimization_barrier((low, high, part))
    others = lax.ppermute(part, "mp", PAIR)
    before_low = shift(low, "y", Y, 1)
    after_high = shift(high, "y", Y, Y - 1)
    before_high = shift(high, "y", Y, 1)
    after_low = shift(low, "y", Y, Y - 1)
    far_low = shift(before_low, "y", Y, 1)
    far_high = shift(after_high, "y", Y, Y - 1)
    mine = [low, high, after_low, after_high, far_low, far_high, before_low, before_high]
    rest = {i: lax.ppermute(mine[i], "c", PAIR) for i in (0, 1, 2, 3, 6, 7)}
    mine, others = lax.optimization_barrier((mine, others))
    rest.update({i: lax.ppermute(mine[i], "c", PAIR) for i in (4, 5)})

    rest = [rest[i] for i in range(8)]
    give, keep, mine, rest = core(where, tokens, others, mine, rest)
    got = lax.ppermute(give, "mp", PAIR)

    def finish(got):
        return add_parts(keep, got)

    def to_frames(x):
        return lax.all_to_all(x, FR, 0, 0, tiled=True)

    weight_grad, back = reduce_weight(mine, rest, got, finish, to_frames)
    input_grad = back.reshape(frames_dev, patches, cols)
    weight_grad = weight_grad * (1.0 / F)
    return (input_grad, weight_grad.reshape(w_qkv.shape))


def solution(mesh):
    fine = Mesh(mesh.devices.reshape(Z, Y, XH, C, MP), ("z", "y", "xh", "c", "mp"))
    in_specs = (P(FR, None, None), P(FR, None, "mp"), P(FR, None, "mp"))
    out_specs = (P(FR, None, "mp"), P(FR, None, "mp"))
    return jax.shard_map(
        on_device, mesh=fine, in_specs=in_specs, out_specs=out_specs, check_vma=False
    )
```
